128 devices in a mesh: pts: 64 (over z, y, x), grp: 2 (over core).
Axes of the slice: x: 4, y: 4, z: 4, core: 2. Of those that a mesh axis runs over, the one named last changes fastest.
Arguments:
- points: bfloat16 [131072, 256], P('pts'), may hold values from -6 to 6
- neighbours: int32 [131072, 27], P('pts'), may hold values from -1 to 131071, as said below
- patch_len: int32 [256], replicated, may hold values from 1 to 1024, as said below
- zorder: int32 [131072], P('pts'), may hold values from 0 to 131071, as said below
- conv_w: bfloat16 [27, 256, 256], P(None, None, 'grp'), may hold values from -0.078125 to 0.078125
- conv_b: float32 [256], P('grp'), may hold values from -3 to 3
- cpe_w: bfloat16 [256, 256], replicated, may hold values from -0.375 to 0.375
- cpe_b: float32 [256], replicated, may hold values from -3 to 3
- cpe_gain: float32 [256], replicated, may hold values from 0.1 to 1.9
- norm1_gain: float32 [256], replicated, may hold values from 0.1 to 1.9
- qkv_w: bfloat16 [256, 3, 256], P(None, None, 'grp'), may hold values from -2 to 2
- qkv_b: float32 [3, 256], P(None, 'grp'), may hold values from -3 to 3
- proj_w: bfloat16 [256, 256], replicated, may hold values from -0.375 to 0.375
- proj_b: float32 [256], replicated, may hold values from -3 to 3
- norm2_gain: float32 [256], replicated, may hold values from 0.1 to 1.9
- fc1_w: bfloat16 [256, 1024], P(None, 'grp'), may hold values from -0.375 to 0.375
- fc1_b: float32 [1024], P('grp'), may hold values from -3 to 3
- fc2_w: bfloat16 [1024, 256], P('grp'), may hold values from -0.1875 to 0.1875
- fc2_b: float32 [256], replicated, may hold values from -3 to 3
Outputs:
- next_rows: bfloat16 [131072, 256], P('pts')
The draws below stay inside these ranges and needn't reach their ends.
Inputs may be any that keep to these rules, and one draw needn't show every extreme that they name: `neighbours`: tap 13 is the row itself; every other entry is -1 or a row at most 256 rows away; rows at exactly 256 away on both sides occur. `zorder`: A permutation. The rows of next_rows on one device come in runs of 64; each run is a whole aligned run of 64 rows of one source device, in one common inner order, and the 64-row runs of one device come from 32 different source devices at relative offsets (mod 64) common to all devices, one of which is 32. `patch_len`: patches sum to 131072 rows, one has exactly 1024.
All inputs are finite; a program needn't handle non-finite values.
Results may differ from the reference program's by a relative error of at most 0.022.
Values may be sent and summed in bfloat16 or wider, within the bound.
No kernel may reach another device: no remote copies, remote signals or barrier semaphores. Data moves between devices by JAX's collectives and lax.ppermute only.
A program may use at most 128 MiB of HBM per device.

```python
import jax
import jax.numpy as jnp
from jax import lax

C = 256
HID = 1024
PATCH = 1024
HALO = 256
ROWS = 2048
TOTAL = 131072
TILE = 64


def draw_neighbours(key, part):
    key_a, key_b, key_c = jax.random.split(key, 3)
    row_shift = jax.random.randint(key_a, (TOTAL, 27), -HALO, HALO + 1)
    present = jax.random.randint(key_b, (TOTAL, 27), 0, 5) < 3
    marked = jax.random.randint(key_c, (TOTAL, 1), 0, 61) == 0
    row_ids = jnp.arange(TOTAL)[:, None]
    tap_ids = jnp.arange(27)[None, :]
    row_shift = jnp.where(tap_ids == 13, 0, row_shift)
    row_shift = jnp.where(marked & (tap_ids == 0), -HALO, row_shift)
    row_shift = jnp.where(marked & (tap_ids == 26), HALO, row_shift)
    present = present | (tap_ids == 13) | marked & ((tap_ids == 0) | (tap_ids == 26))
    target = row_ids + row_shift
    valid = present & (target >= 0) & (target < TOTAL)
    return jnp.where(valid, target, -1).astype(jnp.int32)


def draw_patch_len(key, part):
    key = jax.random.fold_in(key, 5)
    dev_count = TOTAL // ROWS
    per_dev = 2 * ROWS // PATCH
    inner = per_dev - 1
    half_patch = PATCH // 2
    dev_ids = jnp.arange(dev_count, dtype=jnp.int32)
    span = jnp.where(dev_ids == dev_count - 1, ROWS - half_patch, ROWS - PATCH).astype(jnp.int32)
    base_len = span // inner
    leftover = span - base_len * inner
    jitter = jax.random.randint(key, (dev_count, inner), 0, ROWS).astype(jnp.int32)
    jitter = jitter % (base_len[:, None] // 2 + 1)
    jitter = jnp.where(jnp.arange(inner)[None, :] == inner - 1, 0, jitter)
    before = jnp.concatenate([jnp.zeros((dev_count, 1), jnp.int32), jitter[:, :inner - 1]], axis=1)
    inner_len = base_len[:, None] + jitter - before
    inner_len = inner_len + jnp.where(jnp.arange(inner)[None, :] == inner - 1, leftover[:, None], 0)
    first_len = jnp.where(dev_ids == 0, half_patch, PATCH).astype(jnp.int32)
    result = jnp.concatenate([first_len[:, None], inner_len], axis=1)
    return result.reshape(dev_count * per_dev).astype(jnp.int32)


def draw_zorder(key, part):
    peer_count = TOTAL // ROWS
    pieces = ROWS // TILE
    half_axis = peer_count // 2
    key_a, key_b, key_c = jax.random.split(key, 3)
    others = jax.random.permutation(key_a, peer_count - 1)
    others = others + (others >= half_axis).astype(others.dtype)
    offsets = jnp.concatenate([jnp.full((1,), half_axis, others.dtype), others[:pieces - 1]])
    tile_order = jax.random.permutation(key_b, pieces)
    inner_order = jax.random.permutation(key_c, TILE)
    target = jnp.arange(peer_count)[:, None, None]
    source = (target - offsets[None, :, None]) % peer_count
    result = source * ROWS + tile_order[None, :, None] * TILE + inner_order[None, None, :]
    return result.reshape(TOTAL).astype(jnp.int32)


def draw_qkv_w(key, part):
    key_a = jax.random.fold_in(key, 0)
    base_draw = jnp.clip(jax.random.normal(key_a, (C, 3, C), jnp.float32), -4.0, 4.0) * C ** (-0.5)
    return base_draw.astype(jnp.bfloat16)


def level_of(stream_key, dims, shards, low, high):
    gain, own = 1.0, jax.random.fold_in(stream_key, 6)
    for axis_at, shards_of in shards:
        draws = jnp.exp(jax.random.uniform(jax.random.fold_in(own, axis_at), (shards_of,), jnp.float32, low / len(shards), high / len(shards)))
        gain = gain * jnp.repeat(draws, dims[axis_at] // shards_of).reshape([-1 if axis == axis_at else 1 for axis in range(len(dims))])
    return gain


def noise(rng, shape, scale, most, cuts=(), kind=jnp.bfloat16):
    level = level_of(rng, shape, cuts, -0.22, 0.18) if cuts else 1.0
    array = jax.random.normal(rng, shape, jnp.float32) * scale * level
    return jnp.minimum(jnp.maximum(array, -most), most).astype(kind)


def setup_inputs(seed: int = 0) -> dict:
    splits = jax.random.split(jax.random.key(seed), 20)
    points = noise(splits[0], (TOTAL, C), 1.0, 6.0, ((0, 64),))
    neighbours = draw_neighbours(jax.random.fold_in(splits[19], 71), 0)
    patch_len = draw_patch_len(jax.random.fold_in(splits[19], 71), 0)
    zorder = draw_zorder(jax.random.fold_in(splits[19], 71), 0)
    conv_w = noise(splits[4], (27, C, C), (27 * C) ** -0.5, 0.078125, ((2, 2),))
    conv_b = noise(splits[5], (C,), 0.5, 3.0, ((0, 2),), jnp.float32)
    cpe_w = noise(splits[6], (C, C), C ** -0.5, 0.375)
    cpe_b = noise(splits[7], (C,), 0.5, 3.0, (), jnp.float32)
    cpe_gain = jnp.clip(1.0 + 0.18 * jax.random.normal(splits[8], (C,), jnp.float32), 0.1, 1.9)
    norm1_gain = jnp.clip(1.0 + 0.18 * jax.random.normal(splits[9], (C,), jnp.float32), 0.1, 1.9)
    qkv_w = draw_qkv_w(jax.random.fold_in(splits[19], 71), 0)
    qkv_b = noise(splits[11], (3, C), 0.5, 3.0, ((1, 2),), jnp.float32)
    proj_w = noise(splits[12], (C, C), C ** -0.5, 0.375)
    proj_b = noise(splits[13], (C,), 0.5, 3.0, (), jnp.float32)
    norm2_gain = jnp.clip(1.0 + 0.18 * jax.random.normal(splits[14], (C,), jnp.float32), 0.1, 1.9)
    fc1_w = noise(splits[15], (C, HID), C ** -0.5, 0.375, ((1, 2),))
    fc1_b = noise(splits[16], (HID,), 0.5, 3.0, ((0, 2),), jnp.float32)
    fc2_w = noise(splits[17], (HID, C), HID ** -0.5, 0.1875, ((0, 2),))
    fc2_b = noise(splits[18], (C,), 0.5, 3.0, (), jnp.float32)
    return dict(points=points, neighbours=neighbours, patch_len=patch_len, zorder=zorder, conv_w=conv_w, conv_b=conv_b, cpe_w=cpe_w, cpe_b=cpe_b, cpe_gain=cpe_gain, norm1_gain=norm1_gain, qkv_w=qkv_w, qkv_b=qkv_b, proj_w=proj_w, proj_b=proj_b, norm2_gain=norm2_gain, fc1_w=fc1_w, fc1_b=fc1_b, fc2_w=fc2_w, fc2_b=fc2_b)


def layer_norm(values, gain_row):
    center = values - lax.optimization_barrier(jnp.mean(values, axis=-1, keepdims=True))
    spread = lax.optimization_barrier(jnp.mean(center * center, axis=-1, keepdims=True))
    return center * lax.rsqrt(spread + 1e-05) * gain_row

def patch_limits(row_ids, patch_len, row_total):
    patch_ends = jnp.cumsum(patch_len).astype(jnp.int32)
    patch_starts = patch_ends - patch_len
    first_row = lax.optimization_barrier(jnp.max(jnp.where(patch_starts[None, :] <= row_ids[:, None], patch_starts[None, :], 0), axis=1))
    finish = lax.optimization_barrier(jnp.min(jnp.where(patch_ends[None, :] > row_ids[:, None], patch_ends[None, :], row_total), axis=1))
    return (first_row, finish)

def reference(points, neighbours, patch_len, zorder, conv_w, conv_b, cpe_w, cpe_b, cpe_gain, norm1_gain, qkv_w, qkv_b, proj_w, proj_b, norm2_gain, fc1_w, fc1_b, fc2_w, fc2_b):
    row_total = points.shape[0]
    width = points.shape[1]
    padded = jnp.concatenate([points, jnp.zeros((1, width), jnp.bfloat16)], axis=0)
    tap_index = jnp.where(neighbours < 0, row_total, neighbours).astype(jnp.int32)
    flat_conv = conv_w.reshape(27 * width, width)

    def conv_block(number):
        picked = lax.dynamic_slice_in_dim(tap_index, (number * ROWS).astype(jnp.int32), ROWS, 0)
        gathered = jnp.take(padded, picked, axis=0).reshape(ROWS, 27 * width)
        return (jnp.dot(gathered, flat_conv, preferred_element_type=jnp.float32) + conv_b).astype(jnp.bfloat16)
    conv_out = lax.map(conv_block, jnp.arange(row_total // ROWS, dtype=jnp.int32)).reshape(row_total, width)
    cpe_term = layer_norm(jnp.dot(conv_out, cpe_w, preferred_element_type=jnp.float32) + cpe_b, cpe_gain)
    section_one = (points.astype(jnp.float32) + cpe_term).astype(jnp.bfloat16)
    normed = layer_norm(section_one.astype(jnp.float32), norm1_gain).astype(jnp.bfloat16)
    triple = (jnp.dot(normed, qkv_w.reshape(width, 3 * width), preferred_element_type=jnp.float32) + qkv_b.reshape(3 * width)).astype(jnp.bfloat16)
    query_rows = triple[:, :width]
    key_rows = jnp.pad(triple[:, width:2 * width], ((PATCH, PATCH), (0, 0)))
    value_rows = jnp.pad(triple[:, 2 * width:], ((PATCH, PATCH), (0, 0)))
    block_rows = min(512, ROWS)
    window = block_rows + 2 * PATCH
    head_count = width // 16

    def attend(number):
        offset_row = (number * block_rows).astype(jnp.int32)
        query_blk = lax.dynamic_slice_in_dim(query_rows, offset_row, block_rows, 0).reshape(block_rows, head_count, 16).astype(jnp.float32)
        key_blk = lax.dynamic_slice_in_dim(key_rows, offset_row, window, 0).reshape(window, head_count, 16).astype(jnp.float32)
        value_blk = lax.dynamic_slice_in_dim(value_rows, offset_row, window, 0).reshape(window, head_count, 16).astype(jnp.float32)
        row_ids = offset_row + jnp.arange(block_rows, dtype=jnp.int32)
        key_ids = offset_row - PATCH + jnp.arange(window, dtype=jnp.int32)
        first_row, finish = patch_limits(row_ids, patch_len, row_total)
        allowed = (key_ids[None, :] >= first_row[:, None]) & (key_ids[None, :] < finish[:, None])
        scores = jnp.einsum('qhd,khd->hqk', query_blk, key_blk) * 0.25
        scores = jnp.where(allowed[None], scores, -jnp.inf)
        row_max = lax.optimization_barrier(jnp.max(scores, axis=2, keepdims=True))
        expo = jnp.exp(scores - row_max)
        attn_weights = (expo / lax.optimization_barrier(jnp.sum(expo, axis=2, keepdims=True))).astype(jnp.bfloat16)
        mixed_out = jnp.einsum('hqk,khd->qhd', attn_weights.astype(jnp.float32), value_blk)
        return mixed_out.reshape(block_rows, width).astype(jnp.bfloat16)
    attn = lax.map(attend, jnp.arange(row_total // block_rows, dtype=jnp.int32)).reshape(row_total, width)
    section_two = (section_one.astype(jnp.float32) + jnp.dot(attn, proj_w, preferred_element_type=jnp.float32) + proj_b).astype(jnp.bfloat16)
    normed_two = layer_norm(section_two.astype(jnp.float32), norm2_gain).astype(jnp.bfloat16)
    hidden = jax.nn.gelu(jnp.dot(normed_two, fc1_w, preferred_element_type=jnp.float32) + fc1_b, approximate=False).astype(jnp.bfloat16)
    output_rows = (section_two.astype(jnp.float32) + jnp.dot(hidden, fc2_w, preferred_element_type=jnp.float32) + fc2_b).astype(jnp.bfloat16)
    return jnp.take(output_rows, zorder, axis=0)
```

```python
import jax
import jax.numpy as jnp
from jax import lax
from jax.experimental import pallas as pl
from jax.experimental.pallas import tpu as pltpu
from jax.sharding import PartitionSpec as P

F32=jnp.float32; BF=jnp.bfloat16

Q_SCALE = 0.25 * 1.4426950408889634


def layer_norm(v, gain):
    c = v - jnp.mean(v, axis=-1, keepdims=True)
    s = jnp.mean(c * c, axis=-1, keepdims=True)
    return c * lax.rsqrt(s + 1e-05) * gain

RB=128
def conv_kernel(sc, pts, low, high, nb, wm, wo, cbm, cbo, cpw, cpb, cpg, n1g, sec_o, nrm_o, X, OH, G, W):
    g = sc[0]
    base = sc[1]
    X[0:256, :] = low[...]
    X[256:2304, :] = pts[...]
    X[2304:2560, :] = high[...]
    W[:, 0:128] = wm[...]
    W[:, 128:256] = wo[...]
    lanes = lax.broadcasted_iota(jnp.int32, (RB, 768), 1).astype(jnp.int32)
    def block(b, _):
        rel = []
        for j in range(RB // 32):
            rel.append(nb[pl.ds(pl.multiple_of(256 * b + 64 * j + 32 * g, 32), 32), :])
        rel = jnp.concatenate(rel, axis=0)
        off = base + 256 * b - 256
        rel = jnp.where(rel < 0, -1, rel - off).astype(jnp.int32)
        for t in range(27):
            col = rel[:, t:t + 1]
            OH[t * RB:(t + 1) * RB, :] = jnp.where(lanes == col, jnp.array(1, BF), jnp.array(0, BF))
        win = X[pl.ds(pl.multiple_of(256 * b, 256), 768), :]
        for q in range(3):
            out = jnp.dot(OH[q * 9 * RB:(q + 1) * 9 * RB, :], win, preferred_element_type=F32).astype(BF)
            for t in range(9):
                G[pl.ds(pl.multiple_of(b * RB, RB), RB), (q * 9 + t) * 256:(q * 9 + t + 1) * 256] = out[t * RB:(t + 1) * RB, :]
        return 0
    lax.fori_loop(0, 1024 // RB, block, 0)
    cb = jnp.concatenate([cbm[...], cbo[...]], axis=1)
    cpw_s = jnp.concatenate([cpw[pl.ds(pl.multiple_of(128 * g, 128), 128), :], cpw[pl.ds(pl.multiple_of(128 - 128 * g, 128), 128), :]], axis=0)
    def fin(m, _):
        r0 = pl.multiple_of(m * 256, 256)
        acc = jnp.dot(G[pl.ds(r0, 256), :], W[...], preferred_element_type=F32)
        conv = (acc + cb).astype(BF)
        c = jnp.dot(conv, cpw_s, preferred_element_type=F32) + cpb[...]
        own = []
        for j in range(8):
            own.append(pts[pl.ds(pl.multiple_of(512 * m + 64 * j + 32 * g, 32), 32), :])
        own = jnp.concatenate(own, axis=0).astype(F32)
        sec = (own + layer_norm(c, cpg[...])).astype(BF)
        sec_o[pl.ds(r0, 256), :] = sec
        nrm_o[pl.ds(r0, 256), :] = layer_norm(sec.astype(F32), n1g[...]).astype(BF)
        return 0
    lax.fori_loop(0, 4, fin, 0)
def conv_call(sc, pts, low, high, nb, wm, wo, cbm, cbo, cpw, cpb, cpg, n1g):
    sm=pl.BlockSpec(memory_space=pltpu.SMEM); vm=pl.BlockSpec(memory_space=pltpu.VMEM)
    return pl.pallas_call(conv_kernel,
        out_shape=[jax.ShapeDtypeStruct((1024,256),BF)]*2,
        in_specs=[sm]+[vm]*12, out_specs=[vm]*2,
        scratch_shapes=[pltpu.VMEM((2560,256),BF),pltpu.VMEM((27*RB,768),BF),pltpu.VMEM((1024,6912),BF),pltpu.VMEM((6912,256),BF)],
        compiler_params=pltpu.CompilerParams(vmem_limit_bytes=50*2**20),
        cost_estimate=pl.CostEstimate(flops=30*10**9,bytes_accessed=8*10**6,transcendentals=0),
        name="conv")(sc, pts, low, high, nb, wm, wo, cbm, cbo, cpw, cpb, cpg, n1g)


def attn_kernel(
    sc, sel, plen, own, oth, lo_own, lo_oth, hi_own, hi_oth, sec, qkvm, qkvo, qbm, qbo, prw, prb,
    n2g, f1m, f1o, b1m, b1o, f2m, f2o, f2b, send, NE, KT, V, Q8, ACC, OUT, M,
):
    g = sc[0]
    base = sc[1]
    total = sc[2]
    mine = pl.multiple_of(32 * g, 32)
    theirs = pl.multiple_of(32 - 32 * g, 32)

    def spread(count, first, a_ref, b_ref):
        def step(c, _):
            src = pl.multiple_of(32 * c, 32)
            row = first + 64 * c
            NE[pl.ds(pl.multiple_of(row + mine, 32), 32), :] = a_ref[pl.ds(src, 32), :]
            NE[pl.ds(pl.multiple_of(row + theirs, 32), 32), :] = b_ref[pl.ds(src, 32), :]
            return 0

        lax.fori_loop(0, count, step, 0, unroll=4)

    spread(16, 0, lo_own, lo_oth)
    spread(32, 1024, own, oth)
    spread(16, 3072, hi_own, hi_oth)

    wkt = [jnp.transpose(w[:, 128:256]) for w in (qkvm, qkvo)]
    bkc = [jnp.transpose(jnp.broadcast_to(b[:, 128:256], (8, 128)))[:, :1] for b in (qbm, qbo)]
    wv = jnp.concatenate([qkvm[:, 256:384], qkvo[:, 256:384]], axis=1)
    bv = jnp.concatenate([qbm[:, 256:384], qbo[:, 256:384]], axis=1)

    def key_value(i, most):
        r0 = pl.multiple_of(i * 256, 256)
        rows = NE[pl.ds(r0, 256), :]
        for h in range(2):
            kt = (
                lax.dot_general(
                    wkt[h], rows, (((1,), (1,)), ((), ())), preferred_element_type=F32
                )
                + bkc[h]
            )
            most = jnp.maximum(most, jnp.sum((kt * kt).reshape(8, 16, 256), axis=1))
            KT[128 * h : 128 * h + 128, pl.ds(r0, 256)] = kt.astype(BF)
        V[pl.ds(r0, 256), :] = (jnp.dot(rows, wv, preferred_element_type=F32) + bv).astype(BF)
        return most

    key_most = jnp.max(lax.fori_loop(0, 16, key_value, jnp.zeros((8, 256), F32)))

    lens = jnp.broadcast_to(plen[...].astype(F32), (256, 256))
    sub = lax.broadcasted_iota(jnp.int32, (256, 256), 0)
    lane = lax.broadcasted_iota(jnp.int32, (256, 256), 1)
    ends_col = jnp.sum(jnp.where(lane <= sub, lens, 0.0), axis=1, keepdims=True)
    ends_row = jnp.sum(jnp.where(lane == sub, ends_col, 0.0), axis=0, keepdims=True)
    starts_row = ends_row - plen[...].astype(F32)

    wq = jnp.concatenate([qkvm[:, 0:128], qkvo[:, 0:128]], axis=1)
    bq = jnp.concatenate([qbm[:, 0:128], qbo[:, 0:128]], axis=1)
    hs = lax.broadcasted_iota(jnp.int32, (256, 128), 0) // 16
    hl = lax.broadcasted_iota(jnp.int32, (256, 128), 1)
    head_sel = jnp.where(hs == hl, 1.0, 0.0).astype(BF)
    k_low = jnp.where(
        lax.broadcasted_iota(jnp.int32, (32, 128), 0) < 16, 1.0, 0.0
    ).astype(BF)
    k_high = (1.0 - k_low.astype(F32)).astype(BF)
    col_head = lax.broadcasted_iota(jnp.int32, (128, 128), 1) // 16
    cols = [jnp.where(col_head == a, 1.0, 0.0).astype(BF) for a in range(8)]
    prw_s = jnp.concatenate(
        [
            prw[pl.ds(pl.multiple_of(128 * g, 128), 128), :],
            prw[pl.ds(pl.multiple_of(128 - 128 * g, 128), 128), :],
        ],
        axis=0,
    )

    def q_block(qb, _):
        r0 = pl.multiple_of(qb * 256, 256)
        q = (jnp.dot(own[pl.ds(r0, 256), :], wq, preferred_element_type=F32) + bq) * Q_SCALE
        q = q.astype(BF)
        for p in range(8):
            Q8[p] = q[:, 32 * p : 32 * p + 32]
        q_most = jnp.max(jnp.dot(q * q, head_sel, preferred_element_type=F32))
        calm = q_most * key_most * 1.05 <= 1e4
        r = lax.broadcasted_iota(jnp.int32, (256, 1), 0)
        row = (base + 512 * qb + 64 * (r // 32) + 32 * g + r % 32).astype(F32)
        first = jnp.max(jnp.where(starts_row <= row, starts_row, 0.0), axis=1, keepdims=True)
        finish = jnp.min(
            jnp.where(ends_row > row, ends_row, total.astype(F32)), axis=1, keepdims=True
        )
        shift = (1024 - base).astype(F32)
        first = (first + shift).astype(jnp.int32)
        finish = (finish + shift).astype(jnp.int32)
        kb0 = jnp.maximum(jnp.min(first) // 128, 0)
        kb1 = jnp.minimum((jnp.max(finish) + 127) // 128, 32)

        def scores(kb, p, kt, madd):
            part = kt[32 * p : 32 * p + 32, :]
            pair = jnp.concatenate([part * k_low, part * k_high], axis=1)
            s = jnp.dot(Q8[p], pair, preferred_element_type=F32)
            return s + madd

        def mask(kb):
            key = kb * 128 + lax.broadcasted_iota(jnp.int32, (256, 128), 1)
            madd = jnp.where((key >= first) & (key < finish), 0.0, -jnp.inf)
            return jnp.concatenate([madd, madd], axis=1)

        def attend(use_max):
            def step(kb, _):
                k0 = pl.multiple_of(kb * 128, 128)
                kt = KT[:, pl.ds(k0, 128)]
                vb = V[pl.ds(k0, 128), :]
                madd = mask(kb)
                for h in range(2):
                    vh = vb[:, 128 * h : 128 * h + 128]
                    ps, vs = [], []
                    for a in range(4):
                        p = 4 * h + a
                        s = scores(kb, p, kt, madd)
                        if use_max:
                            s = s - M[p]
                        ps.append(jnp.exp2(s).astype(BF))
                        for c in (cols[2 * a], cols[2 * a + 1]):
                            vs.append(jnp.concatenate([vh * c, c], axis=1))
                    ACC[h] += jnp.dot(
                        jnp.concatenate(ps, axis=1),
                        jnp.concatenate(vs, axis=0),
                        preferred_element_type=F32,
                    )
                return 0

            lax.fori_loop(kb0, kb1, step, 0)

        ACC[...] = jnp.zeros_like(ACC)

        @pl.when(calm)
        def _():
            attend(False)

        @pl.when(jnp.logical_not(calm))
        def _():
            M[...] = jnp.full(M.shape, -jnp.inf, F32)

            def top(kb, _):
                kt = KT[:, pl.ds(pl.multiple_of(kb * 128, 128), 128)]
                madd = mask(kb)
                for p in range(8):
                    M[p] = jnp.maximum(M[p], scores(kb, p, kt, madd))
                return 0

            lax.fori_loop(kb0, kb1, top, 0)
            for p in range(8):
                for h in range(2):
                    part = M[p, :, 128 * h : 128 * h + 128]
                    M[p, :, 128 * h : 128 * h + 128] = jnp.broadcast_to(
                        jnp.max(part, axis=1, keepdims=True), (256, 128)
                    )
            attend(True)

        attn = jnp.concatenate(
            [ACC[h, :, 0:128] / ACC[h, :, 128:256] for h in range(2)], axis=1
        ).astype(BF)
        two = (
            sec[pl.ds(r0, 256), :].astype(F32)
            + jnp.dot(attn, prw_s, preferred_element_type=F32)
            + prb[...]
        ).astype(BF)
        wide = two.astype(F32)
        normed = layer_norm(wide, n2g[...]).astype(BF)
        total_rows = wide + f2b[...]
        for f1, b1, f2 in ((f1m, b1m, f2m), (f1o, b1o, f2o)):
            x = jnp.dot(normed, f1[...], preferred_element_type=F32) + b1[...]
            x = (0.5 * x * (1.0 + lax.erf(x * 0.7071067811865476))).astype(BF)
            total_rows = total_rows + jnp.dot(x, f2[...], preferred_element_type=F32)
        OUT[pl.ds(r0, 256), :] = total_rows.astype(BF)
        return 0

    lax.fori_loop(0, 4, q_block, 0)

    def place(d, _):
        send[pl.ds(pl.multiple_of(32 * d, 32), 32), :] = OUT[
            pl.ds(pl.multiple_of(32 * sel[d], 32), 32), :
        ]
        return 0

    lax.fori_loop(0, 64, place, 0, unroll=4)


def attn_call(*args):
    smem, vmem = pl.BlockSpec(memory_space=pltpu.SMEM), pl.BlockSpec(memory_space=pltpu.VMEM)
    return pl.pallas_call(
        attn_kernel,
        out_shape=jax.ShapeDtypeStruct((2048, 256), BF),
        in_specs=[smem] * 2 + [vmem] * (len(args) - 2),
        out_specs=vmem,
        scratch_shapes=[
            pltpu.VMEM((4096, 256), BF),
            pltpu.VMEM((256, 4096), BF),
            pltpu.VMEM((4096, 256), BF),
            pltpu.VMEM((8, 256, 32), BF),
            pltpu.VMEM((2, 256, 256), F32),
            pltpu.VMEM((1024, 256), BF),
            pltpu.VMEM((8, 256, 256), F32),
        ],
        compiler_params=pltpu.CompilerParams(vmem_limit_bytes=48 * 2**20),
        cost_estimate=pl.CostEstimate(
            flops=60 * 10**9, bytes_accessed=8 * 10**6, transcendentals=2 * 10**7
        ),
        name="attention",
    )(*args)


def last_kernel(sc, src, inner, own, oth, out):
    g = sc[0]
    place = inner[...]
    place = place % 32 + jnp.where(place // 32 == g, 0, 32)
    perm = jnp.where(
        lax.broadcasted_iota(jnp.int32, (64, 64), 1) == place, 1.0, 0.0
    ).astype(BF)

    def step(k, _):
        s = pl.multiple_of(32 * src[k], 32)
        rows = jnp.concatenate([own[pl.ds(s, 32), :], oth[pl.ds(s, 32), :]], axis=0)
        out[pl.ds(pl.multiple_of(64 * k, 64), 64), :] = jnp.dot(
            perm, rows, preferred_element_type=F32
        ).astype(BF)
        return 0

    lax.fori_loop(0, 32, step, 0, unroll=4)


def last_call(*args):
    smem, vmem = pl.BlockSpec(memory_space=pltpu.SMEM), pl.BlockSpec(memory_space=pltpu.VMEM)
    return pl.pallas_call(
        last_kernel,
        out_shape=jax.ShapeDtypeStruct((2048, 256), BF),
        in_specs=[smem] * 2 + [vmem] * 3,
        out_specs=vmem,
        compiler_params=pltpu.CompilerParams(vmem_limit_bytes=16 * 2**20),
        name="relabel",
    )(*args)


def local(
    points, neighbours, patch_len, zorder, conv_w, conv_b, cpe_w, cpe_b, cpe_gain, norm1_gain,
    qkv_w, qkv_b, proj_w, proj_b, norm2_gain, fc1_w, fc1_b, fc2_w, fc2_b,
):
    g = lax.axis_index("grp").astype(jnp.int32)
    me = lax.axis_index("pts").astype(jnp.int32)
    peers = lax.axis_size("pts")
    rows = points.shape[0]
    forward = [(i, i + 1) for i in range(peers - 1)]
    backward = [(i + 1, i) for i in range(peers - 1)]

    def swap(x):
        return lax.ppermute(x, "grp", [(0, 1), (1, 0)])

    low = lax.ppermute(points[rows - 256 :], "pts", forward)
    high = lax.ppermute(points[:256], "pts", backward)
    conv_m = conv_w.reshape(27 * 256, 128)
    conv_o = swap(conv_m)
    small = jnp.concatenate([conv_b, qkv_b.reshape(384), fc1_b])
    small_o = swap(small)
    run = zorder[::64] // 64
    table = lax.all_gather(
        jnp.broadcast_to(jnp.pad(run, (0, 96))[None, :], (64, 128)), "pts", axis=0, tiled=True
    ).reshape(peers, 64, 128)[:, 0, :32]
    qkv_m = qkv_w.reshape(256, 384)
    qkv_o, fc1_o, fc2_o = swap(qkv_m), swap(fc1_w), swap(fc2_w)

    scalars = jnp.stack([g, me * rows, jnp.int32(rows * peers)])
    section_one, normed = conv_call(
        scalars, points, low, high, neighbours, conv_m, conv_o, small[None, :128],
        small_o[None, :128], cpe_w, cpe_b[None], cpe_gain[None], norm1_gain[None],
    )
    other = swap(normed)
    lo_own = lax.ppermute(normed[512:], "pts", forward)
    hi_own = lax.ppermute(normed[:512], "pts", backward)
    lo_oth, hi_oth = swap(lo_own), swap(hi_own)
    sel = jnp.max(jnp.where(table // 32 == me, table % 32, 0), axis=1)
    send = attn_call(
        scalars, sel, patch_len[None], normed, other, lo_own, lo_oth, hi_own, hi_oth, section_one,
        qkv_m, qkv_o, small[None, 128:512], small_o[None, 128:512], proj_w, proj_b[None],
        norm2_gain[None], fc1_w, fc1_o, small[None, 512:], small_o[None, 512:], fc2_w, fc2_o,
        fc2_b[None],
    )
    got = lax.all_to_all(send, "pts", split_axis=0, concat_axis=0, tiled=True)
    return last_call(scalars, run // 32, (zorder[:64] % 64)[:, None], got, swap(got))


def solution(mesh):
    placed = (
        P("pts", None), P("pts", None), P(), P("pts"), P(None, None, "grp"), P("grp"), P(), P(), P(),
        P(), P(None, None, "grp"), P(None, "grp"), P(), P(), P(), P(None, "grp"), P("grp"),
        P("grp", None), P(),
    )
    return jax.shard_map(
        local, mesh=mesh, in_specs=placed, out_specs=P("pts", None), check_vma=False
    )
```

```python
import jax
import jax.numpy as jnp
from jax import lax
from jax.experimental import pallas as pl
from jax.experimental.pallas import tpu as pltpu
from jax.sharding import PartitionSpec as P

F32=jnp.float32; BF=jnp.bfloat16

Q_SCALE = 0.25 * 1.4426950408889634


def layer_norm(v, gain):
    c = v - jnp.mean(v, axis=-1, keepdims=True)
    s = jnp.mean(c * c, axis=-1, keepdims=True)
    return c * lax.rsqrt(s + 1e-05) * gain

RB=128
def conv_kernel(sc, pts, low, high, nb, wm, wo, cbm, cbo, cpw, cpb, cpg, n1g, sec_o, nrm_o, X, OH, G, W):
    g = sc[0]
    base = sc[1]
    X[0:256, :] = low[...]
    X[256:2304, :] = pts[...]
    X[2304:2560, :] = high[...]
    W[:, 0:128] = wm[...]
    W[:, 128:256] = wo[...]
    lanes = lax.broadcasted_iota(jnp.int32, (RB, 768), 1).astype(jnp.int32)
    def block(b, _):
        rel = []
        for j in range(RB // 32):
            rel.append(nb[pl.ds(pl.multiple_of(256 * b + 64 * j + 32 * g, 32), 32), :])
        rel = jnp.concatenate(rel, axis=0)
        off = base + 256 * b - 256
        rel = jnp.where(rel < 0, -1, rel - off).astype(jnp.int32)
        for t in range(27):
            col = rel[:, t:t + 1]
            OH[t * RB:(t + 1) * RB, :] = jnp.where(lanes == col, jnp.array(1, BF), jnp.array(0, BF))
        win = X[pl.ds(pl.multiple_of(256 * b, 256), 768), :]
        for q in range(3):
            out = jnp.dot(OH[q * 9 * RB:(q + 1) * 9 * RB, :], win, preferred_element_type=F32).astype(BF)
            for t in range(9):
                G[pl.ds(pl.multiple_of(b * RB, RB), RB), (q * 9 + t) * 256:(q * 9 + t + 1) * 256] = out[t * RB:(t + 1) * RB, :]
        return 0
    lax.fori_loop(0, 1024 // RB, block, 0)
    cb = jnp.concatenate([cbm[...], cbo[...]], axis=1)
    cpw_s = jnp.concatenate([cpw[pl.ds(pl.multiple_of(128 * g, 128), 128), :], cpw[pl.ds(pl.multiple_of(128 - 128 * g, 128), 128), :]], axis=0)
    def fin(m, _):
        r0 = pl.multiple_of(m * 256, 256)
        acc = jnp.dot(G[pl.ds(r0, 256), :], W[...], preferred_element_type=F32)
        conv = (acc + cb).astype(BF)
        c = jnp.dot(conv, cpw_s, preferred_element_type=F32) + cpb[...]
        own = []
        for j in range(8):
            own.append(pts[pl.ds(pl.multiple_of(512 * m + 64 * j + 32 * g, 32), 32), :])
        own = jnp.concatenate(own, axis=0).astype(F32)
        sec = (own + layer_norm(c, cpg[...])).astype(BF)
        sec_o[pl.ds(r0, 256), :] = sec
        nrm_o[pl.ds(r0, 256), :] = layer_norm(sec.astype(F32), n1g[...]).astype(BF)
        return 0
    lax.fori_loop(0, 4, fin, 0)
def conv_call(sc, pts, low, high, nb, wm, wo, cbm, cbo, cpw, cpb, cpg, n1g):
    sm=pl.BlockSpec(memory_space=pltpu.SMEM); vm=pl.BlockSpec(memory_space=pltpu.VMEM)
    return pl.pallas_call(conv_kernel,
        out_shape=[jax.ShapeDtypeStruct((1024,256),BF)]*2,
        in_specs=[sm]+[vm]*12, out_specs=[vm]*2,
        scratch_shapes=[pltpu.VMEM((2560,256),BF),pltpu.VMEM((27*RB,768),BF),pltpu.VMEM((1024,6912),BF),pltpu.VMEM((6912,256),BF)],
        compiler_params=pltpu.CompilerParams(vmem_limit_bytes=50*2**20),
        cost_estimate=pl.CostEstimate(flops=30*10**9,bytes_accessed=8*10**6,transcendentals=0),
        name="conv")(sc, pts, low, high, nb, wm, wo, cbm, cbo, cpw, cpb, cpg, n1g)


def spread(g, NE, count, first, a_ref, b_ref):
    mine = pl.multiple_of(32 * g, 32)
    theirs = pl.multiple_of(32 - 32 * g, 32)

    def step(c, _):
        src = pl.multiple_of(32 * c, 32)
        row = first + 64 * c
        NE[pl.ds(pl.multiple_of(row + mine, 32), 32), :] = a_ref[pl.ds(src, 32), :]
        NE[pl.ds(pl.multiple_of(row + theirs, 32), 32), :] = b_ref[pl.ds(src, 32), :]
        return 0

    lax.fori_loop(0, count, step, 0, unroll=4)


def key_values(NE, KT, V, qkvm, qkvo, qbm, qbo):
    wkt = [jnp.transpose(w[:, 128:256]) for w in (qkvm, qkvo)]
    bkc = [jnp.transpose(jnp.broadcast_to(b[:, 128:256], (8, 128)))[:, :1] for b in (qbm, qbo)]
    wv = jnp.concatenate([qkvm[:, 256:384], qkvo[:, 256:384]], axis=1)
    bv = jnp.concatenate([qbm[:, 256:384], qbo[:, 256:384]], axis=1)

    def block(i, most):
        r0 = pl.multiple_of(i * 256, 256)
        rows = NE[pl.ds(r0, 256), :]
        for h in range(2):
            kt = (
                lax.dot_general(
                    wkt[h], rows, (((1,), (1,)), ((), ())), preferred_element_type=F32
                )
                + bkc[h]
            )
            most = jnp.maximum(most, jnp.sum((kt * kt).reshape(8, 16, 256), axis=1))
            KT[128 * h : 128 * h + 128, pl.ds(r0, 256)] = kt.astype(BF)
        V[pl.ds(r0, 256), :] = (jnp.dot(rows, wv, preferred_element_type=F32) + bv).astype(BF)
        return most

    return block


def patch_rows(plen):
    lens = jnp.broadcast_to(plen[...].astype(F32), (256, 256))
    sub = lax.broadcasted_iota(jnp.int32, (256, 256), 0)
    lane = lax.broadcasted_iota(jnp.int32, (256, 256), 1)
    ends_col = jnp.sum(jnp.where(lane <= sub, lens, 0.0), axis=1, keepdims=True)
    ends_row = jnp.sum(jnp.where(lane == sub, ends_col, 0.0), axis=0, keepdims=True)
    return ends_row - plen[...].astype(F32), ends_row


def limits(qb, g, base, total, starts_row, ends_row):
    r = lax.broadcasted_iota(jnp.int32, (256, 1), 0)
    row = (base + 512 * qb + 64 * (r // 32) + 32 * g + r % 32).astype(F32)
    first = jnp.max(jnp.where(starts_row <= row, starts_row, 0.0), axis=1, keepdims=True)
    finish = jnp.min(jnp.where(ends_row > row, ends_row, total.astype(F32)), axis=1, keepdims=True)
    shift = (1024 - base).astype(F32)
    first = (first + shift).astype(jnp.int32)
    finish = (finish + shift).astype(jnp.int32)
    kb0 = jnp.maximum(jnp.min(first) // 128, 0)
    kb1 = jnp.minimum((jnp.max(finish) + 127) // 128, 32)
    return first, finish, kb0, kb1


def queries(rows, qkvm, qkvo, qbm, qbo):
    wq = jnp.concatenate([qkvm[:, 0:128], qkvo[:, 0:128]], axis=1)
    bq = jnp.concatenate([qbm[:, 0:128], qbo[:, 0:128]], axis=1)
    return ((jnp.dot(rows, wq, preferred_element_type=F32) + bq) * Q_SCALE).astype(BF)


def pair_tools():
    half = lax.broadcasted_iota(jnp.int32, (32, 128), 0) < 16
    k_low = jnp.where(half, 1.0, 0.0).astype(BF)
    k_high = jnp.where(half, 0.0, 1.0).astype(BF)
    col_head = lax.broadcasted_iota(jnp.int32, (128, 128), 1) // 16
    cols = [jnp.where(col_head == a, 1.0, 0.0).astype(BF) for a in range(8)]

    def mask(kb, first, finish):
        key = kb * 128 + lax.broadcasted_iota(jnp.int32, (256, 128), 1)
        madd = jnp.where((key >= first) & (key < finish), 0.0, -jnp.inf)
        return jnp.concatenate([madd, madd], axis=1)

    def scores(Q8, p, kt, madd):
        part = kt[32 * p : 32 * p + 32, :]
        pair = jnp.concatenate([part * k_low, part * k_high], axis=1)
        return jnp.dot(Q8[p], pair, preferred_element_type=F32) + madd

    def step(kb, k0, Q8, KT, V, first, finish, M=None):
        kt = KT[:, pl.ds(k0, 128)]
        vb = V[pl.ds(k0, 128), :]
        madd = mask(kb, first, finish)
        out = []
        for h in range(2):
            vh = vb[:, 128 * h : 128 * h + 128]
            ps, vs = [], []
            for a in range(4):
                p = 4 * h + a
                s = scores(Q8, p, kt, madd)
                if M is not None:
                    s = s - M[p]
                ps.append(jnp.exp2(s).astype(BF))
                for c in (cols[2 * a], cols[2 * a + 1]):
                    vs.append(jnp.concatenate([vh * c, c], axis=1))
            out.append(
                jnp.dot(
                    jnp.concatenate(ps, axis=1),
                    jnp.concatenate(vs, axis=0),
                    preferred_element_type=F32,
                )
            )
        return out

    return mask, scores, step


def near_kernel(
    sc, plen, own, oth, qkvm, qkvo, qbm, qbo, acc_o, q_o, most_o, NE, KT, V, Q8,
):
    g, base, total = sc[0], sc[1], sc[2]
    spread(g, NE, 32, 0, own, oth)
    block = key_values(NE, KT, V, qkvm, qkvo, qbm, qbo)
    most = lax.fori_loop(0, 8, block, jnp.zeros((8, 256), F32))
    most_o[...] = jnp.broadcast_to(jnp.max(most), (8, 128))
    starts_row, ends_row = patch_rows(plen)
    mask, scores, step = pair_tools()

    def q_block(qb, _):
        r0 = pl.multiple_of(qb * 256, 256)
        q = queries(own[pl.ds(r0, 256), :], qkvm, qkvo, qbm, qbo)
        q_o[pl.ds(r0, 256), :] = q
        for p in range(8):
            Q8[p] = q[:, 32 * p : 32 * p + 32]
        first, finish, kb0, kb1 = limits(qb, g, base, total, starts_row, ends_row)
        acc_o[qb] = jnp.zeros((2, 256, 256), F32)

        def body(kb, _):
            k0 = pl.multiple_of((kb - 8) * 128, 128)
            for h, x in enumerate(step(kb, k0, Q8, KT, V, first, finish)):
                acc_o[qb, h] += x
            return 0

        lax.fori_loop(jnp.maximum(kb0, 8), jnp.minimum(kb1, 24), body, 0)
        return 0

    lax.fori_loop(0, 4, q_block, 0)


def near_call(*args):
    smem, vmem = pl.BlockSpec(memory_space=pltpu.SMEM), pl.BlockSpec(memory_space=pltpu.VMEM)
    return pl.pallas_call(
        near_kernel,
        out_shape=[
            jax.ShapeDtypeStruct((4, 2, 256, 256), F32),
            jax.ShapeDtypeStruct((1024, 256), BF),
            jax.ShapeDtypeStruct((8, 128), F32),
        ],
        in_specs=[smem] + [vmem] * (len(args) - 1),
        out_specs=[vmem] * 3,
        scratch_shapes=[
            pltpu.VMEM((2048, 256), BF),
            pltpu.VMEM((256, 2048), BF),
            pltpu.VMEM((2048, 256), BF),
            pltpu.VMEM((8, 256, 32), BF),
        ],
        compiler_params=pltpu.CompilerParams(vmem_limit_bytes=32 * 2**20),
        cost_estimate=pl.CostEstimate(
            flops=20 * 10**9, bytes_accessed=8 * 10**6, transcendentals=10**7
        ),
        name="near",
    )(*args)


def far_kernel(
    sc, sel, plen, own, oth, lo_own, lo_oth, hi_own, hi_oth, sec, acc_i, q_i, most_i, qkvm, qkvo,
    qbm, qbo, prw, prb, n2g, f1m, f1o, b1m, b1o, f2m, f2o, f2b, send, NE, KT, V, Q8, ACC, OUT, M,
):
    g, base, total = sc[0], sc[1], sc[2]
    spread(g, NE, 16, 0, lo_own, lo_oth)
    spread(g, NE, 16, 3072, hi_own, hi_oth)
    block = key_values(NE, KT, V, qkvm, qkvo, qbm, qbo)
    starts_row, ends_row = patch_rows(plen)
    edge_lo = limits(0, g, base, total, starts_row, ends_row)[2]
    edge_hi = limits(3, g, base, total, starts_row, ends_row)[3]
    most = lax.fori_loop(jnp.minimum(edge_lo // 2, 4), 4, block, jnp.zeros((8, 256), F32))
    most = lax.fori_loop(12, jnp.maximum((edge_hi + 1) // 2, 12), block, most)
    key_most = jnp.maximum(jnp.max(most), jnp.max(most_i[...]))
    mask, scores, step = pair_tools()
    hs = lax.broadcasted_iota(jnp.int32, (256, 128), 0) // 16
    hl = lax.broadcasted_iota(jnp.int32, (256, 128), 1)
    head_sel = jnp.where(hs == hl, 1.0, 0.0).astype(BF)
    prw_s = jnp.concatenate(
        [
            prw[pl.ds(pl.multiple_of(128 * g, 128), 128), :],
            prw[pl.ds(pl.multiple_of(128 - 128 * g, 128), 128), :],
        ],
        axis=0,
    )

    def q_most(r0):
        q = q_i[pl.ds(r0, 256), :]
        return jnp.max(jnp.dot(q * q, head_sel, preferred_element_type=F32))

    bound = q_most(0)
    for i in range(1, 4):
        bound = jnp.maximum(bound, q_most(256 * i))
    calm = bound * key_most * 1.05 <= 1e4

    @pl.when(jnp.logical_not(calm))
    def _():
        spread(g, NE, 32, 1024, own, oth)
        lax.fori_loop(4, 12, block, jnp.zeros((8, 256), F32))

    def q_block(qb, _):
        r0 = pl.multiple_of(qb * 256, 256)
        q = q_i[pl.ds(r0, 256), :]
        for p in range(8):
            Q8[p] = q[:, 32 * p : 32 * p + 32]
        first, finish, kb0, kb1 = limits(qb, g, base, total, starts_row, ends_row)

        def body(kb, _, M=None):
            k0 = pl.multiple_of(kb * 128, 128)
            for h, x in enumerate(step(kb, k0, Q8, KT, V, first, finish, M)):
                ACC[h] += x
            return 0

        @pl.when(calm)
        def _():
            ACC[...] = acc_i[qb]
            lax.fori_loop(kb0, jnp.minimum(kb1, 8), body, 0)
            lax.fori_loop(jnp.maximum(kb0, 24), kb1, body, 0)

        @pl.when(jnp.logical_not(calm))
        def _():
            ACC[...] = jnp.zeros_like(ACC)
            M[...] = jnp.full(M.shape, -jnp.inf, F32)

            def top(kb, _):
                kt = KT[:, pl.ds(pl.multiple_of(kb * 128, 128), 128)]
                madd = mask(kb, first, finish)
                for p in range(8):
                    M[p] = jnp.maximum(M[p], scores(Q8, p, kt, madd))
                return 0

            lax.fori_loop(kb0, kb1, top, 0)
            for p in range(8):
                for h in range(2):
                    part = M[p, :, 128 * h : 128 * h + 128]
                    M[p, :, 128 * h : 128 * h + 128] = jnp.broadcast_to(
                        jnp.max(part, axis=1, keepdims=True), (256, 128)
                    )
            lax.fori_loop(kb0, kb1, lambda kb, c: body(kb, c, M), 0)

        attn = jnp.concatenate(
            [ACC[h, :, 0:128] / ACC[h, :, 128:256] for h in range(2)], axis=1
        ).astype(BF)
        two = (
            sec[pl.ds(r0, 256), :].astype(F32)
            + jnp.dot(attn, prw_s, preferred_element_type=F32)
            + prb[...]
        ).astype(BF)
        wide = two.astype(F32)
        normed = layer_norm(wide, n2g[...]).astype(BF)
        total_rows = wide + f2b[...]
        for f1, b1, f2 in ((f1m, b1m, f2m), (f1o, b1o, f2o)):
            x = jnp.dot(normed, f1[...], preferred_element_type=F32) + b1[...]
            x = (0.5 * x * (1.0 + lax.erf(x * 0.7071067811865476))).astype(BF)
            total_rows = total_rows + jnp.dot(x, f2[...], preferred_element_type=F32)
        OUT[pl.ds(r0, 256), :] = total_rows.astype(BF)
        return 0

    lax.fori_loop(0, 4, q_block, 0)

    def place(d, _):
        send[pl.ds(pl.multiple_of(32 * d, 32), 32), :] = OUT[
            pl.ds(pl.multiple_of(32 * sel[d], 32), 32), :
        ]
        return 0

    lax.fori_loop(0, 64, place, 0, unroll=4)


def far_call(*args):
    smem, vmem = pl.BlockSpec(memory_space=pltpu.SMEM), pl.BlockSpec(memory_space=pltpu.VMEM)
    return pl.pallas_call(
        far_kernel,
        out_shape=jax.ShapeDtypeStruct((2048, 256), BF),
        in_specs=[smem] * 2 + [vmem] * (len(args) - 2),
        out_specs=vmem,
        scratch_shapes=[
            pltpu.VMEM((4096, 256), BF),
            pltpu.VMEM((256, 4096), BF),
            pltpu.VMEM((4096, 256), BF),
            pltpu.VMEM((8, 256, 32), BF),
            pltpu.VMEM((2, 256, 256), F32),
            pltpu.VMEM((1024, 256), BF),
            pltpu.VMEM((8, 256, 256), F32),
        ],
        compiler_params=pltpu.CompilerParams(vmem_limit_bytes=48 * 2**20),
        cost_estimate=pl.CostEstimate(
            flops=20 * 10**9, bytes_accessed=8 * 10**6, transcendentals=10**7
        ),
        name="far",
    )(*args)


def last_kernel(sc, src, inner, own, oth, out):
    g = sc[0]
    place = inner[...]
    place = place % 32 + jnp.where(place // 32 == g, 0, 32)
    perm = jnp.where(
        lax.broadcasted_iota(jnp.int32, (64, 64), 1) == place, 1.0, 0.0
    ).astype(BF)

    def step(k, _):
        s = pl.multiple_of(32 * src[k], 32)
        rows = jnp.concatenate([own[pl.ds(s, 32), :], oth[pl.ds(s, 32), :]], axis=0)
        out[pl.ds(pl.multiple_of(64 * k, 64), 64), :] = jnp.dot(
            perm, rows, preferred_element_type=F32
        ).astype(BF)
        return 0

    lax.fori_loop(0, 32, step, 0, unroll=4)


def last_call(*args):
    smem, vmem = pl.BlockSpec(memory_space=pltpu.SMEM), pl.BlockSpec(memory_space=pltpu.VMEM)
    return pl.pallas_call(
        last_kernel,
        out_shape=jax.ShapeDtypeStruct((2048, 256), BF),
        in_specs=[smem] * 2 + [vmem] * 3,
        out_specs=vmem,
        compiler_params=pltpu.CompilerParams(vmem_limit_bytes=16 * 2**20),
        name="relabel",
    )(*args)


def local(
    points, neighbours, patch_len, zorder, conv_w, conv_b, cpe_w, cpe_b, cpe_gain, norm1_gain,
    qkv_w, qkv_b, proj_w, proj_b, norm2_gain, fc1_w, fc1_b, fc2_w, fc2_b,
):
    g = lax.axis_index("grp").astype(jnp.int32)
    me = lax.axis_index("pts").astype(jnp.int32)
    peers = lax.axis_size("pts")
    rows = points.shape[0]
    forward = [(i, i + 1) for i in range(peers - 1)]
    backward = [(i + 1, i) for i in range(peers - 1)]

    def swap(x):
        return lax.ppermute(x, "grp", [(0, 1), (1, 0)])

    low = lax.ppermute(points[rows - 256 :], "pts", forward)
    high = lax.ppermute(points[:256], "pts", backward)
    conv_m = conv_w.reshape(27 * 256, 128)
    conv_o = swap(conv_m)
    small = jnp.concatenate([conv_b, qkv_b.reshape(384), fc1_b])
    small_o = swap(small)
    run = zorder[::64] // 64
    wanted = jnp.max(
        jnp.where(run[None, :] // 32 == jnp.arange(peers, dtype=jnp.int32)[:, None], run[None, :] % 32, 0),
        axis=1,
    )
    wanted = jnp.broadcast_to(wanted[:, None, None], (peers, 1, 128)).astype(jnp.int32)
    qkv_m = qkv_w.reshape(256, 384)
    qkv_o, fc1_o, fc2_o = swap(qkv_m), swap(fc1_w), swap(fc2_w)

    scalars = jnp.stack([g, me * rows, jnp.int32(rows * peers)])
    section_one, normed = conv_call(
        scalars, points, low, high, neighbours, conv_m, conv_o, small[None, :128],
        small_o[None, :128], cpe_w, cpe_b[None], cpe_gain[None], norm1_gain[None],
    )
    other = swap(normed)
    wanted, other = lax.optimization_barrier((wanted, other))
    sel = lax.all_to_all(wanted, "pts", split_axis=0, concat_axis=0, tiled=True)[:, 0, 0].astype(jnp.int32)
    lo_own = lax.ppermute(normed[512:], "pts", forward)
    hi_own = lax.ppermute(normed[:512], "pts", backward)
    lo_oth = lax.ppermute(
        normed[512:], ("pts", "grp"), [(2 * i + c, 2 * i + 3 - c) for i in range(peers - 1) for c in (0, 1)]
    )
    hi_oth = lax.ppermute(
        normed[:512], ("pts", "grp"), [(2 * i + 2 + c, 2 * i + 1 - c) for i in range(peers - 1) for c in (0, 1)]
    )
    weights = (
        qkv_m, qkv_o, small[None, 128:512], small_o[None, 128:512],
    )
    acc, query, most = near_call(scalars, patch_len[None], normed, other, *weights)
    send = far_call(
        scalars, sel, patch_len[None], normed, other, lo_own, lo_oth, hi_own, hi_oth, section_one,
        acc, query, most, *weights, proj_w, proj_b[None], norm2_gain[None], fc1_w, fc1_o,
        small[None, 512:], small_o[None, 512:], fc2_w, fc2_o, fc2_b[None],
    )
    got = lax.all_to_all(send, "pts", split_axis=0, concat_axis=0, tiled=True)
    return last_call(scalars, run // 32, (zorder[:64] % 64)[:, None], got, swap(got))


def solution(mesh):
    placed = (
        P("pts", None), P("pts", None), P(), P("pts"), P(None, None, "grp"), P("grp"), P(), P(), P(),
        P(), P(None, None, "grp"), P(None, "grp"), P(), P(), P(), P(None, "grp"), P("grp"),
        P("grp", None), P(),
    )
    return jax.shard_map(
        local, mesh=mesh, in_specs=placed, out_specs=P("pts", None), check_vma=False
    )
```

```python
import jax
import jax.numpy as jnp
from jax import lax
from jax.experimental import pallas as pl
from jax.experimental.pallas import tpu as pltpu
from jax.sharding import PartitionSpec as P

F32=jnp.float32; BF=jnp.bfloat16

Q_SCALE = 0.25 * 1.4426950408889634


def layer_norm(v, gain):
    c = v - jnp.mean(v, axis=-1, keepdims=True)
    s = jnp.mean(c * c, axis=-1, keepdims=True)
    return c * lax.rsqrt(s + 1e-05) * gain

RB = 128


def copies(sems, pairs):
    out = [pltpu.make_async_copy(src, dst, sems.at[i]) for i, (src, dst) in enumerate(pairs)]
    for copy in out:
        copy.start()
    return out


def wait(some):
    for copy in some:
        copy.wait()


def turned(ref, g):
    first = ref.at[pl.ds(pl.multiple_of(128 * g, 128), 128)]
    return first, ref.at[pl.ds(pl.multiple_of(128 - 128 * g, 128), 128)]


def conv_kernel(
    sc, pts, low, high, nbs, wm, wo, cbm, cbo, cpw, cpb, cpg, n1g, sec_o, nrm_o, lo_o, hi_o,
    X, NT, NB, OH, G, W, CW, CB, CV, sems,
):
    g = sc[0]
    base = sc[1]
    cw_a, cw_b = turned(cpw, g)
    started = copies(
        sems,
        [
            (nbs, NT), (pts, X.at[256:2304]), (low, X.at[0:256]), (high, X.at[2304:2560]),
            (wm, W.at[:, 0:128]), (wo, W.at[:, 128:256]), (cw_a, CW.at[0:128]),
            (cw_b, CW.at[128:256]), (cbm, CB.at[:, 0:128]), (cbo, CB.at[:, 128:256]),
            (cpb, CV.at[0]), (cpg, CV.at[1]), (n1g, CV.at[2]),
        ],
    )
    wait(started[:4])
    lanes = lax.broadcasted_iota(jnp.int32, (RB, 768), 1)
    for b in range(8):
        NB[256 * b : 256 * b + 256, :] = jnp.transpose(NT[:, 256 * b : 256 * b + 256])

    def block(b, _):
        rel = []
        for j in range(RB // 32):
            rel.append(NB[pl.ds(pl.multiple_of(256 * b + 64 * j + 32 * g, 32), 32), :])
        rel = jnp.concatenate(rel, axis=0)
        rel = jnp.where(rel < 0, -1, rel - (base + 256 * b - 256))
        for t in range(27):
            col = rel[:, t : t + 1]
            OH[t * RB : (t + 1) * RB, :] = jnp.where(
                lanes == col, jnp.array(1, BF), jnp.array(0, BF)
            )
        win = X[pl.ds(pl.multiple_of(256 * b, 256), 768), :]
        for q in range(3):
            out = jnp.dot(
                OH[q * 9 * RB : (q + 1) * 9 * RB, :], win, preferred_element_type=F32
            ).astype(BF)
            for t in range(9):
                G[
                    pl.ds(pl.multiple_of(b * RB, RB), RB),
                    (q * 9 + t) * 256 : (q * 9 + t + 1) * 256,
                ] = out[t * RB : (t + 1) * RB, :]
        return 0

    lax.fori_loop(0, 1024 // RB, block, 0)
    wait(started[4:])

    def finish(m, _):
        r0 = pl.multiple_of(m * 256, 256)
        acc = jnp.dot(G[pl.ds(r0, 256), :], W[...], preferred_element_type=F32)
        conv = (acc + CB[...]).astype(BF)
        c = jnp.dot(conv, CW[...], preferred_element_type=F32) + CV[0]
        own = []
        for j in range(8):
            own.append(X[pl.ds(pl.multiple_of(256 + 512 * m + 64 * j + 32 * g, 32), 32), :])
        own = jnp.concatenate(own, axis=0).astype(F32)
        sec = (own + layer_norm(c, CV[1])).astype(BF)
        sec_o[pl.ds(r0, 256), :] = sec
        normed = layer_norm(sec.astype(F32), CV[2]).astype(BF)
        nrm_o[pl.ds(r0, 256), :] = normed

        @pl.when(m < 2)
        def _():
            hi_o[pl.ds(r0, 256), :] = normed

        @pl.when(m >= 2)
        def _():
            lo_o[pl.ds(r0 - 512, 256), :] = normed

        return 0

    lax.fori_loop(0, 4, finish, 0)


def call(kernel, name, smem, args, out_shape, scratch, sems, mib, flops):
    return pl.pallas_call(
        kernel,
        out_shape=out_shape,
        in_specs=[pl.BlockSpec(memory_space=pltpu.SMEM)] * smem
        + [pl.BlockSpec(memory_space=pl.ANY)] * (len(args) - smem),
        out_specs=[pl.BlockSpec(memory_space=pltpu.VMEM)] * len(out_shape),
        scratch_shapes=[pltpu.VMEM(*x) for x in scratch] + [pltpu.SemaphoreType.DMA((sems,))],
        compiler_params=pltpu.CompilerParams(vmem_limit_bytes=mib * 2**20),
        cost_estimate=pl.CostEstimate(flops=flops, bytes_accessed=8 * 10**6, transcendentals=10**7),
        name=name,
    )(*args)


def conv_call(*args):
    out = [jax.ShapeDtypeStruct((n, 256), BF) for n in (1024, 1024, 512, 512)]
    scratch = [
        ((2560, 256), BF), ((27, 2048), jnp.int32), ((2048, 27), jnp.int32), ((27 * RB, 768), BF), ((1024, 6912), BF),
        ((6912, 256), BF), ((256, 256), BF), ((1, 256), F32), ((3, 1, 256), F32),
    ]
    return call(conv_kernel, "conv", 1, args, out, scratch, 13, 50, 30 * 10**9)


def key_values(NE, KT, V, QW, QB):
    wkt = [jnp.transpose(QW[h, 1]) for h in range(2)]
    bkc = [jnp.transpose(jnp.broadcast_to(QB[h, 1:2, :], (8, 128)))[:, :1] for h in range(2)]
    wv = jnp.concatenate([QW[0, 2], QW[1, 2]], axis=1)
    bv = jnp.concatenate([QB[0, 2:3, :], QB[1, 2:3, :]], axis=1)

    def block(i, most):
        r0 = pl.multiple_of(i * 256, 256)
        rows = NE[pl.ds(4 * i, 4)].reshape(256, 256)
        for h in range(2):
            kt = (
                lax.dot_general(
                    wkt[h], rows, (((1,), (1,)), ((), ())), preferred_element_type=F32
                )
                + bkc[h]
            )
            most = jnp.maximum(most, jnp.sum((kt * kt).reshape(8, 16, 256), axis=1))
            KT[128 * h : 128 * h + 128, pl.ds(r0, 256)] = kt.astype(BF)
        V[pl.ds(r0, 256), :] = (jnp.dot(rows, wv, preferred_element_type=F32) + bv).astype(BF)
        return most

    return block


def patch_rows(plen):
    lens = jnp.broadcast_to(plen.astype(F32), (256, 256))
    sub = lax.broadcasted_iota(jnp.int32, (256, 256), 0)
    lane = lax.broadcasted_iota(jnp.int32, (256, 256), 1)
    ends_col = jnp.sum(jnp.where(lane <= sub, lens, 0.0), axis=1, keepdims=True)
    ends_row = jnp.sum(jnp.where(lane == sub, ends_col, 0.0), axis=0, keepdims=True)
    return ends_row - plen.astype(F32), ends_row


def limits(qb, g, base, total, starts_row, ends_row):
    r = lax.broadcasted_iota(jnp.int32, (256, 1), 0)
    row = (base + 512 * qb + 64 * (r // 32) + 32 * g + r % 32).astype(F32)
    first = jnp.max(jnp.where(starts_row <= row, starts_row, 0.0), axis=1, keepdims=True)
    finish = jnp.min(jnp.where(ends_row > row, ends_row, total.astype(F32)), axis=1, keepdims=True)
    shift = (1024 - base).astype(F32)
    first = (first + shift).astype(jnp.int32)
    finish = (finish + shift).astype(jnp.int32)
    kb0 = jnp.maximum(jnp.min(first) // 128, 0)
    kb1 = jnp.minimum((jnp.max(finish) + 127) // 128, 32)
    return first, finish, kb0, kb1


def queries(rows, QW, QB):
    wq = jnp.concatenate([QW[0, 0], QW[1, 0]], axis=1)
    bq = jnp.concatenate([QB[0, 0:1, :], QB[1, 0:1, :]], axis=1)
    return ((jnp.dot(rows, wq, preferred_element_type=F32) + bq) * Q_SCALE).astype(BF)


def pair_tools():
    half = lax.broadcasted_iota(jnp.int32, (32, 128), 0) < 16
    k_low = jnp.where(half, 1.0, 0.0).astype(BF)
    k_high = jnp.where(half, 0.0, 1.0).astype(BF)
    col_head = lax.broadcasted_iota(jnp.int32, (128, 128), 1) // 16
    cols = [jnp.where(col_head == a, 1.0, 0.0).astype(BF) for a in range(8)]

    def mask(kb, first, finish):
        key = kb * 128 + lax.broadcasted_iota(jnp.int32, (256, 128), 1)
        madd = jnp.where((key >= first) & (key < finish), 0.0, -jnp.inf)
        return jnp.concatenate([madd, madd], axis=1)

    def scores(Q8, p, kt, madd):
        part = kt[32 * p : 32 * p + 32, :]
        pair = jnp.concatenate([part * k_low, part * k_high], axis=1)
        return jnp.dot(Q8[p], pair, preferred_element_type=F32) + madd

    def step(kb, k0, Q8, KT, V, first, finish, M=None):
        kt = KT[:, pl.ds(k0, 128)]
        vb = V[pl.ds(k0, 128), :]
        madd = mask(kb, first, finish)
        out = []
        for h in range(2):
            vh = vb[:, 128 * h : 128 * h + 128]
            ps, vs = [], []
            for a in range(4):
                p = 4 * h + a
                s = scores(Q8, p, kt, madd)
                if M is not None:
                    s = s - M[p]
                ps.append(jnp.exp2(s).astype(BF))
                for c in (cols[2 * a], cols[2 * a + 1]):
                    vs.append(jnp.concatenate([vh * c, c], axis=1))
            out.append(
                jnp.dot(
                    jnp.concatenate(ps, axis=1),
                    jnp.concatenate(vs, axis=0),
                    preferred_element_type=F32,
                )
            )
        return out

    return mask, scores, step


def near_kernel(
    sc, plen, own, oth, qkvm, qkvo, qbm, qbo, acc_o, q_o, most_o, NE, KT, V, Q8, QW, QB, PL, sems,
):
    g, base, total = sc[0], sc[1], sc[2]
    wait(
        copies(
            sems,
            [
                (own, NE.at[:, g]), (oth, NE.at[:, 1 - g]), (qkvm, QW.at[0]), (qkvo, QW.at[1]),
                (qbm, QB.at[0]), (qbo, QB.at[1]), (plen, PL),
            ],
        )
    )
    block = key_values(NE, KT, V, QW, QB)
    most = lax.fori_loop(0, 8, block, jnp.zeros((8, 256), F32))
    most_o[...] = jnp.broadcast_to(jnp.max(most), (8, 128))
    starts_row, ends_row = patch_rows(PL[...])
    mask, scores, step = pair_tools()

    def q_block(qb, _):
        r0 = pl.multiple_of(qb * 256, 256)
        q = queries(NE[pl.ds(8 * qb, 8), g].reshape(256, 256), QW, QB)
        q_o[pl.ds(r0, 256), :] = q
        for p in range(8):
            Q8[p] = q[:, 32 * p : 32 * p + 32]
        first, finish, kb0, kb1 = limits(qb, g, base, total, starts_row, ends_row)
        acc_o[qb] = jnp.zeros((2, 256, 256), F32)

        def body(kb, _):
            k0 = pl.multiple_of((kb - 8) * 128, 128)
            for h, x in enumerate(step(kb, k0, Q8, KT, V, first, finish)):
                acc_o[qb, h] += x
            return 0

        lax.fori_loop(jnp.maximum(kb0, 8), jnp.minimum(kb1, 24), body, 0)
        return 0

    lax.fori_loop(0, 4, q_block, 0)


QKV_SCRATCH = [((2, 3, 256, 128), BF), ((2, 3, 128), F32), ((1, 256), jnp.int32)]


def near_call(*args):
    out = [
        jax.ShapeDtypeStruct((4, 2, 256, 256), F32),
        jax.ShapeDtypeStruct((1024, 256), BF),
        jax.ShapeDtypeStruct((8, 128), F32),
    ]
    scratch = [
        ((32, 2, 32, 256), BF), ((256, 2048), BF), ((2048, 256), BF), ((8, 256, 32), BF),
    ] + QKV_SCRATCH
    return call(near_kernel, "near", 1, args, out, scratch, 7, 32, 20 * 10**9)


def far_kernel(
    sc, sel, plen, own, oth, lo_own, lo_oth, hi_own, hi_oth, sec_i, acc_i, q_i, most_i, qkvm, qkvo,
    qbm, qbo, prw, prb, n2g, f1m, f1o, b1m, b1o, f2m, f2o, f2b, send, NE, KT, V, Q8, ACC, OUT, M,
    SEC, AI, QI, MI, PW, VEC, F1, B1, F2, QW, QB, PL, sems,
):
    g, base, total = sc[0], sc[1], sc[2]
    pw_a, pw_b = turned(prw, g)
    started = copies(
        sems,
        [
            (lo_own, NE.at[0:16, g]), (lo_oth, NE.at[0:16, 1 - g]), (hi_own, NE.at[48:64, g]),
            (hi_oth, NE.at[48:64, 1 - g]), (qkvm, QW.at[0]), (qkvo, QW.at[1]), (qbm, QB.at[0]),
            (qbo, QB.at[1]), (plen, PL), (most_i, MI), (q_i, QI), (acc_i, AI), (sec_i, SEC),
            (pw_a, PW.at[0:128]), (pw_b, PW.at[128:256]), (prb, VEC.at[0]), (n2g, VEC.at[1]),
            (f2b, VEC.at[2]), (f1m, F1.at[0]), (f1o, F1.at[1]), (b1m, B1.at[0]), (b1o, B1.at[1]),
            (f2m, F2.at[0]), (f2o, F2.at[1]),
        ],
    )
    wait(started[:11])
    block = key_values(NE, KT, V, QW, QB)
    starts_row, ends_row = patch_rows(PL[...])
    edge_lo = limits(0, g, base, total, starts_row, ends_row)[2]
    edge_hi = limits(3, g, base, total, starts_row, ends_row)[3]
    most = lax.fori_loop(jnp.minimum(edge_lo // 2, 4), 4, block, jnp.zeros((8, 256), F32))
    most = lax.fori_loop(12, jnp.maximum((edge_hi + 1) // 2, 12), block, most)
    key_most = jnp.maximum(jnp.max(most), jnp.max(MI[...]))
    mask, scores, step = pair_tools()
    hs = lax.broadcasted_iota(jnp.int32, (256, 128), 0) // 16
    hl = lax.broadcasted_iota(jnp.int32, (256, 128), 1)
    head_sel = jnp.where(hs == hl, 1.0, 0.0).astype(BF)
    def q_most(r0):
        q = QI[pl.ds(r0, 256), :]
        return jnp.max(jnp.dot(q * q, head_sel, preferred_element_type=F32))

    bound = q_most(0)
    for i in range(1, 4):
        bound = jnp.maximum(bound, q_most(256 * i))
    calm = bound * key_most * 1.05 <= 1e4

    @pl.when(jnp.logical_not(calm))
    def _():
        wait(copies(sems.at[24:26], [(own, NE.at[16:48, g]), (oth, NE.at[16:48, 1 - g])]))
        lax.fori_loop(4, 12, block, jnp.zeros((8, 256), F32))

    wait(started[11:])

    def q_block(qb, _):
        r0 = pl.multiple_of(qb * 256, 256)
        q = QI[pl.ds(r0, 256), :]
        for p in range(8):
            Q8[p] = q[:, 32 * p : 32 * p + 32]
        first, finish, kb0, kb1 = limits(qb, g, base, total, starts_row, ends_row)

        def body(kb, _, M=None):
            k0 = pl.multiple_of(kb * 128, 128)
            for h, x in enumerate(step(kb, k0, Q8, KT, V, first, finish, M)):
                ACC[h] += x
            return 0

        @pl.when(calm)
        def _():
            ACC[...] = AI[qb]
            lax.fori_loop(kb0, jnp.minimum(kb1, 8), body, 0)
            lax.fori_loop(jnp.maximum(kb0, 24), kb1, body, 0)

        @pl.when(jnp.logical_not(calm))
        def _():
            ACC[...] = jnp.zeros_like(ACC)
            M[...] = jnp.full(M.shape, -jnp.inf, F32)

            def top(kb, _):
                kt = KT[:, pl.ds(pl.multiple_of(kb * 128, 128), 128)]
                madd = mask(kb, first, finish)
                for p in range(8):
                    M[p] = jnp.maximum(M[p], scores(Q8, p, kt, madd))
                return 0

            lax.fori_loop(kb0, kb1, top, 0)
            for p in range(8):
                for h in range(2):
                    part = M[p, :, 128 * h : 128 * h + 128]
                    M[p, :, 128 * h : 128 * h + 128] = jnp.broadcast_to(
                        jnp.max(part, axis=1, keepdims=True), (256, 128)
                    )
            lax.fori_loop(kb0, kb1, lambda kb, c: body(kb, c, M), 0)

        attn = jnp.concatenate(
            [ACC[h, :, 0:128] / ACC[h, :, 128:256] for h in range(2)], axis=1
        ).astype(BF)
        two = (
            SEC[pl.ds(r0, 256), :].astype(F32)
            + jnp.dot(attn, PW[...], preferred_element_type=F32)
            + VEC[0]
        ).astype(BF)
        wide = two.astype(F32)
        normed = layer_norm(wide, VEC[1]).astype(BF)
        total_rows = wide + VEC[2]
        for h in range(2):
            x = jnp.dot(normed, F1[h], preferred_element_type=F32) + B1[h]
            x = (0.5 * x * (1.0 + lax.erf(x * 0.7071067811865476))).astype(BF)
            total_rows = total_rows + jnp.dot(x, F2[h], preferred_element_type=F32)
        OUT[pl.ds(r0, 256), :] = total_rows.astype(BF)
        return 0

    lax.fori_loop(0, 4, q_block, 0)

    def place(d, _):
        send[pl.ds(pl.multiple_of(32 * d, 32), 32), :] = OUT[
            pl.ds(pl.multiple_of(32 * sel[d], 32), 32), :
        ]
        return 0

    lax.fori_loop(0, 64, place, 0, unroll=4)


def far_call(*args):
    scratch = [
        ((64, 2, 32, 256), BF), ((256, 4096), BF), ((4096, 256), BF), ((8, 256, 32), BF),
        ((2, 256, 256), F32), ((1024, 256), BF), ((8, 256, 256), F32), ((1024, 256), BF),
        ((4, 2, 256, 256), F32), ((1024, 256), BF), ((8, 128), F32), ((256, 256), BF),
        ((3, 1, 256), F32), ((2, 256, 512), BF), ((2, 1, 512), F32), ((2, 512, 256), BF),
    ] + QKV_SCRATCH
    out = [jax.ShapeDtypeStruct((2048, 256), BF)]
    return call(far_kernel, "far", 2, args, out, scratch, 26, 48, 20 * 10**9)[0]


def last_kernel(sc, zs, zv, own, oth, out, R, Z, sems, zsem):
    g = sc[0]
    order = pltpu.make_async_copy(zv, Z, zsem)
    order.start()

    def piece(k, side, ref):
        src = ref.at[zs[64 * k] // 2048]
        return pltpu.make_async_copy(src, R.at[k, side], sems.at[k, side])

    def start(k, _):
        piece(k, g, own).start()
        piece(k, 1 - g, oth).start()
        return 0

    lax.fori_loop(0, 32, start, 0, unroll=4)
    order.wait()
    place = jnp.where(
        lax.broadcasted_iota(jnp.int32, (64, 64), 0) == Z[0:1, 0:64] % 64, 1.0, 0.0
    )
    perm = jnp.transpose(place).astype(BF)

    def step(k, _):
        piece(k, g, own).wait()
        piece(k, 1 - g, oth).wait()
        out[pl.ds(pl.multiple_of(64 * k, 64), 64), :] = jnp.dot(
            perm, R[k].reshape(64, 256), preferred_element_type=F32
        ).astype(BF)
        return 0

    lax.fori_loop(0, 32, step, 0, unroll=4)


def last_call(*args):
    smem, hbm = pl.BlockSpec(memory_space=pltpu.SMEM), pl.BlockSpec(memory_space=pl.ANY)
    return pl.pallas_call(
        last_kernel,
        out_shape=jax.ShapeDtypeStruct((2048, 256), BF),
        in_specs=[smem] * 2 + [hbm] * 3,
        out_specs=pl.BlockSpec(memory_space=pltpu.VMEM),
        scratch_shapes=[
            pltpu.VMEM((32, 2, 32, 256), BF),
            pltpu.VMEM((16, 128), jnp.int32),
            pltpu.SemaphoreType.DMA((32, 2)),
            pltpu.SemaphoreType.DMA,
        ],
        compiler_params=pltpu.CompilerParams(vmem_limit_bytes=16 * 2**20),
        name="relabel",
    )(*args)


def local(
    points, neighbours, patch_len, zorder, conv_w, conv_b, cpe_w, cpe_b, cpe_gain, norm1_gain,
    qkv_w, qkv_b, proj_w, proj_b, norm2_gain, fc1_w, fc1_b, fc2_w, fc2_b,
):
    g = lax.axis_index("grp").astype(jnp.int32)
    me = lax.axis_index("pts").astype(jnp.int32)
    peers = lax.axis_size("pts")
    rows = points.shape[0]
    forward = [(i, i + 1) for i in range(peers - 1)]
    backward = [(i + 1, i) for i in range(peers - 1)]

    def swap(x):
        return lax.ppermute(x, "grp", [(0, 1), (1, 0)])

    def pieces(x):
        return x.reshape(-1, 32, 256)

    order = zorder.reshape(16, 128)
    inner = [[8 * i + j for j in range(8)] for i in range(8)]
    outer = [[8 * j + i for j in range(8)] for i in range(8)]
    table = lax.all_gather(
        jnp.concatenate([order] * 16), "pts", axis=0, tiled=False, axis_index_groups=inner
    )[:, :32].reshape(256, 128)
    table = lax.all_gather(table, "pts", axis=0, tiled=True, axis_index_groups=outer)
    low = lax.ppermute(points[rows - 256 :], "pts", forward)
    high = lax.ppermute(points[:256], "pts", backward)
    conv_m = conv_w.reshape(27 * 256, 128)
    conv_o, bias_o = swap(conv_m), swap(conv_b)
    scalars = jnp.stack([g, me * rows, jnp.int32(rows * peers)])
    section_one, normed, lo_half, hi_half = conv_call(
        scalars, points, low, high, neighbours.T, conv_m, conv_o, conv_b[None], bias_o[None],
        cpe_w, cpe_b[None], cpe_gain[None], norm1_gain[None],
    )
    qkv_m = jnp.transpose(qkv_w, (1, 0, 2))
    weights = (qkv_m, swap(qkv_m), qkv_b, swap(qkv_b))
    fc1_o, fc2_o, b1_o = swap(fc1_w), swap(fc2_w), swap(fc1_b)
    other = swap(normed)
    lo_own = lax.ppermute(lo_half, "pts", forward)
    hi_own = lax.ppermute(hi_half, "pts", backward)
    acc, query, most = near_call(scalars, patch_len[None], pieces(normed), pieces(other), *weights)
    lo_own, hi_own, most = lax.optimization_barrier((lo_own, hi_own, most))
    lo_oth, hi_oth = swap(lo_own), swap(hi_own)
    table = table.reshape(peers, 32, 128)
    sel = jnp.max(jnp.where(table // rows == me, table % rows // 64, 0), axis=(1, 2))
    send = far_call(
        scalars, sel, patch_len[None], pieces(normed), pieces(other), pieces(lo_own),
        pieces(lo_oth), pieces(hi_own), pieces(hi_oth), section_one, acc, query, most, *weights,
        proj_w, proj_b[None], norm2_gain[None], fc1_w, fc1_o, fc1_b[None], b1_o[None], fc2_w,
        fc2_o, fc2_b[None],
    )
    got = lax.all_to_all(send, "pts", split_axis=0, concat_axis=0, tiled=True)
    return last_call(scalars, zorder, order, pieces(got), pieces(swap(got)))


def solution(mesh):
    placed = (
        P("pts", None), P("pts", None), P(), P("pts"), P(None, None, "grp"), P("grp"), P(), P(), P(),
        P(), P(None, None, "grp"), P(None, "grp"), P(), P(), P(), P(None, "grp"), P("grp"),
        P("grp", None), P(),
    )
    return jax.shard_map(
        local, mesh=mesh, in_specs=placed, out_specs=P("pts", None), check_vma=False
    )
```

```python
import jax
import jax.numpy as jnp
from jax import lax
from jax.experimental import pallas as pl
from jax.experimental.pallas import tpu as pltpu
from jax.sharding import PartitionSpec as P

F32=jnp.float32; BF=jnp.bfloat16

VMEM_BYTES = 64 * 2**20 - 65536
Q_SCALE = 0.25 * 1.4426950408889634


def layer_norm(v, gain):
    c = v - jnp.mean(v, axis=-1, keepdims=True)
    s = jnp.mean(c * c, axis=-1, keepdims=True)
    return c * lax.rsqrt(s + 1e-05) * gain

RB = 128


def copies(sems, pairs):
    out = [pltpu.make_async_copy(src, dst, sems.at[i]) for i, (src, dst) in enumerate(pairs)]
    for copy in out:
        copy.start()
    return out


def wait(some):
    for copy in some:
        copy.wait()


def turned(ref, g):
    first = ref.at[pl.ds(pl.multiple_of(128 * g, 128), 128)]
    return first, ref.at[pl.ds(pl.multiple_of(128 - 128 * g, 128), 128)]


def conv_kernel(
    sc, pts, low, high, nbs, wm, wo, cbm, cbo, cpw, cpb, cpg, n1g, sec_o, nrm_o, lo_o, hi_o,
    X, NT, NB, OH, G, W, CW, CB, CV, sems,
):
    g = sc[0]
    base = sc[1]
    cw_a, cw_b = turned(cpw, g)
    started = copies(
        sems,
        [
            (nbs, NT), (pts, X.at[256:2304]), (low, X.at[0:256]), (high, X.at[2304:2560]),
            (wm, W.at[:, 0:128]), (wo, W.at[:, 128:256]), (cw_a, CW.at[0:128]),
            (cw_b, CW.at[128:256]), (cbm, CB.at[:, 0:128]), (cbo, CB.at[:, 128:256]),
            (cpb, CV.at[0]), (cpg, CV.at[1]), (n1g, CV.at[2]),
        ],
    )
    wait(started[:4])
    lanes = lax.broadcasted_iota(jnp.int32, (RB, 768), 1)
    for b in range(8):
        NB[256 * b : 256 * b + 256, :] = jnp.transpose(NT[:, 256 * b : 256 * b + 256])

    def block(b, _):
        rel = []
        for j in range(RB // 32):
            rel.append(NB[pl.ds(pl.multiple_of(256 * b + 64 * j + 32 * g, 32), 32), :])
        rel = jnp.concatenate(rel, axis=0)
        rel = jnp.where(rel < 0, -1, rel - (base + 256 * b - 256))
        for t in range(27):
            col = rel[:, t : t + 1]
            OH[t * RB : (t + 1) * RB, :] = jnp.where(
                lanes == col, jnp.array(1, BF), jnp.array(0, BF)
            )
        win = X[pl.ds(pl.multiple_of(256 * b, 256), 768), :]
        for q in range(3):
            out = jnp.dot(
                OH[q * 9 * RB : (q + 1) * 9 * RB, :], win, preferred_element_type=F32
            ).astype(BF)
            for t in range(9):
                G[
                    pl.ds(pl.multiple_of(b * RB, RB), RB),
                    (q * 9 + t) * 256 : (q * 9 + t + 1) * 256,
                ] = out[t * RB : (t + 1) * RB, :]
        return 0

    lax.fori_loop(0, 1024 // RB, block, 0)
    wait(started[4:])

    def finish(m, _):
        r0 = pl.multiple_of(m * 256, 256)
        acc = jnp.dot(G[pl.ds(r0, 256), :], W[...], preferred_element_type=F32)
        conv = (acc + CB[...]).astype(BF)
        c = jnp.dot(conv, CW[...], preferred_element_type=F32) + CV[0]
        own = []
        for j in range(8):
            own.append(X[pl.ds(pl.multiple_of(256 + 512 * m + 64 * j + 32 * g, 32), 32), :])
        own = jnp.concatenate(own, axis=0).astype(F32)
        sec = (own + layer_norm(c, CV[1])).astype(BF)
        sec_o[pl.ds(r0, 256), :] = sec
        normed = layer_norm(sec.astype(F32), CV[2]).astype(BF)
        nrm_o[pl.ds(r0, 256), :] = normed

        @pl.when(m < 2)
        def _():
            hi_o[pl.ds(r0, 256), :] = normed

        @pl.when(m >= 2)
        def _():
            lo_o[pl.ds(r0 - 512, 256), :] = normed

        return 0

    lax.fori_loop(0, 4, finish, 0)


def call(kernel, name, smem, args, out_shape, scratch, sems, flops):
    return pl.pallas_call(
        kernel,
        out_shape=out_shape,
        in_specs=[pl.BlockSpec(memory_space=pltpu.SMEM)] * smem
        + [pl.BlockSpec(memory_space=pltpu.HBM)] * (len(args) - smem),
        out_specs=[pl.BlockSpec(memory_space=pltpu.VMEM)] * len(out_shape),
        scratch_shapes=[pltpu.VMEM(*x) for x in scratch] + [pltpu.SemaphoreType.DMA((sems,))],
        compiler_params=pltpu.CompilerParams(vmem_limit_bytes=VMEM_BYTES),
        cost_estimate=pl.CostEstimate(flops=flops, bytes_accessed=8 * 10**6, transcendentals=10**7),
        name=name,
    )(*args)


def conv_call(*args):
    out = [jax.ShapeDtypeStruct((n, 256), BF) for n in (1024, 1024, 512, 512)]
    scratch = [
        ((2560, 256), BF), ((27, 2048), jnp.int32), ((2048, 27), jnp.int32), ((27 * RB, 768), BF), ((1024, 6912), BF),
        ((6912, 256), BF), ((256, 256), BF), ((1, 256), F32), ((3, 1, 256), F32),
    ]
    return call(conv_kernel, "conv", 1, args, out, scratch, 13, 30 * 10**9)


def key_values(NE, KT, V, QW, QB):
    wkt = [jnp.transpose(QW[h, 1]) for h in range(2)]
    bkc = [jnp.transpose(jnp.broadcast_to(QB[h, 1:2, :], (8, 128)))[:, :1] for h in range(2)]
    wv = jnp.concatenate([QW[0, 2], QW[1, 2]], axis=1)
    bv = jnp.concatenate([QB[0, 2:3, :], QB[1, 2:3, :]], axis=1)

    def block(i, most):
        r0 = pl.multiple_of(i * 256, 256)
        rows = NE[pl.ds(4 * i, 4)].reshape(256, 256)
        for h in range(2):
            kt = (
                lax.dot_general(
                    wkt[h], rows, (((1,), (1,)), ((), ())), preferred_element_type=F32
                )
                + bkc[h]
            )
            most = jnp.maximum(most, jnp.sum((kt * kt).reshape(8, 16, 256), axis=1))
            KT[128 * h : 128 * h + 128, pl.ds(r0, 256)] = kt.astype(BF)
        V[pl.ds(r0, 256), :] = (jnp.dot(rows, wv, preferred_element_type=F32) + bv).astype(BF)
        return most

    return block


def patch_rows(plen):
    lens = jnp.broadcast_to(plen.astype(F32), (256, 256))
    sub = lax.broadcasted_iota(jnp.int32, (256, 256), 0)
    lane = lax.broadcasted_iota(jnp.int32, (256, 256), 1)
    ends_col = jnp.sum(jnp.where(lane <= sub, lens, 0.0), axis=1, keepdims=True)
    ends_row = jnp.sum(jnp.where(lane == sub, ends_col, 0.0), axis=0, keepdims=True)
    return ends_row - plen.astype(F32), ends_row


def limits(qb, g, base, total, starts_row, ends_row):
    r = lax.broadcasted_iota(jnp.int32, (256, 1), 0)
    row = (base + 512 * qb + 64 * (r // 32) + 32 * g + r % 32).astype(F32)
    first = jnp.max(jnp.where(starts_row <= row, starts_row, 0.0), axis=1, keepdims=True)
    finish = jnp.min(jnp.where(ends_row > row, ends_row, total.astype(F32)), axis=1, keepdims=True)
    shift = (1024 - base).astype(F32)
    first = (first + shift).astype(jnp.int32)
    finish = (finish + shift).astype(jnp.int32)
    kb0 = jnp.maximum(jnp.min(first) // 128, 0)
    kb1 = jnp.minimum((jnp.max(finish) + 127) // 128, 32)
    return first, finish, kb0, kb1


def queries(rows, QW, QB):
    wq = jnp.concatenate([QW[0, 0], QW[1, 0]], axis=1)
    bq = jnp.concatenate([QB[0, 0:1, :], QB[1, 0:1, :]], axis=1)
    return ((jnp.dot(rows, wq, preferred_element_type=F32) + bq) * Q_SCALE).astype(BF)


def pair_tools():
    half = lax.broadcasted_iota(jnp.int32, (32, 128), 0) < 16
    k_low = jnp.where(half, 1.0, 0.0).astype(BF)
    k_high = jnp.where(half, 0.0, 1.0).astype(BF)
    col_head = lax.broadcasted_iota(jnp.int32, (128, 128), 1) // 16
    cols = [jnp.where(col_head == a, 1.0, 0.0).astype(BF) for a in range(8)]

    def mask(kb, first, finish):
        key = kb * 128 + lax.broadcasted_iota(jnp.int32, (256, 128), 1)
        madd = jnp.where((key >= first) & (key < finish), 0.0, -jnp.inf)
        return jnp.concatenate([madd, madd], axis=1)

    def scores(Q8, p, kt, madd):
        part = kt[32 * p : 32 * p + 32, :]
        pair = jnp.concatenate([part * k_low, part * k_high], axis=1)
        return jnp.dot(Q8[p], pair, preferred_element_type=F32) + madd

    def step(kb, k0, Q8, KT, V, first, finish, M=None):
        kt = KT[:, pl.ds(k0, 128)]
        vb = V[pl.ds(k0, 128), :]
        madd = mask(kb, first, finish)
        out = []
        for h in range(2):
            vh = vb[:, 128 * h : 128 * h + 128]
            ps, vs = [], []
            for a in range(4):
                p = 4 * h + a
                s = scores(Q8, p, kt, madd)
                if M is not None:
                    s = s - M[p]
                ps.append(jnp.exp2(s).astype(BF))
                for c in (cols[2 * a], cols[2 * a + 1]):
                    vs.append(jnp.concatenate([vh * c, c], axis=1))
            out.append(
                jnp.dot(
                    jnp.concatenate(ps, axis=1),
                    jnp.concatenate(vs, axis=0),
                    preferred_element_type=F32,
                )
            )
        return out

    return mask, scores, step


def near_kernel(
    sc, plen, own, oth, qkvm, qkvo, qbm, qbo, acc_o, q_o, most_o, NE, KT, V, Q8, QW, QB, PL, sems,
):
    g, base, total = sc[0], sc[1], sc[2]
    wait(
        copies(
            sems,
            [
                (own, NE.at[:, g]), (oth, NE.at[:, 1 - g]), (qkvm, QW.at[0]), (qkvo, QW.at[1]),
                (qbm, QB.at[0]), (qbo, QB.at[1]), (plen, PL),
            ],
        )
    )
    block = key_values(NE, KT, V, QW, QB)
    most = lax.fori_loop(0, 8, block, jnp.zeros((8, 256), F32))
    most_o[...] = jnp.broadcast_to(jnp.max(most), (8, 128))
    starts_row, ends_row = patch_rows(PL[...])
    mask, scores, step = pair_tools()

    def q_block(qb, _):
        r0 = pl.multiple_of(qb * 256, 256)
        q = queries(NE[pl.ds(8 * qb, 8), g].reshape(256, 256), QW, QB)
        q_o[pl.ds(r0, 256), :] = q
        for p in range(8):
            Q8[p] = q[:, 32 * p : 32 * p + 32]
        first, finish, kb0, kb1 = limits(qb, g, base, total, starts_row, ends_row)
        acc_o[qb] = jnp.zeros((2, 256, 256), F32)

        def body(kb, _):
            k0 = pl.multiple_of((kb - 8) * 128, 128)
            for h, x in enumerate(step(kb, k0, Q8, KT, V, first, finish)):
                acc_o[qb, h] += x
            return 0

        lax.fori_loop(jnp.maximum(kb0, 8), jnp.minimum(kb1, 24), body, 0)
        return 0

    lax.fori_loop(0, 4, q_block, 0)


QKV_SCRATCH = [((2, 3, 256, 128), BF), ((2, 3, 128), F32), ((1, 256), jnp.int32)]


def near_call(*args):
    out = [
        jax.ShapeDtypeStruct((4, 2, 256, 256), F32),
        jax.ShapeDtypeStruct((1024, 256), BF),
        jax.ShapeDtypeStruct((8, 128), F32),
    ]
    scratch = [
        ((32, 2, 32, 256), BF), ((256, 2048), BF), ((2048, 256), BF), ((8, 256, 32), BF),
    ] + QKV_SCRATCH
    return call(near_kernel, "near", 1, args, out, scratch, 7, 20 * 10**9)


def far_kernel(
    sc, sel, plen, own, oth, lo_own, lo_oth, hi_own, hi_oth, sec_i, acc_i, q_i, most_i, qkvm, qkvo,
    qbm, qbo, prw, prb, n2g, f1m, f1o, b1m, b1o, f2m, f2o, f2b, send, NE, KT, V, Q8, ACC, OUT, M,
    SEC, AI, QI, MI, PW, VEC, F1, B1, F2, QW, QB, PL, sems,
):
    g, base, total = sc[0], sc[1], sc[2]
    pw_a, pw_b = turned(prw, g)
    started = copies(
        sems,
        [
            (lo_own, NE.at[0:16, g]), (lo_oth, NE.at[0:16, 1 - g]), (hi_own, NE.at[48:64, g]),
            (hi_oth, NE.at[48:64, 1 - g]), (qkvm, QW.at[0]), (qkvo, QW.at[1]), (qbm, QB.at[0]),
            (qbo, QB.at[1]), (plen, PL), (most_i, MI), (q_i, QI), (acc_i, AI), (sec_i, SEC),
            (pw_a, PW.at[0:128]), (pw_b, PW.at[128:256]), (prb, VEC.at[0]), (n2g, VEC.at[1]),
            (f2b, VEC.at[2]), (f1m, F1.at[0]), (f1o, F1.at[1]), (b1m, B1.at[0]), (b1o, B1.at[1]),
            (f2m, F2.at[0]), (f2o, F2.at[1]),
        ],
    )
    wait(started[:11])
    block = key_values(NE, KT, V, QW, QB)
    starts_row, ends_row = patch_rows(PL[...])
    edge_lo = limits(0, g, base, total, starts_row, ends_row)[2]
    edge_hi = limits(3, g, base, total, starts_row, ends_row)[3]
    most = lax.fori_loop(jnp.minimum(edge_lo // 2, 4), 4, block, jnp.zeros((8, 256), F32))
    most = lax.fori_loop(12, jnp.maximum((edge_hi + 1) // 2, 12), block, most)
    key_most = jnp.maximum(jnp.max(most), jnp.max(MI[...]))
    mask, scores, step = pair_tools()
    hs = lax.broadcasted_iota(jnp.int32, (256, 128), 0) // 16
    hl = lax.broadcasted_iota(jnp.int32, (256, 128), 1)
    head_sel = jnp.where(hs == hl, 1.0, 0.0).astype(BF)
    def q_most(r0):
        q = QI[pl.ds(r0, 256), :]
        return jnp.max(jnp.dot(q * q, head_sel, preferred_element_type=F32))

    bound = q_most(0)
    for i in range(1, 4):
        bound = jnp.maximum(bound, q_most(256 * i))
    calm = bound * key_most * 1.05 <= 1e4

    @pl.when(jnp.logical_not(calm))
    def _():
        wait(copies(sems.at[24:26], [(own, NE.at[16:48, g]), (oth, NE.at[16:48, 1 - g])]))
        lax.fori_loop(4, 12, block, jnp.zeros((8, 256), F32))

    wait(started[11:])

    def q_block(qb, _):
        r0 = pl.multiple_of(qb * 256, 256)
        q = QI[pl.ds(r0, 256), :]
        for p in range(8):
            Q8[p] = q[:, 32 * p : 32 * p + 32]
        first, finish, kb0, kb1 = limits(qb, g, base, total, starts_row, ends_row)

        def body(kb, _, M=None):
            k0 = pl.multiple_of(kb * 128, 128)
            for h, x in enumerate(step(kb, k0, Q8, KT, V, first, finish, M)):
                ACC[h] += x
            return 0

        @pl.when(calm)
        def _():
            ACC[...] = AI[qb]
            lax.fori_loop(kb0, jnp.minimum(kb1, 8), body, 0)
            lax.fori_loop(jnp.maximum(kb0, 24), kb1, body, 0)

        @pl.when(jnp.logical_not(calm))
        def _():
            ACC[...] = jnp.zeros_like(ACC)
            M[...] = jnp.full(M.shape, -jnp.inf, F32)

            def top(kb, _):
                kt = KT[:, pl.ds(pl.multiple_of(kb * 128, 128), 128)]
                madd = mask(kb, first, finish)
                for p in range(8):
                    M[p] = jnp.maximum(M[p], scores(Q8, p, kt, madd))
                return 0

            lax.fori_loop(kb0, kb1, top, 0)
            for p in range(8):
                for h in range(2):
                    part = M[p, :, 128 * h : 128 * h + 128]
                    M[p, :, 128 * h : 128 * h + 128] = jnp.broadcast_to(
                        jnp.max(part, axis=1, keepdims=True), (256, 128)
                    )
            lax.fori_loop(kb0, kb1, lambda kb, c: body(kb, c, M), 0)

        attn = jnp.concatenate(
            [ACC[h, :, 0:128] / ACC[h, :, 128:256] for h in range(2)], axis=1
        ).astype(BF)
        two = (
            SEC[pl.ds(r0, 256), :].astype(F32)
            + jnp.dot(attn, PW[...], preferred_element_type=F32)
            + VEC[0]
        ).astype(BF)
        wide = two.astype(F32)
        normed = layer_norm(wide, VEC[1]).astype(BF)
        total_rows = wide + VEC[2]
        for h in range(2):
            x = jnp.dot(normed, F1[h], preferred_element_type=F32) + B1[h]
            x = (0.5 * x * (1.0 + lax.erf(x * 0.7071067811865476))).astype(BF)
            total_rows = total_rows + jnp.dot(x, F2[h], preferred_element_type=F32)
        OUT[pl.ds(r0, 256), :] = total_rows.astype(BF)
        return 0

    lax.fori_loop(0, 4, q_block, 0)

    def place(d, _):
        send[pl.ds(pl.multiple_of(32 * d, 32), 32), :] = OUT[
            pl.ds(pl.multiple_of(32 * sel[d], 32), 32), :
        ]
        return 0

    lax.fori_loop(0, 64, place, 0, unroll=4)


def far_call(*args):
    scratch = [
        ((64, 2, 32, 256), BF), ((256, 4096), BF), ((4096, 256), BF), ((8, 256, 32), BF),
        ((2, 256, 256), F32), ((1024, 256), BF), ((8, 256, 256), F32), ((1024, 256), BF),
        ((4, 2, 256, 256), F32), ((1024, 256), BF), ((8, 128), F32), ((256, 256), BF),
        ((3, 1, 256), F32), ((2, 256, 512), BF), ((2, 1, 512), F32), ((2, 512, 256), BF),
    ] + QKV_SCRATCH
    out = [jax.ShapeDtypeStruct((2048, 256), BF)]
    return call(far_kernel, "far", 2, args, out, scratch, 26, 20 * 10**9)[0]


def last_kernel(sc, zs, zv, own, oth, out, R, Z, sems):
    g = sc[0]
    wait(copies(sems, [(zv, Z), (own, R.at[:, g]), (oth, R.at[:, 1 - g])]))
    place = jnp.where(
        lax.broadcasted_iota(jnp.int32, (64, 64), 0) == Z[0:1, 0:64] % 64, 1.0, 0.0
    )
    perm = jnp.transpose(place).astype(BF)

    def step(k, _):
        rows = R[lax.shift_right_logical(zs[64 * k], 11)].reshape(64, 256)
        out[pl.ds(pl.multiple_of(64 * k, 64), 64), :] = jnp.dot(
            perm, rows, preferred_element_type=F32
        ).astype(BF)
        return 0

    lax.fori_loop(0, 32, step, 0, unroll=8)


def last_call(*args):
    out = [jax.ShapeDtypeStruct((2048, 256), BF)]
    scratch = [((64, 2, 32, 256), BF), ((16, 128), jnp.int32)]
    return call(last_kernel, "relabel", 2, args, out, scratch, 3, 10**9)[0]


def local(
    points, neighbours, patch_len, zorder, conv_w, conv_b, cpe_w, cpe_b, cpe_gain, norm1_gain,
    qkv_w, qkv_b, proj_w, proj_b, norm2_gain, fc1_w, fc1_b, fc2_w, fc2_b,
):
    g = lax.axis_index("grp").astype(jnp.int32)
    me = lax.axis_index("pts").astype(jnp.int32)
    peers = lax.axis_size("pts")
    rows = points.shape[0]
    forward = [(i, i + 1) for i in range(peers - 1)]
    backward = [(i + 1, i) for i in range(peers - 1)]

    def swap(x):
        return lax.ppermute(x, "grp", [(0, 1), (1, 0)])

    def pieces(x):
        return x.reshape(-1, 32, 256)

    order = zorder.reshape(16, 128)
    inner = [[8 * i + j for j in range(8)] for i in range(8)]
    outer = [[8 * j + i for j in range(8)] for i in range(8)]
    sources = jnp.arange(64, dtype=jnp.int32).reshape(8, 8).T[:, :, None, None]
    wanted = jnp.max(
        jnp.where(order // rows == sources, order % rows // 64, 0), axis=2
    )
    wanted = lax.all_to_all(
        wanted, "pts", split_axis=0, concat_axis=0, tiled=True, axis_index_groups=inner
    )
    low = lax.ppermute(points[rows - 256 :], "pts", forward)
    high = lax.ppermute(points[:256], "pts", backward)
    wanted, low = lax.optimization_barrier((wanted, low))
    conv_m = conv_w.reshape(27 * 256, 128)
    conv_o, bias_o = swap(conv_m), swap(conv_b)
    scalars = jnp.stack([g, me * rows, jnp.int32(rows * peers)])
    section_one, normed, lo_half, hi_half = conv_call(
        scalars, points, low, high, neighbours.T, conv_m, conv_o, conv_b[None], bias_o[None],
        cpe_w, cpe_b[None], cpe_gain[None], norm1_gain[None],
    )
    qkv_m = jnp.transpose(qkv_w, (1, 0, 2))
    weights = (qkv_m, swap(qkv_m), qkv_b, swap(qkv_b))
    fc1_o, fc2_o, b1_o = swap(fc1_w), swap(fc2_w), swap(fc1_b)
    other = swap(normed)
    wanted, other = lax.optimization_barrier((jnp.transpose(wanted, (1, 0, 2)), other))
    sel = lax.all_to_all(
        wanted, "pts", split_axis=0, concat_axis=0, tiled=True, axis_index_groups=outer
    )
    lo_own = lax.ppermute(lo_half, "pts", forward)
    hi_own = lax.ppermute(hi_half, "pts", backward)
    acc, query, most = near_call(scalars, patch_len[None], pieces(normed), pieces(other), *weights)
    lo_own, hi_own, most = lax.optimization_barrier((lo_own, hi_own, most))
    lo_oth, hi_oth = swap(lo_own), swap(hi_own)
    sel = jnp.max(sel, axis=2).reshape(64)
    send = far_call(
        scalars, sel, patch_len[None], pieces(normed), pieces(other), pieces(lo_own),
        pieces(lo_oth), pieces(hi_own), pieces(hi_oth), section_one, acc, query, most, *weights,
        proj_w, proj_b[None], norm2_gain[None], fc1_w, fc1_o, fc1_b[None], b1_o[None], fc2_w,
        fc2_o, fc2_b[None],
    )
    got = lax.all_to_all(send, "pts", split_axis=0, concat_axis=0, tiled=True)
    return last_call(scalars, zorder, order, pieces(got), pieces(swap(got)))


def solution(mesh):
    placed = (
        P("pts", None), P("pts", None), P(), P("pts"), P(None, None, "grp"), P("grp"), P(), P(), P(),
        P(), P(None, None, "grp"), P(None, "grp"), P(), P(), P(), P(None, "grp"), P("grp"),
        P("grp", None), P(),
    )
    return jax.shard_map(
        local, mesh=mesh, in_specs=placed, out_specs=P("pts", None), check_vma=False
    )
```

```python
import jax
import jax.numpy as jnp
from jax import lax
from jax.experimental import pallas as pl
from jax.experimental.pallas import tpu as pltpu
from jax.sharding import PartitionSpec as P

F32=jnp.float32; BF=jnp.bfloat16

VMEM_BYTES = 64 * 2**20 - 65536
Q_SCALE = 0.25 * 1.4426950408889634


def layer_norm(v, gain):
    c = v - jnp.mean(v, axis=-1, keepdims=True)
    s = jnp.mean(c * c, axis=-1, keepdims=True)
    return c * lax.rsqrt(s + 1e-05) * gain

RB = 128


def copies(sems, pairs):
    out = [pltpu.make_async_copy(src, dst, sems.at[i]) for i, (src, dst) in enumerate(pairs)]
    for copy in out:
        copy.start()
    return out


def wait(some):
    for copy in some:
        copy.wait()


def turned(ref, g):
    first = ref.at[pl.ds(pl.multiple_of(128 * g, 128), 128)]
    return first, ref.at[pl.ds(pl.multiple_of(128 - 128 * g, 128), 128)]


def conv_kernel(
    sc, pts, low, high, nbs, wm, wo, cbm, cbo, cpw, cpb, cpg, n1g, sec_o, nrm_o, lo_o, hi_o,
    X, NT, NB, OH, G, W, CW, CB, CV, sems,
):
    g = sc[0]
    base = sc[1]
    cw_a, cw_b = turned(cpw, g)
    started = copies(
        sems,
        [
            (nbs, NT), (pts, X.at[256:2304]), (low, X.at[0:256]), (high, X.at[2304:2560]),
            (wm, W.at[:, 0:128]), (wo, W.at[:, 128:256]), (cw_a, CW.at[0:128]),
            (cw_b, CW.at[128:256]), (cbm, CB.at[:, 0:128]), (cbo, CB.at[:, 128:256]),
            (cpb, CV.at[0]), (cpg, CV.at[1]), (n1g, CV.at[2]),
        ],
    )
    wait(started[:4])
    lanes = lax.broadcasted_iota(jnp.int32, (RB, 768), 1)
    for b in range(8):
        NB[256 * b : 256 * b + 256, :] = jnp.transpose(NT[:, 256 * b : 256 * b + 256])

    def block(b, _):
        rel = []
        for j in range(RB // 32):
            rel.append(NB[pl.ds(pl.multiple_of(256 * b + 64 * j + 32 * g, 32), 32), :])
        rel = jnp.concatenate(rel, axis=0)
        rel = jnp.where(rel < 0, -1, rel - (base + 256 * b - 256))
        for t in range(27):
            col = rel[:, t : t + 1]
            OH[t * RB : (t + 1) * RB, :] = jnp.where(
                lanes == col, jnp.array(1, BF), jnp.array(0, BF)
            )
        win = X[pl.ds(pl.multiple_of(256 * b, 256), 768), :]
        for q in range(3):
            out = jnp.dot(
                OH[q * 9 * RB : (q + 1) * 9 * RB, :], win, preferred_element_type=F32
            ).astype(BF)
            for t in range(9):
                G[
                    pl.ds(pl.multiple_of(b * RB, RB), RB),
                    (q * 9 + t) * 256 : (q * 9 + t + 1) * 256,
                ] = out[t * RB : (t + 1) * RB, :]
        return 0

    lax.fori_loop(0, 1024 // RB, block, 0)
    wait(started[4:])

    def finish(m, _):
        r0 = pl.multiple_of(m * 256, 256)
        acc = jnp.dot(G[pl.ds(r0, 256), :], W[...], preferred_element_type=F32)
        conv = (acc + CB[...]).astype(BF)
        c = jnp.dot(conv, CW[...], preferred_element_type=F32) + CV[0]
        own = []
        for j in range(8):
            own.append(X[pl.ds(pl.multiple_of(256 + 512 * m + 64 * j + 32 * g, 32), 32), :])
        own = jnp.concatenate(own, axis=0).astype(F32)
        sec = (own + layer_norm(c, CV[1])).astype(BF)
        sec_o[pl.ds(r0, 256), :] = sec
        normed = layer_norm(sec.astype(F32), CV[2]).astype(BF)
        nrm_o[pl.ds(r0, 256), :] = normed

        @pl.when(m < 2)
        def _():
            hi_o[pl.ds(r0, 256), :] = normed

        @pl.when(m >= 2)
        def _():
            lo_o[pl.ds(r0 - 512, 256), :] = normed

        return 0

    lax.fori_loop(0, 4, finish, 0)


def call(kernel, name, smem, args, out_shape, scratch, sems, flops, moved=8 * 10**6):
    return pl.pallas_call(
        kernel,
        out_shape=out_shape,
        in_specs=[pl.BlockSpec(memory_space=pltpu.SMEM)] * smem
        + [pl.BlockSpec(memory_space=pltpu.HBM)] * (len(args) - smem),
        out_specs=[pl.BlockSpec(memory_space=pltpu.VMEM)] * len(out_shape),
        scratch_shapes=[pltpu.VMEM(*x) for x in scratch] + [pltpu.SemaphoreType.DMA((sems,))],
        compiler_params=pltpu.CompilerParams(vmem_limit_bytes=VMEM_BYTES),
        cost_estimate=pl.CostEstimate(flops=flops, bytes_accessed=moved, transcendentals=0),
        name=name,
    )(*args)


def conv_call(*args):
    out = [jax.ShapeDtypeStruct((n, 256), BF) for n in (1024, 1024, 512, 512)]
    scratch = [
        ((2560, 256), BF), ((27, 2048), jnp.int32), ((2048, 27), jnp.int32), ((27 * RB, 768), BF), ((1024, 6912), BF),
        ((6912, 256), BF), ((256, 256), BF), ((1, 256), F32), ((3, 1, 256), F32),
    ]
    return call(conv_kernel, "conv", 1, args, out, scratch, 13, 30 * 10**9)


def key_values(NE, KT, V, QW, QB):
    wkt = [jnp.transpose(QW[h, 1]) for h in range(2)]
    bkc = [jnp.transpose(jnp.broadcast_to(QB[h, 1:2, :], (8, 128)))[:, :1] for h in range(2)]
    wv = jnp.concatenate([QW[0, 2], QW[1, 2]], axis=1)
    bv = jnp.concatenate([QB[0, 2:3, :], QB[1, 2:3, :]], axis=1)

    def block(i, most):
        r0 = pl.multiple_of(i * 256, 256)
        rows = NE[pl.ds(4 * i, 4)].reshape(256, 256)
        for h in range(2):
            kt = (
                lax.dot_general(
                    wkt[h], rows, (((1,), (1,)), ((), ())), preferred_element_type=F32
                )
                + bkc[h]
            )
            most = jnp.maximum(most, jnp.sum((kt * kt).reshape(8, 16, 256), axis=1))
            KT[128 * h : 128 * h + 128, pl.ds(r0, 256)] = kt.astype(BF)
        V[pl.ds(r0, 256), :] = (jnp.dot(rows, wv, preferred_element_type=F32) + bv).astype(BF)
        return most

    return block


def patch_rows(plen):
    lens = jnp.broadcast_to(plen.astype(F32), (256, 256))
    sub = lax.broadcasted_iota(jnp.int32, (256, 256), 0)
    lane = lax.broadcasted_iota(jnp.int32, (256, 256), 1)
    ends_col = jnp.sum(jnp.where(lane <= sub, lens, 0.0), axis=1, keepdims=True)
    ends_row = jnp.sum(jnp.where(lane == sub, ends_col, 0.0), axis=0, keepdims=True)
    return ends_row - plen.astype(F32), ends_row


def limits(qb, g, base, total, starts_row, ends_row):
    r = lax.broadcasted_iota(jnp.int32, (256, 1), 0)
    row = (base + 512 * qb + 64 * (r // 32) + 32 * g + r % 32).astype(F32)
    first = jnp.max(jnp.where(starts_row <= row, starts_row, 0.0), axis=1, keepdims=True)
    finish = jnp.min(jnp.where(ends_row > row, ends_row, total.astype(F32)), axis=1, keepdims=True)
    shift = (1024 - base).astype(F32)
    first = (first + shift).astype(jnp.int32)
    finish = (finish + shift).astype(jnp.int32)
    kb0 = jnp.maximum(jnp.min(first) // 128, 0)
    kb1 = jnp.minimum((jnp.max(finish) + 127) // 128, 32)
    return first, finish, kb0, kb1


def queries(rows, QW, QB):
    wq = jnp.concatenate([QW[0, 0], QW[1, 0]], axis=1)
    bq = jnp.concatenate([QB[0, 0:1, :], QB[1, 0:1, :]], axis=1)
    return ((jnp.dot(rows, wq, preferred_element_type=F32) + bq) * Q_SCALE).astype(BF)


def pair_tools():
    half = lax.broadcasted_iota(jnp.int32, (32, 128), 0) < 16
    k_low = jnp.where(half, 1.0, 0.0).astype(BF)
    k_high = jnp.where(half, 0.0, 1.0).astype(BF)
    col_head = lax.broadcasted_iota(jnp.int32, (128, 128), 1) // 16
    cols = [jnp.where(col_head == a, 1.0, 0.0).astype(BF) for a in range(8)]

    def mask(kb, first, finish):
        key = kb * 128 + lax.broadcasted_iota(jnp.int32, (256, 128), 1)
        madd = jnp.where((key >= first) & (key < finish), 0.0, -jnp.inf)
        return jnp.concatenate([madd, madd], axis=1)

    def scores(Q8, p, kt, madd):
        part = kt[32 * p : 32 * p + 32, :]
        pair = jnp.concatenate([part * k_low, part * k_high], axis=1)
        return jnp.dot(Q8[p], pair, preferred_element_type=F32) + madd

    def step(kb, k0, Q8, KT, V, first, finish, M=None):
        kt = KT[:, pl.ds(k0, 128)]
        vb = V[pl.ds(k0, 128), :]
        madd = mask(kb, first, finish)
        out = []
        for h in range(2):
            vh = vb[:, 128 * h : 128 * h + 128]
            ps, vs = [], []
            for a in range(4):
                p = 4 * h + a
                s = scores(Q8, p, kt, madd)
                if M is not None:
                    s = s - M[p]
                ps.append(jnp.exp2(s).astype(BF))
                for c in (cols[2 * a], cols[2 * a + 1]):
                    vs.append(jnp.concatenate([vh * c, c], axis=1))
            out.append(
                jnp.dot(
                    jnp.concatenate(ps, axis=1),
                    jnp.concatenate(vs, axis=0),
                    preferred_element_type=F32,
                )
            )
        return out

    return mask, scores, step


def near_kernel(
    sc, plen, own, oth, qkvm, qkvo, qbm, qbo, acc_o, q_o, most_o, NE, KT, V, Q8, QW, QB, PL, sems,
):
    g, base, total = sc[0], sc[1], sc[2]
    wait(
        copies(
            sems,
            [
                (own, NE.at[:, g]), (oth, NE.at[:, 1 - g]), (qkvm, QW.at[0]), (qkvo, QW.at[1]),
                (qbm, QB.at[0]), (qbo, QB.at[1]), (plen, PL),
            ],
        )
    )
    block = key_values(NE, KT, V, QW, QB)
    most = lax.fori_loop(0, 8, block, jnp.zeros((8, 256), F32))
    most_o[...] = jnp.broadcast_to(jnp.max(most), (8, 128))
    starts_row, ends_row = patch_rows(PL[...])
    mask, scores, step = pair_tools()

    def q_block(qb, _):
        r0 = pl.multiple_of(qb * 256, 256)
        q = queries(NE[pl.ds(8 * qb, 8), g].reshape(256, 256), QW, QB)
        q_o[pl.ds(r0, 256), :] = q
        for p in range(8):
            Q8[p] = q[:, 32 * p : 32 * p + 32]
        first, finish, kb0, kb1 = limits(qb, g, base, total, starts_row, ends_row)
        acc_o[qb] = jnp.zeros((2, 256, 256), F32)

        def body(kb, _):
            k0 = pl.multiple_of((kb - 8) * 128, 128)
            for h, x in enumerate(step(kb, k0, Q8, KT, V, first, finish)):
                acc_o[qb, h] += x
            return 0

        lax.fori_loop(jnp.maximum(kb0, 8), jnp.minimum(kb1, 24), body, 0)
        return 0

    lax.fori_loop(0, 4, q_block, 0)


QKV_SCRATCH = [((2, 3, 256, 128), BF), ((2, 3, 128), F32), ((1, 256), jnp.int32)]


def near_call(*args):
    out = [
        jax.ShapeDtypeStruct((4, 2, 256, 256), F32),
        jax.ShapeDtypeStruct((1024, 256), BF),
        jax.ShapeDtypeStruct((8, 128), F32),
    ]
    scratch = [
        ((32, 2, 32, 256), BF), ((256, 2048), BF), ((2048, 256), BF), ((8, 256, 32), BF),
    ] + QKV_SCRATCH
    return call(near_kernel, "near", 1, args, out, scratch, 7, 0, 0)


def far_kernel(
    sc, sel, plen, own, oth, lo_own, lo_oth, hi_own, hi_oth, sec_i, acc_i, q_i, most_i, qkvm, qkvo,
    qbm, qbo, prw, prb, n2g, f1m, f1o, b1m, b1o, f2m, f2o, f2b, send, NE, KT, V, Q8, ACC, OUT, M,
    SEC, AI, QI, MI, PW, VEC, F1, B1, F2, QW, QB, PL, sems,
):
    g, base, total = sc[0], sc[1], sc[2]
    pw_a, pw_b = turned(prw, g)
    started = copies(
        sems,
        [
            (lo_own, NE.at[0:16, g]), (lo_oth, NE.at[0:16, 1 - g]), (hi_own, NE.at[48:64, g]),
            (hi_oth, NE.at[48:64, 1 - g]), (qkvm, QW.at[0]), (qkvo, QW.at[1]), (qbm, QB.at[0]),
            (qbo, QB.at[1]), (plen, PL), (most_i, MI), (q_i, QI), (acc_i, AI), (sec_i, SEC),
            (pw_a, PW.at[0:128]), (pw_b, PW.at[128:256]), (prb, VEC.at[0]), (n2g, VEC.at[1]),
            (f2b, VEC.at[2]), (f1m, F1.at[0]), (f1o, F1.at[1]), (b1m, B1.at[0]), (b1o, B1.at[1]),
            (f2m, F2.at[0]), (f2o, F2.at[1]),
        ],
    )
    wait(started[:11])
    block = key_values(NE, KT, V, QW, QB)
    starts_row, ends_row = patch_rows(PL[...])
    edge_lo = limits(0, g, base, total, starts_row, ends_row)[2]
    edge_hi = limits(3, g, base, total, starts_row, ends_row)[3]
    most = lax.fori_loop(jnp.minimum(edge_lo // 2, 4), 4, block, jnp.zeros((8, 256), F32))
    most = lax.fori_loop(12, jnp.maximum((edge_hi + 1) // 2, 12), block, most)
    key_most = jnp.maximum(jnp.max(most), jnp.max(MI[...]))
    mask, scores, step = pair_tools()
    hs = lax.broadcasted_iota(jnp.int32, (256, 128), 0) // 16
    hl = lax.broadcasted_iota(jnp.int32, (256, 128), 1)
    head_sel = jnp.where(hs == hl, 1.0, 0.0).astype(BF)
    def q_most(r0):
        q = QI[pl.ds(r0, 256), :]
        return jnp.max(jnp.dot(q * q, head_sel, preferred_element_type=F32))

    bound = q_most(0)
    for i in range(1, 4):
        bound = jnp.maximum(bound, q_most(256 * i))
    calm = bound * key_most * 1.05 <= 1e4

    @pl.when(jnp.logical_not(calm))
    def _():
        wait(copies(sems.at[24:26], [(own, NE.at[16:48, g]), (oth, NE.at[16:48, 1 - g])]))
        lax.fori_loop(4, 12, block, jnp.zeros((8, 256), F32))

    wait(started[11:])

    def q_block(qb, _):
        r0 = pl.multiple_of(qb * 256, 256)
        q = QI[pl.ds(r0, 256), :]
        for p in range(8):
            Q8[p] = q[:, 32 * p : 32 * p + 32]
        first, finish, kb0, kb1 = limits(qb, g, base, total, starts_row, ends_row)

        def body(kb, _, M=None):
            k0 = pl.multiple_of(kb * 128, 128)
            for h, x in enumerate(step(kb, k0, Q8, KT, V, first, finish, M)):
                ACC[h] += x
            return 0

        @pl.when(calm)
        def _():
            ACC[...] = AI[qb]
            lax.fori_loop(kb0, jnp.minimum(kb1, 8), body, 0)
            lax.fori_loop(jnp.maximum(kb0, 24), kb1, body, 0)

        @pl.when(jnp.logical_not(calm))
        def _():
            ACC[...] = jnp.zeros_like(ACC)
            M[...] = jnp.full(M.shape, -jnp.inf, F32)

            def top(kb, _):
                kt = KT[:, pl.ds(pl.multiple_of(kb * 128, 128), 128)]
                madd = mask(kb, first, finish)
                for p in range(8):
                    M[p] = jnp.maximum(M[p], scores(Q8, p, kt, madd))
                return 0

            lax.fori_loop(kb0, kb1, top, 0)
            for p in range(8):
                for h in range(2):
                    part = M[p, :, 128 * h : 128 * h + 128]
                    M[p, :, 128 * h : 128 * h + 128] = jnp.broadcast_to(
                        jnp.max(part, axis=1, keepdims=True), (256, 128)
                    )
            lax.fori_loop(kb0, kb1, lambda kb, c: body(kb, c, M), 0)

        attn = jnp.concatenate(
            [ACC[h, :, 0:128] / ACC[h, :, 128:256] for h in range(2)], axis=1
        ).astype(BF)
        two = (
            SEC[pl.ds(r0, 256), :].astype(F32)
            + jnp.dot(attn, PW[...], preferred_element_type=F32)
            + VEC[0]
        ).astype(BF)
        wide = two.astype(F32)
        normed = layer_norm(wide, VEC[1]).astype(BF)
        total_rows = wide + VEC[2]
        for h in range(2):
            x = jnp.dot(normed, F1[h], preferred_element_type=F32) + B1[h]
            x = (0.5 * x * (1.0 + lax.erf(x * 0.7071067811865476))).astype(BF)
            total_rows = total_rows + jnp.dot(x, F2[h], preferred_element_type=F32)
        OUT[pl.ds(r0, 256), :] = total_rows.astype(BF)
        return 0

    lax.fori_loop(0, 4, q_block, 0)

    def place(d, _):
        send[pl.ds(pl.multiple_of(32 * d, 32), 32), :] = OUT[
            pl.ds(pl.multiple_of(32 * sel[d], 32), 32), :
        ]
        return 0

    lax.fori_loop(0, 64, place, 0, unroll=4)


def far_call(*args):
    scratch = [
        ((64, 2, 32, 256), BF), ((256, 4096), BF), ((4096, 256), BF), ((8, 256, 32), BF),
        ((2, 256, 256), F32), ((1024, 256), BF), ((8, 256, 256), F32), ((1024, 256), BF),
        ((4, 2, 256, 256), F32), ((1024, 256), BF), ((8, 128), F32), ((256, 256), BF),
        ((3, 1, 256), F32), ((2, 256, 512), BF), ((2, 1, 512), F32), ((2, 512, 256), BF),
    ] + QKV_SCRATCH
    out = [jax.ShapeDtypeStruct((2048, 256), BF)]
    return call(far_kernel, "far", 2, args, out, scratch, 26, 20 * 10**9)[0]


def last_kernel(sc, zs, zv, own, oth, out):
    g = sc[0]
    place = zv[0:1, 0:64] % 64
    place = place % 32 + jnp.where(place // 32 == g, 0, 32)
    place = jnp.where(lax.broadcasted_iota(jnp.int32, (64, 64), 0) == place, 1.0, 0.0)
    perm = jnp.transpose(place).astype(BF)

    def step(k, _):
        source = lax.shift_right_logical(zs[64 * k], 11)
        rows = jnp.concatenate([own[source], oth[source]], axis=0)
        out[pl.ds(pl.multiple_of(64 * k, 64), 64), :] = jnp.dot(
            perm, rows, preferred_element_type=F32
        ).astype(BF)
        return 0

    lax.fori_loop(0, 32, step, 0, unroll=8)


def last_call(*args):
    smem, vmem = pl.BlockSpec(memory_space=pltpu.SMEM), pl.BlockSpec(memory_space=pltpu.VMEM)
    return pl.pallas_call(
        last_kernel,
        out_shape=jax.ShapeDtypeStruct((2048, 256), BF),
        in_specs=[smem] * 2 + [vmem] * 3,
        out_specs=vmem,
        compiler_params=pltpu.CompilerParams(vmem_limit_bytes=16 * 2**20),
        name="relabel",
    )(*args)


def local(
    points, neighbours, patch_len, zorder, conv_w, conv_b, cpe_w, cpe_b, cpe_gain, norm1_gain,
    qkv_w, qkv_b, proj_w, proj_b, norm2_gain, fc1_w, fc1_b, fc2_w, fc2_b,
):
    g = lax.axis_index("grp").astype(jnp.int32)
    me = lax.axis_index("pts").astype(jnp.int32)
    peers = lax.axis_size("pts")
    rows = points.shape[0]
    forward = [(i, i + 1) for i in range(peers - 1)]
    backward = [(i + 1, i) for i in range(peers - 1)]

    def swap(x):
        return lax.ppermute(x, "grp", [(0, 1), (1, 0)])

    def pieces(x):
        return x.reshape(-1, 32, 256)

    order = zorder.reshape(16, 128)
    run = zorder[::64] // 64
    table = lax.all_gather(
        jnp.broadcast_to(jnp.pad(run, (0, 96))[None], (32, 128)), "pts", axis=0, tiled=True
    )
    low = lax.ppermute(points[rows - 256 :], "pts", forward)
    high = lax.ppermute(points[:256], "pts", backward)
    conv_m = conv_w.reshape(27 * 256, 128)
    conv_o, bias_o = swap(conv_m), swap(conv_b)
    scalars = jnp.stack([g, me * rows, jnp.int32(rows * peers)])
    section_one, normed, lo_half, hi_half = conv_call(
        scalars, points, low, high, neighbours.T, conv_m, conv_o, conv_b[None], bias_o[None],
        cpe_w, cpe_b[None], cpe_gain[None], norm1_gain[None],
    )
    qkv_m = jnp.transpose(qkv_w, (1, 0, 2))
    weights = (qkv_m, swap(qkv_m), qkv_b, swap(qkv_b))
    fc1_o, fc2_o, b1_o = swap(fc1_w), swap(fc2_w), swap(fc1_b)
    other = swap(normed)
    lo_own = lax.ppermute(lo_half, "pts", forward)
    hi_own = lax.ppermute(hi_half, "pts", backward)
    acc, query, most = near_call(scalars, patch_len[None], pieces(normed), pieces(other), *weights)
    lo_own, hi_own, table, most = lax.optimization_barrier((lo_own, hi_own, table, most))
    lo_oth, hi_oth = swap(lo_own), swap(hi_own)
    table = table.reshape(64, 32, 128)[:, 0, :32]
    sel = jnp.max(jnp.where(table // 32 == me, table % 32, 0), axis=1)
    send = far_call(
        scalars, sel, patch_len[None], pieces(normed), pieces(other), pieces(lo_own),
        pieces(lo_oth), pieces(hi_own), pieces(hi_oth), section_one, acc, query, most, *weights,
        proj_w, proj_b[None], norm2_gain[None], fc1_w, fc1_o, fc1_b[None], b1_o[None], fc2_w,
        fc2_o, fc2_b[None],
    )
    got = lax.all_to_all(send, "pts", split_axis=0, concat_axis=0, tiled=True)
    return last_call(scalars, zorder, order, pieces(got), pieces(swap(got)))


def solution(mesh):
    placed = (
        P("pts", None), P("pts", None), P(), P("pts"), P(None, None, "grp"), P("grp"), P(), P(), P(),
        P(), P(None, None, "grp"), P(None, "grp"), P(), P(), P(), P(None, "grp"), P("grp"),
        P("grp", None), P(),
    )
    return jax.shard_map(
        local, mesh=mesh, in_specs=placed, out_specs=P("pts", None), check_vma=False
    )
```

```python
import jax
import jax.numpy as jnp
from jax import lax
from jax.experimental import pallas as pl
from jax.experimental.pallas import tpu as pltpu
from jax.sharding import PartitionSpec as P

F32=jnp.float32; BF=jnp.bfloat16

VMEM_BYTES = 64 * 2**20 - 65536
Q_SCALE = 0.25 * 1.4426950408889634


def layer_norm(v, gain):
    c = v - jnp.mean(v, axis=-1, keepdims=True)
    s = jnp.mean(c * c, axis=-1, keepdims=True)
    return c * lax.rsqrt(s + 1e-05) * gain

RB = 128
TAPS = [t for t in range(27) if t != 13]


def copies(sems, pairs):
    out = [pltpu.make_async_copy(src, dst, sems.at[i]) for i, (src, dst) in enumerate(pairs)]
    for copy in out:
        copy.start()
    return out


def wait(some):
    for copy in some:
        copy.wait()


def turned(ref, g):
    first = ref.at[pl.ds(pl.multiple_of(128 * g, 128), 128)]
    return first, ref.at[pl.ds(pl.multiple_of(128 - 128 * g, 128), 128)]


def conv_kernel(
    sc, pts, low, high, nbs, wm, wo, cbm, cbo, cpw, cpb, cpg, n1g, sec_o, nrm_o, lo_o, hi_o,
    X, NT, NB, OH, G, W, CW, CB, CV, sems,
):
    g = sc[0]
    base = sc[1]
    cw_a, cw_b = turned(cpw, g)
    started = copies(
        sems,
        [
            (nbs, NT), (pts, X.at[256:2304]), (low, X.at[0:256]), (high, X.at[2304:2560]),
            (wm, W.at[:, 0:128]), (wo, W.at[:, 128:256]), (cw_a, CW.at[0:128]),
            (cw_b, CW.at[128:256]), (cbm, CB.at[:, 0:128]), (cbo, CB.at[:, 128:256]),
            (cpb, CV.at[0]), (cpg, CV.at[1]), (n1g, CV.at[2]),
        ],
    )
    wait(started[:4])
    lanes = lax.broadcasted_iota(jnp.int32, (RB, 768), 1)
    for b in range(8):
        NB[256 * b : 256 * b + 256, :] = jnp.transpose(NT[:, 256 * b : 256 * b + 256])

    def block(b, _):
        rel = []
        for j in range(RB // 32):
            rel.append(NB[pl.ds(pl.multiple_of(256 * b + 64 * j + 32 * g, 32), 32), :])
        rel = jnp.concatenate(rel, axis=0)
        rel = jnp.where(rel < 0, -1, rel - (base + 256 * b - 256))
        for i, t in enumerate(TAPS):
            col = rel[:, t : t + 1]
            OH[i * RB : (i + 1) * RB, :] = jnp.where(
                lanes == col, jnp.array(1, BF), jnp.array(0, BF)
            )
        win = X[pl.ds(pl.multiple_of(256 * b, 256), 768), :]
        to = pl.ds(pl.multiple_of(b * RB, RB), RB)
        for q in range(2):
            out = jnp.dot(
                OH[q * 13 * RB : (q + 1) * 13 * RB, :], win, preferred_element_type=F32
            ).astype(BF)
            for i in range(13):
                t = TAPS[13 * q + i]
                G[to, t * 256 : (t + 1) * 256] = out[i * RB : (i + 1) * RB, :]
        for j in range(RB // 32):
            G[pl.ds(pl.multiple_of(b * RB + 32 * j, 32), 32), 13 * 256 : 14 * 256] = X[
                pl.ds(pl.multiple_of(256 + 256 * b + 64 * j + 32 * g, 32), 32), :
            ]
        return 0

    lax.fori_loop(0, 1024 // RB, block, 0)
    wait(started[4:])

    def finish(m, _):
        r0 = pl.multiple_of(m * 512, 512)
        at = pl.ds(r0, 512)
        acc = jnp.dot(G[at, :], W[...], preferred_element_type=F32)
        conv = (acc + CB[...]).astype(BF)
        c = jnp.dot(conv, CW[...], preferred_element_type=F32) + CV[0]
        own = G[at, 13 * 256 : 14 * 256].astype(F32)
        sec = (own + layer_norm(c, CV[1])).astype(BF)
        sec_o[at, :] = sec
        normed = layer_norm(sec.astype(F32), CV[2]).astype(BF)
        nrm_o[at, :] = normed

        @pl.when(m == 0)
        def _():
            hi_o[...] = normed

        @pl.when(m == 1)
        def _():
            lo_o[...] = normed

        return 0

    lax.fori_loop(0, 2, finish, 0)


def call(kernel, name, smem, args, out_shape, scratch, sems, flops, space=pltpu.VMEM):
    return pl.pallas_call(
        kernel,
        out_shape=out_shape,
        in_specs=[pl.BlockSpec(memory_space=pltpu.SMEM)] * smem
        + [pl.BlockSpec(memory_space=pltpu.HBM)] * (len(args) - smem),
        out_specs=[pl.BlockSpec(memory_space=space)] * len(out_shape),
        scratch_shapes=[pltpu.VMEM(*x) for x in scratch] + [pltpu.SemaphoreType.DMA((sems,))],
        compiler_params=pltpu.CompilerParams(vmem_limit_bytes=VMEM_BYTES),
        cost_estimate=pl.CostEstimate(flops=flops, bytes_accessed=8 * 10**6, transcendentals=0),
        name=name,
    )(*args)


def conv_call(*args):
    out = [jax.ShapeDtypeStruct((n, 256), BF) for n in (1024, 1024, 512, 512)]
    scratch = [
        ((2560, 256), BF), ((27, 2048), jnp.int32), ((2048, 27), jnp.int32), ((26 * RB, 768), BF), ((1024, 6912), BF),
        ((6912, 256), BF), ((256, 256), BF), ((1, 256), F32), ((3, 1, 256), F32),
    ]
    return call(conv_kernel, "conv", 1, args, out, scratch, 13, 30 * 10**9)


def key_values(NE, KT, V, QW, QB):
    wkt = [jnp.transpose(QW[h, 1]) for h in range(2)]
    bkc = [jnp.transpose(jnp.broadcast_to(QB[h, 1:2, :], (8, 128)))[:, :1] for h in range(2)]
    wv = jnp.concatenate([QW[0, 2], QW[1, 2]], axis=1)
    bv = jnp.concatenate([QB[0, 2:3, :], QB[1, 2:3, :]], axis=1)

    def block(i, most):
        r0 = pl.multiple_of(i * 256, 256)
        rows = NE[pl.ds(4 * i, 4)].reshape(256, 256)
        for h in range(2):
            kt = (
                lax.dot_general(
                    wkt[h], rows, (((1,), (1,)), ((), ())), preferred_element_type=F32
                )
                + bkc[h]
            )
            most = jnp.maximum(most, jnp.sum((kt * kt).reshape(8, 16, 256), axis=1))
            KT[128 * h : 128 * h + 128, pl.ds(r0, 256)] = kt.astype(BF)
        V[pl.ds(r0, 256), :] = (jnp.dot(rows, wv, preferred_element_type=F32) + bv).astype(BF)
        return most

    return block


def patch_rows(plen):
    lens = jnp.broadcast_to(plen.astype(F32), (256, 256))
    sub = lax.broadcasted_iota(jnp.int32, (256, 256), 0)
    lane = lax.broadcasted_iota(jnp.int32, (256, 256), 1)
    ends_col = jnp.sum(jnp.where(lane <= sub, lens, 0.0), axis=1, keepdims=True)
    ends_row = jnp.sum(jnp.where(lane == sub, ends_col, 0.0), axis=0, keepdims=True)
    return ends_row - plen.astype(F32), ends_row


def limits(qb, g, base, total, starts_row, ends_row):
    r = lax.broadcasted_iota(jnp.int32, (256, 1), 0)
    row = (base + 512 * qb + 64 * (r // 32) + 32 * g + r % 32).astype(F32)
    first = jnp.max(jnp.where(starts_row <= row, starts_row, 0.0), axis=1, keepdims=True)
    finish = jnp.min(jnp.where(ends_row > row, ends_row, total.astype(F32)), axis=1, keepdims=True)
    shift = (1024 - base).astype(F32)
    first = (first + shift).astype(jnp.int32)
    finish = (finish + shift).astype(jnp.int32)
    kb0 = jnp.maximum(jnp.min(first) // 128, 0)
    kb1 = jnp.minimum((jnp.max(finish) + 127) // 128, 32)
    return first, finish, kb0, kb1


def queries(rows, QW, QB):
    wq = jnp.concatenate([QW[0, 0], QW[1, 0]], axis=1)
    bq = jnp.concatenate([QB[0, 0:1, :], QB[1, 0:1, :]], axis=1)
    return ((jnp.dot(rows, wq, preferred_element_type=F32) + bq) * Q_SCALE).astype(BF)


def pair_tools():
    half = lax.broadcasted_iota(jnp.int32, (32, 128), 0) < 16
    k_low = jnp.where(half, 1.0, 0.0).astype(BF)
    k_high = jnp.where(half, 0.0, 1.0).astype(BF)
    col_head = lax.broadcasted_iota(jnp.int32, (128, 128), 1) // 16
    cols = [jnp.where(col_head == a, 1.0, 0.0).astype(BF) for a in range(8)]

    def mask(kb, first, finish):
        key = kb * 128 + lax.broadcasted_iota(jnp.int32, (256, 128), 1)
        madd = jnp.where((key >= first) & (key < finish), 0.0, -jnp.inf)
        return jnp.concatenate([madd, madd], axis=1)

    def scores(Q8, p, kt, madd):
        part = kt[32 * p : 32 * p + 32, :]
        pair = jnp.concatenate([part * k_low, part * k_high], axis=1)
        return jnp.dot(Q8[p], pair, preferred_element_type=F32) + madd

    def step(kb, k0, Q8, KT, V, first, finish, M=None):
        kt = KT[:, pl.ds(k0, 128)]
        vb = V[pl.ds(k0, 128), :]
        madd = mask(kb, first, finish)
        out = []
        for h in range(2):
            vh = vb[:, 128 * h : 128 * h + 128]
            ps, vs = [], []
            for a in range(4):
                p = 4 * h + a
                s = scores(Q8, p, kt, madd)
                if M is not None:
                    s = s - M[p]
                ps.append(jnp.exp2(s).astype(BF))
                for c in (cols[2 * a], cols[2 * a + 1]):
                    vs.append(jnp.concatenate([vh * c, c], axis=1))
            out.append(
                jnp.dot(
                    jnp.concatenate(ps, axis=1),
                    jnp.concatenate(vs, axis=0),
                    preferred_element_type=F32,
                )
            )
        return out

    return mask, scores, step


def near_kernel(
    sc, plen, own, oth, qkvm, qkvo, qbm, qbo, acc_h, q_h, most_h, NE, KT, V, Q8, acc_o, q_o,
    most_o, QW, QB, PL, sems,
):
    g, base, total = sc[0], sc[1], sc[2]
    wait(
        copies(
            sems,
            [
                (own, NE.at[:, g]), (oth, NE.at[:, 1 - g]), (qkvm, QW.at[0]), (qkvo, QW.at[1]),
                (qbm, QB.at[0]), (qbo, QB.at[1]), (plen, PL),
            ],
        )
    )
    block = key_values(NE, KT, V, QW, QB)
    most = lax.fori_loop(0, 8, block, jnp.zeros((8, 256), F32))
    most_o[...] = jnp.broadcast_to(jnp.max(most), (8, 128))
    leave = pltpu.make_async_copy(most_o, most_h, sems.at[7])
    leave.start()

    def results(qb):
        at = pl.ds(pl.multiple_of(256 * qb, 256), 256)
        return (
            pltpu.make_async_copy(acc_o.at[qb], acc_h.at[qb], sems.at[8 + qb]),
            pltpu.make_async_copy(q_o.at[at], q_h.at[at], sems.at[12 + qb]),
        )

    starts_row, ends_row = patch_rows(PL[...])
    mask, scores, step = pair_tools()

    def q_block(qb, _):
        r0 = pl.multiple_of(qb * 256, 256)
        q = queries(NE[pl.ds(8 * qb, 8), g].reshape(256, 256), QW, QB)
        q_o[pl.ds(r0, 256), :] = q
        for p in range(8):
            Q8[p] = q[:, 32 * p : 32 * p + 32]
        first, finish, kb0, kb1 = limits(qb, g, base, total, starts_row, ends_row)
        acc_o[qb] = jnp.zeros((2, 256, 256), F32)

        def body(kb, _):
            k0 = pl.multiple_of((kb - 8) * 128, 128)
            for h, x in enumerate(step(kb, k0, Q8, KT, V, first, finish)):
                acc_o[qb, h] += x
            return 0

        lax.fori_loop(jnp.maximum(kb0, 8), jnp.minimum(kb1, 24), body, 0)
        for copy in results(qb):
            copy.start()
        return 0

    lax.fori_loop(0, 4, q_block, 0)
    leave.wait()
    for qb in range(4):
        wait(results(qb))


QKV_SCRATCH = [((2, 3, 256, 128), BF), ((2, 3, 128), F32), ((1, 256), jnp.int32)]


def near_call(*args):
    out = [
        jax.ShapeDtypeStruct((4, 2, 256, 256), F32),
        jax.ShapeDtypeStruct((1024, 256), BF),
        jax.ShapeDtypeStruct((8, 128), F32),
    ]
    scratch = [
        ((32, 2, 32, 256), BF), ((256, 2048), BF), ((2048, 256), BF), ((8, 256, 32), BF),
        ((4, 2, 256, 256), F32), ((1024, 256), BF), ((8, 128), F32),
    ] + QKV_SCRATCH
    return call(near_kernel, "near", 1, args, out, scratch, 16, 20 * 10**9, space=pltpu.HBM)


def far_kernel(
    sc, sel, plen, own, oth, lo_own, lo_oth, hi_own, hi_oth, sec_i, acc_i, q_i, most_i, qkvm, qkvo,
    qbm, qbo, prw, prb, n2g, f1m, f1o, b1m, b1o, f2m, f2o, f2b, send, NE, KT, V, Q8, ACC, OUT, M,
    SEC, AI, QI, MI, PW, VEC, F1, B1, F2, QW, QB, PL, sems,
):
    g, base, total = sc[0], sc[1], sc[2]
    pw_a, pw_b = turned(prw, g)
    started = copies(
        sems,
        [
            (lo_own, NE.at[0:16, g]), (lo_oth, NE.at[0:16, 1 - g]), (hi_own, NE.at[48:64, g]),
            (hi_oth, NE.at[48:64, 1 - g]), (qkvm, QW.at[0]), (qkvo, QW.at[1]), (qbm, QB.at[0]),
            (qbo, QB.at[1]), (plen, PL), (most_i, MI), (q_i, QI), (acc_i, AI), (sec_i, SEC),
            (pw_a, PW.at[0:128]), (pw_b, PW.at[128:256]), (prb, VEC.at[0]), (n2g, VEC.at[1]),
            (f2b, VEC.at[2]), (f1m, F1.at[0]), (f1o, F1.at[1]), (b1m, B1.at[0]), (b1o, B1.at[1]),
            (f2m, F2.at[0]), (f2o, F2.at[1]),
        ],
    )
    wait(started[:11])
    block = key_values(NE, KT, V, QW, QB)
    starts_row, ends_row = patch_rows(PL[...])
    edge_lo = limits(0, g, base, total, starts_row, ends_row)[2]
    edge_hi = limits(3, g, base, total, starts_row, ends_row)[3]
    most = lax.fori_loop(jnp.minimum(edge_lo // 2, 4), 4, block, jnp.zeros((8, 256), F32))
    most = lax.fori_loop(12, jnp.maximum((edge_hi + 1) // 2, 12), block, most)
    key_most = jnp.maximum(jnp.max(most), jnp.max(MI[...]))
    mask, scores, step = pair_tools()
    hs = lax.broadcasted_iota(jnp.int32, (256, 128), 0) // 16
    hl = lax.broadcasted_iota(jnp.int32, (256, 128), 1)
    head_sel = jnp.where(hs == hl, 1.0, 0.0).astype(BF)
    def q_most(r0):
        q = QI[pl.ds(r0, 256), :]
        return jnp.max(jnp.dot(q * q, head_sel, preferred_element_type=F32))

    bound = q_most(0)
    for i in range(1, 4):
        bound = jnp.maximum(bound, q_most(256 * i))
    calm = bound * key_most * 1.05 <= 1e4

    @pl.when(jnp.logical_not(calm))
    def _():
        wait(copies(sems.at[24:26], [(own, NE.at[16:48, g]), (oth, NE.at[16:48, 1 - g])]))
        lax.fori_loop(4, 12, block, jnp.zeros((8, 256), F32))

    wait(started[11:])

    def q_block(qb, _):
        r0 = pl.multiple_of(qb * 256, 256)
        q = QI[pl.ds(r0, 256), :]
        for p in range(8):
            Q8[p] = q[:, 32 * p : 32 * p + 32]
        first, finish, kb0, kb1 = limits(qb, g, base, total, starts_row, ends_row)

        def body(kb, _, M=None):
            k0 = pl.multiple_of(kb * 128, 128)
            for h, x in enumerate(step(kb, k0, Q8, KT, V, first, finish, M)):
                ACC[h] += x
            return 0

        @pl.when(calm)
        def _():
            ACC[...] = AI[qb]
            lax.fori_loop(kb0, jnp.minimum(kb1, 8), body, 0)
            lax.fori_loop(jnp.maximum(kb0, 24), kb1, body, 0)

        @pl.when(jnp.logical_not(calm))
        def _():
            ACC[...] = jnp.zeros_like(ACC)
            M[...] = jnp.full(M.shape, -jnp.inf, F32)

            def top(kb, _):
                kt = KT[:, pl.ds(pl.multiple_of(kb * 128, 128), 128)]
                madd = mask(kb, first, finish)
                for p in range(8):
                    M[p] = jnp.maximum(M[p], scores(Q8, p, kt, madd))
                return 0

            lax.fori_loop(kb0, kb1, top, 0)
            for p in range(8):
                for h in range(2):
                    part = M[p, :, 128 * h : 128 * h + 128]
                    M[p, :, 128 * h : 128 * h + 128] = jnp.broadcast_to(
                        jnp.max(part, axis=1, keepdims=True), (256, 128)
                    )
            lax.fori_loop(kb0, kb1, lambda kb, c: body(kb, c, M), 0)

        attn = jnp.concatenate(
            [ACC[h, :, 0:128] / ACC[h, :, 128:256] for h in range(2)], axis=1
        ).astype(BF)
        two = (
            SEC[pl.ds(r0, 256), :].astype(F32)
            + jnp.dot(attn, PW[...], preferred_element_type=F32)
            + VEC[0]
        ).astype(BF)
        wide = two.astype(F32)
        normed = layer_norm(wide, VEC[1]).astype(BF)
        total_rows = wide + VEC[2]
        for h in range(2):
            x = jnp.dot(normed, F1[h], preferred_element_type=F32) + B1[h]
            x = (0.5 * x * (1.0 + lax.erf(x * 0.7071067811865476))).astype(BF)
            total_rows = total_rows + jnp.dot(x, F2[h], preferred_element_type=F32)
        OUT[pl.ds(r0, 256), :] = total_rows.astype(BF)
        return 0

    lax.fori_loop(0, 4, q_block, 0)

    def place(d, _):
        send[pl.ds(pl.multiple_of(32 * d, 32), 32), :] = OUT[
            pl.ds(pl.multiple_of(32 * sel[d], 32), 32), :
        ]
        return 0

    lax.fori_loop(0, 64, place, 0, unroll=4)


def far_call(*args):
    scratch = [
        ((64, 2, 32, 256), BF), ((256, 4096), BF), ((4096, 256), BF), ((8, 256, 32), BF),
        ((2, 256, 256), F32), ((1024, 256), BF), ((8, 256, 256), F32), ((1024, 256), BF),
        ((4, 2, 256, 256), F32), ((1024, 256), BF), ((8, 128), F32), ((256, 256), BF),
        ((3, 1, 256), F32), ((2, 256, 512), BF), ((2, 1, 512), F32), ((2, 512, 256), BF),
    ] + QKV_SCRATCH
    out = [jax.ShapeDtypeStruct((2048, 256), BF)]
    return call(far_kernel, "far", 2, args, out, scratch, 26, 20 * 10**9)[0]


def last_kernel(sc, zs, zv, own, oth, out):
    g = sc[0]
    place = zv[0:1, 0:64] % 64
    place = place % 32 + jnp.where(place // 32 == g, 0, 32)
    place = jnp.where(lax.broadcasted_iota(jnp.int32, (64, 64), 0) == place, 1.0, 0.0)
    perm = jnp.transpose(place).astype(BF)

    def step(k, _):
        source = lax.shift_right_logical(zs[64 * k], 11)
        rows = jnp.concatenate([own[source], oth[source]], axis=0)
        out[pl.ds(pl.multiple_of(64 * k, 64), 64), :] = jnp.dot(
            perm, rows, preferred_element_type=F32
        ).astype(BF)
        return 0

    lax.fori_loop(0, 32, step, 0, unroll=8)


def last_call(*args):
    smem, vmem = pl.BlockSpec(memory_space=pltpu.SMEM), pl.BlockSpec(memory_space=pltpu.VMEM)
    return pl.pallas_call(
        last_kernel,
        out_shape=jax.ShapeDtypeStruct((2048, 256), BF),
        in_specs=[smem] * 2 + [vmem] * 3,
        out_specs=vmem,
        compiler_params=pltpu.CompilerParams(vmem_limit_bytes=16 * 2**20),
        name="relabel",
    )(*args)


def local(
    points, neighbours, patch_len, zorder, conv_w, conv_b, cpe_w, cpe_b, cpe_gain, norm1_gain,
    qkv_w, qkv_b, proj_w, proj_b, norm2_gain, fc1_w, fc1_b, fc2_w, fc2_b,
):
    g = lax.axis_index("grp").astype(jnp.int32)
    me = lax.axis_index("pts").astype(jnp.int32)
    peers = lax.axis_size("pts")
    rows = points.shape[0]
    forward = [(i, i + 1) for i in range(peers - 1)]
    backward = [(i + 1, i) for i in range(peers - 1)]

    def swap(x):
        return lax.ppermute(x, "grp", [(0, 1), (1, 0)])

    def pieces(x):
        return x.reshape(-1, 32, 256)

    order = zorder.reshape(16, 128)
    low = lax.ppermute(points[rows - 256 :], "pts", forward)
    high = lax.ppermute(points[:256], "pts", backward)
    conv_m = conv_w.reshape(27 * 256, 128)
    conv_o, bias_o = swap(conv_m), swap(conv_b)
    scalars = jnp.stack([g, me * rows, jnp.int32(rows * peers)])
    section_one, normed, lo_half, hi_half = conv_call(
        scalars, points, low, high, neighbours.T, conv_m, conv_o, conv_b[None], bias_o[None],
        cpe_w, cpe_b[None], cpe_gain[None], norm1_gain[None],
    )
    qkv_m = jnp.transpose(qkv_w, (1, 0, 2))
    weights = (qkv_m, swap(qkv_m), qkv_b, swap(qkv_b))
    fc1_o, fc2_o, b1_o = swap(fc1_w), swap(fc2_w), swap(fc1_b)
    other = swap(normed)
    sources = jnp.arange(peers, dtype=jnp.int32)[:, None]
    run = zorder[::64][None, :]
    wanted = jnp.max(jnp.where(run // rows == sources, run % rows // 64, 0), axis=1)
    wanted = jnp.broadcast_to(wanted[:, None, None], (peers, 1, 128))
    wanted, other = lax.optimization_barrier((wanted, other))
    sel = lax.all_to_all(wanted, "pts", split_axis=0, concat_axis=0, tiled=True)[:, 0, 0]
    lo_own = lax.ppermute(lo_half, "pts", forward)
    hi_own = lax.ppermute(hi_half, "pts", backward)
    acc, query, most = near_call(scalars, patch_len[None], pieces(normed), pieces(other), *weights)
    lo_own, hi_own, sel, most = lax.optimization_barrier((lo_own, hi_own, sel, most))
    lo_oth, hi_oth = swap(lo_own), swap(hi_own)
    send = far_call(
        scalars, sel, patch_len[None], pieces(normed), pieces(other), pieces(lo_own),
        pieces(lo_oth), pieces(hi_own), pieces(hi_oth), section_one, acc, query, most, *weights,
        proj_w, proj_b[None], norm2_gain[None], fc1_w, fc1_o, fc1_b[None], b1_o[None], fc2_w,
        fc2_o, fc2_b[None],
    )
    got = lax.all_to_all(send, "pts", split_axis=0, concat_axis=0, tiled=True)
    return last_call(scalars, zorder, order, pieces(got), pieces(swap(got)))


def solution(mesh):
    placed = (
        P("pts", None), P("pts", None), P(), P("pts"), P(None, None, "grp"), P("grp"), P(), P(), P(),
        P(), P(None, None, "grp"), P(None, "grp"), P(), P(), P(), P(None, "grp"), P("grp"),
        P("grp", None), P(),
    )
    return jax.shard_map(
        local, mesh=mesh, in_specs=placed, out_specs=P("pts", None), check_vma=False
    )
```

```python
import jax
import jax.numpy as jnp
from jax import lax
from jax.experimental import pallas as pl
from jax.experimental.pallas import tpu as pltpu
from jax.sharding import PartitionSpec as P

F32=jnp.float32; BF=jnp.bfloat16

VMEM_BYTES = 64 * 2**20 - 65536
Q_SCALE = 0.25 * 1.4426950408889634


def layer_norm(v, gain):
    c = v - jnp.mean(v, axis=-1, keepdims=True)
    s = jnp.mean(c * c, axis=-1, keepdims=True)
    return c * lax.rsqrt(s + 1e-05) * gain

RB = 128
TAPS = [t for t in range(27) if t != 13]


def copies(sems, pairs):
    out = [pltpu.make_async_copy(src, dst, sems.at[i]) for i, (src, dst) in enumerate(pairs)]
    for copy in out:
        copy.start()
    return out


def wait(some):
    for copy in some:
        copy.wait()


def turned(ref, g):
    first = ref.at[pl.ds(pl.multiple_of(128 * g, 128), 128)]
    return first, ref.at[pl.ds(pl.multiple_of(128 - 128 * g, 128), 128)]


def conv_kernel(
    sc, pts, low, high, nbs, wm, wo, cbm, cbo, cpw, cpb, cpg, n1g, sec_o, nrm_o, lo_o, hi_o,
    X, NT, NB, OH, G, W, CW, CB, CV, sems,
):
    g = sc[0]
    base = sc[1]
    cw_a, cw_b = turned(cpw, g)
    started = copies(
        sems,
        [
            (nbs, NT), (pts, X.at[256:2304]), (low, X.at[0:256]), (high, X.at[2304:2560]),
            (wm, W.at[:, 0:128]), (wo, W.at[:, 128:256]), (cw_a, CW.at[0:128]),
            (cw_b, CW.at[128:256]), (cbm, CB.at[:, 0:128]), (cbo, CB.at[:, 128:256]),
            (cpb, CV.at[0]), (cpg, CV.at[1]), (n1g, CV.at[2]),
        ],
    )
    wait(started[:4])
    lanes = lax.broadcasted_iota(jnp.int32, (RB, 768), 1)
    for b in range(8):
        NB[256 * b : 256 * b + 256, :] = jnp.transpose(NT[:, 256 * b : 256 * b + 256])

    def block(b, OH):
        rel = []
        for j in range(RB // 32):
            rel.append(NB[pl.ds(pl.multiple_of(256 * b + 64 * j + 32 * g, 32), 32), :])
        rel = jnp.concatenate(rel, axis=0)
        rel = jnp.where(rel < 0, -1, rel - (base + 256 * b - 256))
        for i, t in enumerate(TAPS):
            col = rel[:, t : t + 1]
            OH[i * RB : (i + 1) * RB, :] = jnp.where(
                lanes == col, jnp.array(1, BF), jnp.array(0, BF)
            )
        win = X[pl.ds(256 * b, 768), :]
        to = pl.ds(b * RB, RB)
        out = jnp.dot(OH[...], win, preferred_element_type=F32).astype(BF)
        for i, t in enumerate(TAPS):
            G[to, t * 256 : (t + 1) * 256] = out[i * RB : (i + 1) * RB, :]
        for j in range(RB // 32):
            G[pl.ds(b * RB + 32 * j, 32), 13 * 256 : 14 * 256] = X[
                pl.ds(pl.multiple_of(256 + 256 * b + 64 * j + 32 * g, 32), 32), :
            ]

    for b in range(1024 // RB):
        block(b, OH.at[b % 2])
    wait(started[4:])

    def finish(m, _):
        r0 = pl.multiple_of(m * 512, 512)
        at = pl.ds(r0, 512)
        acc = jnp.dot(G[at, :], W[...], preferred_element_type=F32)
        conv = (acc + CB[...]).astype(BF)
        c = jnp.dot(conv, CW[...], preferred_element_type=F32) + CV[0]
        own = G[at, 13 * 256 : 14 * 256].astype(F32)
        sec = (own + layer_norm(c, CV[1])).astype(BF)
        sec_o[at, :] = sec
        normed = layer_norm(sec.astype(F32), CV[2]).astype(BF)
        nrm_o[at, :] = normed

        @pl.when(m == 0)
        def _():
            hi_o[...] = normed

        @pl.when(m == 1)
        def _():
            lo_o[...] = normed

        return 0

    lax.fori_loop(0, 2, finish, 0)


def call(kernel, name, smem, args, out_shape, scratch, sems, flops, space=pltpu.VMEM):
    return pl.pallas_call(
        kernel,
        out_shape=out_shape,
        in_specs=[pl.BlockSpec(memory_space=pltpu.SMEM)] * smem
        + [pl.BlockSpec(memory_space=pltpu.HBM)] * (len(args) - smem),
        out_specs=[pl.BlockSpec(memory_space=space)] * len(out_shape),
        scratch_shapes=[pltpu.VMEM(*x) for x in scratch] + [pltpu.SemaphoreType.DMA((sems,))],
        compiler_params=pltpu.CompilerParams(vmem_limit_bytes=VMEM_BYTES),
        cost_estimate=pl.CostEstimate(flops=flops, bytes_accessed=8 * 10**6, transcendentals=0),
        name=name,
    )(*args)


def conv_call(*args):
    out = [jax.ShapeDtypeStruct((n, 256), BF) for n in (1024, 1024, 512, 512)]
    scratch = [
        ((2560, 256), BF), ((27, 2048), jnp.int32), ((2048, 27), jnp.int32), ((2, 26 * RB, 768), BF), ((1024, 6912), BF),
        ((6912, 256), BF), ((256, 256), BF), ((1, 256), F32), ((3, 1, 256), F32),
    ]
    return call(conv_kernel, "conv", 1, args, out, scratch, 13, 30 * 10**9)


def key_values(NE, KT, V, QW, QB):
    wkt = [jnp.transpose(QW[h, 1]) for h in range(2)]
    bkc = [jnp.transpose(jnp.broadcast_to(QB[h, 1:2, :], (8, 128)))[:, :1] for h in range(2)]
    wv = jnp.concatenate([QW[0, 2], QW[1, 2]], axis=1)
    bv = jnp.concatenate([QB[0, 2:3, :], QB[1, 2:3, :]], axis=1)

    def block(i, most):
        r0 = pl.multiple_of(i * 256, 256)
        rows = NE[pl.ds(4 * i, 4)].reshape(256, 256)
        for h in range(2):
            kt = (
                lax.dot_general(
                    wkt[h], rows, (((1,), (1,)), ((), ())), preferred_element_type=F32
                )
                + bkc[h]
            )
            most = jnp.maximum(most, jnp.sum((kt * kt).reshape(8, 16, 256), axis=1))
            KT[128 * h : 128 * h + 128, pl.ds(r0, 256)] = kt.astype(BF)
        V[pl.ds(r0, 256), :] = (jnp.dot(rows, wv, preferred_element_type=F32) + bv).astype(BF)
        return most

    return block


def patch_rows(plen):
    lens = jnp.broadcast_to(plen.astype(F32), (256, 256))
    sub = lax.broadcasted_iota(jnp.int32, (256, 256), 0)
    lane = lax.broadcasted_iota(jnp.int32, (256, 256), 1)
    ends_col = jnp.sum(jnp.where(lane <= sub, lens, 0.0), axis=1, keepdims=True)
    ends_row = jnp.sum(jnp.where(lane == sub, ends_col, 0.0), axis=0, keepdims=True)
    return ends_row - plen.astype(F32), ends_row


def limits(qb, g, base, total, starts_row, ends_row):
    r = lax.broadcasted_iota(jnp.int32, (256, 1), 0)
    row = (base + 512 * qb + 64 * (r // 32) + 32 * g + r % 32).astype(F32)
    first = jnp.max(jnp.where(starts_row <= row, starts_row, 0.0), axis=1, keepdims=True)
    finish = jnp.min(jnp.where(ends_row > row, ends_row, total.astype(F32)), axis=1, keepdims=True)
    shift = (1024 - base).astype(F32)
    first = (first + shift).astype(jnp.int32)
    finish = (finish + shift).astype(jnp.int32)
    kb0 = jnp.maximum(jnp.min(first) // 128, 0)
    kb1 = jnp.minimum((jnp.max(finish) + 127) // 128, 32)
    return first, finish, kb0, kb1


def queries(rows, QW, QB):
    wq = jnp.concatenate([QW[0, 0], QW[1, 0]], axis=1)
    bq = jnp.concatenate([QB[0, 0:1, :], QB[1, 0:1, :]], axis=1)
    return ((jnp.dot(rows, wq, preferred_element_type=F32) + bq) * Q_SCALE).astype(BF)


def pair_tools():
    half = lax.broadcasted_iota(jnp.int32, (32, 128), 0) < 16
    k_low = jnp.where(half, 1.0, 0.0).astype(BF)
    k_high = jnp.where(half, 0.0, 1.0).astype(BF)
    col_head = lax.broadcasted_iota(jnp.int32, (128, 128), 1) // 16
    cols = [jnp.where(col_head == a, 1.0, 0.0).astype(BF) for a in range(8)]

    def mask(kb, first, finish):
        key = kb * 128 + lax.broadcasted_iota(jnp.int32, (256, 128), 1)
        madd = jnp.where((key >= first) & (key < finish), 0.0, -jnp.inf)
        return jnp.concatenate([madd, madd], axis=1)

    def scores(Q8, p, kt, madd):
        part = kt[32 * p : 32 * p + 32, :]
        pair = jnp.concatenate([part * k_low, part * k_high], axis=1)
        return jnp.dot(Q8[p], pair, preferred_element_type=F32) + madd

    def step(kb, k0, Q8, KT, V, first, finish, M=None):
        kt = KT[:, pl.ds(k0, 128)]
        vb = V[pl.ds(k0, 128), :]
        madd = mask(kb, first, finish)
        out = []
        for h in range(2):
            vh = vb[:, 128 * h : 128 * h + 128]
            ps, vs = [], []
            for a in range(4):
                p = 4 * h + a
                s = scores(Q8, p, kt, madd)
                if M is not None:
                    s = s - M[p]
                ps.append(jnp.exp2(s).astype(BF))
                for c in (cols[2 * a], cols[2 * a + 1]):
                    vs.append(jnp.concatenate([vh * c, c], axis=1))
            out.append(
                jnp.dot(
                    jnp.concatenate(ps, axis=1),
                    jnp.concatenate(vs, axis=0),
                    preferred_element_type=F32,
                )
            )
        return out

    return mask, scores, step


def near_kernel(
    sc, plen, own, oth, qkvm, qkvo, qbm, qbo, acc_h, q_h, most_h, NE, KT, V, Q8, acc_o, q_o,
    most_o, QW, QB, PL, sems,
):
    g, base, total = sc[0], sc[1], sc[2]
    wait(
        copies(
            sems,
            [
                (own, NE.at[:, g]), (oth, NE.at[:, 1 - g]), (qkvm, QW.at[0]), (qkvo, QW.at[1]),
                (qbm, QB.at[0]), (qbo, QB.at[1]), (plen, PL),
            ],
        )
    )
    block = key_values(NE, KT, V, QW, QB)
    most = lax.fori_loop(0, 8, block, jnp.zeros((8, 256), F32))
    most_o[...] = jnp.broadcast_to(jnp.max(most), (8, 128))
    leave = pltpu.make_async_copy(most_o, most_h, sems.at[7])
    leave.start()

    def results(qb):
        at = pl.ds(pl.multiple_of(256 * qb, 256), 256)
        return (
            pltpu.make_async_copy(acc_o.at[qb], acc_h.at[qb], sems.at[8 + qb]),
            pltpu.make_async_copy(q_o.at[at], q_h.at[at], sems.at[12 + qb]),
        )

    starts_row, ends_row = patch_rows(PL[...])
    mask, scores, step = pair_tools()

    def q_block(qb, _):
        r0 = pl.multiple_of(qb * 256, 256)
        q = queries(NE[pl.ds(8 * qb, 8), g].reshape(256, 256), QW, QB)
        q_o[pl.ds(r0, 256), :] = q
        for p in range(8):
            Q8[p] = q[:, 32 * p : 32 * p + 32]
        first, finish, kb0, kb1 = limits(qb, g, base, total, starts_row, ends_row)
        acc_o[qb] = jnp.zeros((2, 256, 256), F32)

        def body(kb, _):
            k0 = pl.multiple_of((kb - 8) * 128, 128)
            for h, x in enumerate(step(kb, k0, Q8, KT, V, first, finish)):
                acc_o[qb, h] += x
            return 0

        lax.fori_loop(jnp.maximum(kb0, 8), jnp.minimum(kb1, 24), body, 0)
        for copy in results(qb):
            copy.start()
        return 0

    lax.fori_loop(0, 4, q_block, 0)
    leave.wait()
    for qb in range(4):
        wait(results(qb))


QKV_SCRATCH = [((2, 3, 256, 128), BF), ((2, 3, 128), F32), ((1, 256), jnp.int32)]


def near_call(*args):
    out = [
        jax.ShapeDtypeStruct((4, 2, 256, 256), F32),
        jax.ShapeDtypeStruct((1024, 256), BF),
        jax.ShapeDtypeStruct((8, 128), F32),
    ]
    scratch = [
        ((32, 2, 32, 256), BF), ((256, 2048), BF), ((2048, 256), BF), ((8, 256, 32), BF),
        ((4, 2, 256, 256), F32), ((1024, 256), BF), ((8, 128), F32),
    ] + QKV_SCRATCH
    return call(near_kernel, "near", 1, args, out, scratch, 16, 20 * 10**9, space=pltpu.HBM)


def far_kernel(
    sc, sel, plen, own, oth, lo_own, lo_oth, hi_own, hi_oth, sec_i, acc_i, q_i, most_i, qkvm, qkvo,
    qbm, qbo, prw, prb, n2g, f1m, f1o, b1m, b1o, f2m, f2o, f2b, send, NE, KT, V, Q8, ACC, OUT, M,
    SEC, AI, QI, MI, PW, VEC, F1, B1, F2, QW, QB, PL, sems,
):
    g, base, total = sc[0], sc[1], sc[2]
    pw_a, pw_b = turned(prw, g)
    started = copies(
        sems,
        [
            (lo_own, NE.at[0:16, g]), (lo_oth, NE.at[0:16, 1 - g]), (hi_own, NE.at[48:64, g]),
            (hi_oth, NE.at[48:64, 1 - g]), (qkvm, QW.at[0]), (qkvo, QW.at[1]), (qbm, QB.at[0]),
            (qbo, QB.at[1]), (plen, PL), (most_i, MI), (q_i, QI), (acc_i, AI), (sec_i, SEC),
            (pw_a, PW.at[0:128]), (pw_b, PW.at[128:256]), (prb, VEC.at[0]), (n2g, VEC.at[1]),
            (f2b, VEC.at[2]), (f1m, F1.at[0]), (f1o, F1.at[1]), (b1m, B1.at[0]), (b1o, B1.at[1]),
            (f2m, F2.at[0]), (f2o, F2.at[1]),
        ],
    )
    wait(started[:11])
    block = key_values(NE, KT, V, QW, QB)
    starts_row, ends_row = patch_rows(PL[...])
    edge_lo = limits(0, g, base, total, starts_row, ends_row)[2]
    edge_hi = limits(3, g, base, total, starts_row, ends_row)[3]
    most = lax.fori_loop(jnp.minimum(edge_lo // 2, 4), 4, block, jnp.zeros((8, 256), F32))
    most = lax.fori_loop(12, jnp.maximum((edge_hi + 1) // 2, 12), block, most)
    key_most = jnp.maximum(jnp.max(most), jnp.max(MI[...]))
    mask, scores, step = pair_tools()
    hs = lax.broadcasted_iota(jnp.int32, (256, 128), 0) // 16
    hl = lax.broadcasted_iota(jnp.int32, (256, 128), 1)
    head_sel = jnp.where(hs == hl, 1.0, 0.0).astype(BF)
    def q_most(r0):
        q = QI[pl.ds(r0, 256), :]
        return jnp.max(jnp.dot(q * q, head_sel, preferred_element_type=F32))

    bound = q_most(0)
    for i in range(1, 4):
        bound = jnp.maximum(bound, q_most(256 * i))
    calm = bound * key_most * 1.05 <= 1e4

    @pl.when(jnp.logical_not(calm))
    def _():
        wait(copies(sems.at[24:26], [(own, NE.at[16:48, g]), (oth, NE.at[16:48, 1 - g])]))
        lax.fori_loop(4, 12, block, jnp.zeros((8, 256), F32))

    wait(started[11:])

    def q_block(qb, _):
        r0 = pl.multiple_of(qb * 256, 256)
        q = QI[pl.ds(r0, 256), :]
        for p in range(8):
            Q8[p] = q[:, 32 * p : 32 * p + 32]
        first, finish, kb0, kb1 = limits(qb, g, base, total, starts_row, ends_row)

        def body(kb, _, M=None):
            k0 = pl.multiple_of(kb * 128, 128)
            for h, x in enumerate(step(kb, k0, Q8, KT, V, first, finish, M)):
                ACC[h] += x
            return 0

        @pl.when(calm)
        def _():
            ACC[...] = AI[qb]
            lax.fori_loop(kb0, jnp.minimum(kb1, 8), body, 0)
            lax.fori_loop(jnp.maximum(kb0, 24), kb1, body, 0)

        @pl.when(jnp.logical_not(calm))
        def _():
            ACC[...] = jnp.zeros_like(ACC)
            M[...] = jnp.full(M.shape, -jnp.inf, F32)

            def top(kb, _):
                kt = KT[:, pl.ds(pl.multiple_of(kb * 128, 128), 128)]
                madd = mask(kb, first, finish)
                for p in range(8):
                    M[p] = jnp.maximum(M[p], scores(Q8, p, kt, madd))
                return 0

            lax.fori_loop(kb0, kb1, top, 0)
            for p in range(8):
                for h in range(2):
                    part = M[p, :, 128 * h : 128 * h + 128]
                    M[p, :, 128 * h : 128 * h + 128] = jnp.broadcast_to(
                        jnp.max(part, axis=1, keepdims=True), (256, 128)
                    )
            lax.fori_loop(kb0, kb1, lambda kb, c: body(kb, c, M), 0)

        attn = jnp.concatenate(
            [ACC[h, :, 0:128] / ACC[h, :, 128:256] for h in range(2)], axis=1
        ).astype(BF)
        two = (
            SEC[pl.ds(r0, 256), :].astype(F32)
            + jnp.dot(attn, PW[...], preferred_element_type=F32)
            + VEC[0]
        ).astype(BF)
        wide = two.astype(F32)
        normed = layer_norm(wide, VEC[1]).astype(BF)
        total_rows = wide + VEC[2]
        for h in range(2):
            x = jnp.dot(normed, F1[h], preferred_element_type=F32) + B1[h]
            x = (0.5 * x * (1.0 + lax.erf(x * 0.7071067811865476))).astype(BF)
            total_rows = total_rows + jnp.dot(x, F2[h], preferred_element_type=F32)
        OUT[pl.ds(r0, 256), :] = total_rows.astype(BF)
        return 0

    lax.fori_loop(0, 4, q_block, 0)

    def place(d, _):
        send[pl.ds(pl.multiple_of(32 * d, 32), 32), :] = OUT[
            pl.ds(pl.multiple_of(32 * sel[d], 32), 32), :
        ]
        return 0

    lax.fori_loop(0, 64, place, 0, unroll=4)


def far_call(*args):
    scratch = [
        ((64, 2, 32, 256), BF), ((256, 4096), BF), ((4096, 256), BF), ((8, 256, 32), BF),
        ((2, 256, 256), F32), ((1024, 256), BF), ((8, 256, 256), F32), ((1024, 256), BF),
        ((4, 2, 256, 256), F32), ((1024, 256), BF), ((8, 128), F32), ((256, 256), BF),
        ((3, 1, 256), F32), ((2, 256, 512), BF), ((2, 1, 512), F32), ((2, 512, 256), BF),
    ] + QKV_SCRATCH
    out = [jax.ShapeDtypeStruct((2048, 256), BF)]
    return call(far_kernel, "far", 2, args, out, scratch, 26, 20 * 10**9)[0]


def last_kernel(sc, zs, zv, own, oth, out):
    g = sc[0]
    place = zv[0:1, 0:64] % 64
    place = place % 32 + jnp.where(place // 32 == g, 0, 32)
    place = jnp.where(lax.broadcasted_iota(jnp.int32, (64, 64), 0) == place, 1.0, 0.0)
    perm = jnp.transpose(place).astype(BF)

    def step(k, _):
        source = lax.shift_right_logical(zs[64 * k], 11)
        rows = jnp.concatenate([own[source], oth[source]], axis=0)
        out[pl.ds(pl.multiple_of(64 * k, 64), 64), :] = jnp.dot(
            perm, rows, preferred_element_type=F32
        ).astype(BF)
        return 0

    lax.fori_loop(0, 32, step, 0, unroll=8)


def last_call(*args):
    smem, vmem = pl.BlockSpec(memory_space=pltpu.SMEM), pl.BlockSpec(memory_space=pltpu.VMEM)
    return pl.pallas_call(
        last_kernel,
        out_shape=jax.ShapeDtypeStruct((2048, 256), BF),
        in_specs=[smem] * 2 + [vmem] * 3,
        out_specs=vmem,
        compiler_params=pltpu.CompilerParams(vmem_limit_bytes=16 * 2**20),
        name="relabel",
    )(*args)


def local(
    points, neighbours, patch_len, zorder, conv_w, conv_b, cpe_w, cpe_b, cpe_gain, norm1_gain,
    qkv_w, qkv_b, proj_w, proj_b, norm2_gain, fc1_w, fc1_b, fc2_w, fc2_b,
):
    g = lax.axis_index("grp").astype(jnp.int32)
    me = lax.axis_index("pts").astype(jnp.int32)
    peers = lax.axis_size("pts")
    rows = points.shape[0]
    forward = [(i, i + 1) for i in range(peers - 1)]
    backward = [(i + 1, i) for i in range(peers - 1)]

    def swap(x):
        return lax.ppermute(x, "grp", [(0, 1), (1, 0)])

    def pieces(x):
        return x.reshape(-1, 32, 256)

    order = zorder.reshape(16, 128)
    low = lax.ppermute(points[rows - 256 :], "pts", forward)
    high = lax.ppermute(points[:256], "pts", backward)
    sources = jnp.arange(peers, dtype=jnp.int32)[:, None]
    run = zorder[::64][None, :]
    wanted = jnp.max(jnp.where(run // rows == sources, run % rows // 64, 0), axis=1)
    wanted = jnp.broadcast_to(wanted[:, None, None], (peers, 1, 128))
    sel = lax.all_to_all(wanted, "pts", split_axis=0, concat_axis=0, tiled=True)[:, 0, 0]
    sel, low = lax.optimization_barrier((sel, low))
    conv_m = conv_w.reshape(27 * 256, 128)
    conv_o, bias_o = swap(conv_m), swap(conv_b)
    scalars = jnp.stack([g, me * rows, jnp.int32(rows * peers)])
    section_one, normed, lo_half, hi_half = conv_call(
        scalars, points, low, high, neighbours.T, conv_m, conv_o, conv_b[None], bias_o[None],
        cpe_w, cpe_b[None], cpe_gain[None], norm1_gain[None],
    )
    qkv_m = jnp.transpose(qkv_w, (1, 0, 2))
    weights = (qkv_m, swap(qkv_m), qkv_b, swap(qkv_b))
    fc1_o, fc2_o, b1_o = swap(fc1_w), swap(fc2_w), swap(fc1_b)
    other = swap(normed)
    lo_own = lax.ppermute(lo_half, "pts", forward)
    hi_own = lax.ppermute(hi_half, "pts", backward)
    acc, query, most = near_call(scalars, patch_len[None], pieces(normed), pieces(other), *weights)
    lo_own, hi_own, most = lax.optimization_barrier((lo_own, hi_own, most))
    lo_oth, hi_oth = swap(lo_own), swap(hi_own)
    send = far_call(
        scalars, sel, patch_len[None], pieces(normed), pieces(other), pieces(lo_own),
        pieces(lo_oth), pieces(hi_own), pieces(hi_oth), section_one, acc, query, most, *weights,
        proj_w, proj_b[None], norm2_gain[None], fc1_w, fc1_o, fc1_b[None], b1_o[None], fc2_w,
        fc2_o, fc2_b[None],
    )
    got = lax.all_to_all(send, "pts", split_axis=0, concat_axis=0, tiled=True)
    return last_call(scalars, zorder, order, pieces(got), pieces(swap(got)))


def solution(mesh):
    placed = (
        P("pts", None), P("pts", None), P(), P("pts"), P(None, None, "grp"), P("grp"), P(), P(), P(),
        P(), P(None, None, "grp"), P(None, "grp"), P(), P(), P(), P(None, "grp"), P("grp"),
        P("grp", None), P(),
    )
    return jax.shard_map(
        local, mesh=mesh, in_specs=placed, out_specs=P("pts", None), check_vma=False
    )
```

```python
import jax
import jax.numpy as jnp
from jax import lax
from jax.experimental import pallas as pl
from jax.experimental.pallas import tpu as pltpu
from jax.sharding import PartitionSpec as P

F32=jnp.float32; BF=jnp.bfloat16

VMEM_BYTES = 64 * 2**20 - 65536
Q_SCALE = 0.25 * 1.4426950408889634


def layer_norm(v, gain):
    c = v - jnp.mean(v, axis=-1, keepdims=True)
    s = jnp.mean(c * c, axis=-1, keepdims=True)
    return c * lax.rsqrt(s + 1e-05) * gain

RB = 128
TAPS = [t for t in range(27) if t != 13]


def copies(sems, pairs):
    out = [pltpu.make_async_copy(src, dst, sems.at[i]) for i, (src, dst) in enumerate(pairs)]
    for copy in out:
        copy.start()
    return out


def wait(some):
    for copy in some:
        copy.wait()


def turned(ref, g):
    first = ref.at[pl.ds(pl.multiple_of(128 * g, 128), 128)]
    return first, ref.at[pl.ds(pl.multiple_of(128 - 128 * g, 128), 128)]


def conv_kernel(
    sc, pts, low, high, nbs, wm, wo, cbm, cbo, cpw, cpb, cpg, n1g, sec_o, nrm_o, lo_o, hi_o,
    X, NT, NB, OH, G, W, CW, CB, CV, sems,
):
    g = sc[0]
    base = sc[1]
    cw_a, cw_b = turned(cpw, g)
    started = copies(
        sems,
        [
            (nbs, NT), (pts, X.at[256:2304]), (low, X.at[0:256]), (high, X.at[2304:2560]),
            (wm, W.at[:, 0:128]), (wo, W.at[:, 128:256]), (cw_a, CW.at[0:128]),
            (cw_b, CW.at[128:256]), (cbm, CB.at[:, 0:128]), (cbo, CB.at[:, 128:256]),
            (cpb, CV.at[0]), (cpg, CV.at[1]), (n1g, CV.at[2]),
        ],
    )
    wait(started[:4])
    lanes = lax.broadcasted_iota(jnp.int32, (RB, 768), 1)
    for b in range(8):
        NB[256 * b : 256 * b + 256, :] = jnp.transpose(NT[:, 256 * b : 256 * b + 256])

    def block(b, OH):
        rel = []
        for j in range(RB // 32):
            rel.append(NB[pl.ds(pl.multiple_of(256 * b + 64 * j + 32 * g, 32), 32), :])
        rel = jnp.concatenate(rel, axis=0)
        rel = jnp.where(rel < 0, -1, rel - (base + 256 * b - 256))
        for i, t in enumerate(TAPS):
            col = rel[:, t : t + 1]
            OH[i * RB : (i + 1) * RB, :] = jnp.where(
                lanes == col, jnp.array(1, BF), jnp.array(0, BF)
            )
        win = X[pl.ds(256 * b, 768), :]
        to = pl.ds(b * RB, RB)
        out = jnp.dot(OH[...], win, preferred_element_type=F32).astype(BF)
        for i, t in enumerate(TAPS):
            G[to, t * 256 : (t + 1) * 256] = out[i * RB : (i + 1) * RB, :]
        for j in range(RB // 32):
            G[pl.ds(b * RB + 32 * j, 32), 13 * 256 : 14 * 256] = X[
                pl.ds(pl.multiple_of(256 + 256 * b + 64 * j + 32 * g, 32), 32), :
            ]

    for b in range(1024 // RB):
        block(b, OH.at[b % 2])
    wait(started[4:])

    def finish(m, _):
        r0 = pl.multiple_of(m * 512, 512)
        at = pl.ds(r0, 512)
        acc = jnp.dot(G[at, :], W[...], preferred_element_type=F32)
        conv = (acc + CB[...]).astype(BF)
        c = jnp.dot(conv, CW[...], preferred_element_type=F32) + CV[0]
        own = G[at, 13 * 256 : 14 * 256].astype(F32)
        sec = (own + layer_norm(c, CV[1])).astype(BF)
        sec_o[at, :] = sec
        normed = layer_norm(sec.astype(F32), CV[2]).astype(BF)
        nrm_o[at, :] = normed

        @pl.when(m == 0)
        def _():
            hi_o[...] = normed

        @pl.when(m == 1)
        def _():
            lo_o[...] = normed

        return 0

    lax.fori_loop(0, 2, finish, 0)


def call(kernel, name, smem, args, out_shape, scratch, sems, flops, space=pltpu.VMEM):
    return pl.pallas_call(
        kernel,
        out_shape=out_shape,
        in_specs=[pl.BlockSpec(memory_space=pltpu.SMEM)] * smem
        + [pl.BlockSpec(memory_space=pltpu.HBM)] * (len(args) - smem),
        out_specs=[pl.BlockSpec(memory_space=space)] * len(out_shape),
        scratch_shapes=[pltpu.VMEM(*x) for x in scratch] + [pltpu.SemaphoreType.DMA((sems,))],
        compiler_params=pltpu.CompilerParams(vmem_limit_bytes=VMEM_BYTES),
        cost_estimate=pl.CostEstimate(flops=flops, bytes_accessed=8 * 10**6, transcendentals=0),
        name=name,
    )(*args)


def conv_call(*args):
    out = [jax.ShapeDtypeStruct((n, 256), BF) for n in (1024, 1024, 512, 512)]
    scratch = [
        ((2560, 256), BF), ((27, 2048), jnp.int32), ((2048, 27), jnp.int32), ((2, 26 * RB, 768), BF), ((1024, 6912), BF),
        ((6912, 256), BF), ((256, 256), BF), ((1, 256), F32), ((3, 1, 256), F32),
    ]
    return call(conv_kernel, "conv", 1, args, out, scratch, 13, 30 * 10**9)


def key_values(NE, KT, V, QW, QB):
    wkt = [jnp.transpose(QW[h, 1]) for h in range(2)]
    bkc = [jnp.transpose(jnp.broadcast_to(QB[h, 1:2, :], (8, 128)))[:, :1] for h in range(2)]
    wv = jnp.concatenate([QW[0, 2], QW[1, 2]], axis=1)
    bv = jnp.concatenate([QB[0, 2:3, :], QB[1, 2:3, :]], axis=1)

    def block(i, most):
        r0 = pl.multiple_of(i * 256, 256)
        rows = NE[pl.ds(4 * i, 4)].reshape(256, 256)
        for h in range(2):
            kt = (
                lax.dot_general(
                    wkt[h], rows, (((1,), (1,)), ((), ())), preferred_element_type=F32
                )
                + bkc[h]
            )
            most = jnp.maximum(most, jnp.sum((kt * kt).reshape(8, 16, 256), axis=1))
            KT[128 * h : 128 * h + 128, pl.ds(r0, 256)] = kt.astype(BF)
        V[pl.ds(r0, 256), :] = (jnp.dot(rows, wv, preferred_element_type=F32) + bv).astype(BF)
        return most

    return block


def patch_rows(plen):
    lens = jnp.broadcast_to(plen.astype(F32), (256, 256))
    sub = lax.broadcasted_iota(jnp.int32, (256, 256), 0)
    lane = lax.broadcasted_iota(jnp.int32, (256, 256), 1)
    ends_col = jnp.sum(jnp.where(lane <= sub, lens, 0.0), axis=1, keepdims=True)
    ends_row = jnp.sum(jnp.where(lane == sub, ends_col, 0.0), axis=0, keepdims=True)
    return ends_row - plen.astype(F32), ends_row


def limits(qb, g, base, total, starts_row, ends_row):
    r = lax.broadcasted_iota(jnp.int32, (256, 1), 0)
    row = (base + 512 * qb + 64 * (r // 32) + 32 * g + r % 32).astype(F32)
    first = jnp.max(jnp.where(starts_row <= row, starts_row, 0.0), axis=1, keepdims=True)
    finish = jnp.min(jnp.where(ends_row > row, ends_row, total.astype(F32)), axis=1, keepdims=True)
    shift = (1024 - base).astype(F32)
    first = (first + shift).astype(jnp.int32)
    finish = (finish + shift).astype(jnp.int32)
    kb0 = jnp.maximum(jnp.min(first) // 128, 0)
    kb1 = jnp.minimum((jnp.max(finish) + 127) // 128, 32)
    return first, finish, kb0, kb1


def queries(rows, QW, QB):
    wq = jnp.concatenate([QW[0, 0], QW[1, 0]], axis=1)
    bq = jnp.concatenate([QB[0, 0:1, :], QB[1, 0:1, :]], axis=1)
    return ((jnp.dot(rows, wq, preferred_element_type=F32) + bq) * Q_SCALE).astype(BF)


def pair_tools():
    half = lax.broadcasted_iota(jnp.int32, (32, 128), 0) < 16
    k_low = jnp.where(half, 1.0, 0.0).astype(BF)
    k_high = jnp.where(half, 0.0, 1.0).astype(BF)
    col_head = lax.broadcasted_iota(jnp.int32, (128, 128), 1) // 16
    cols = [jnp.where(col_head == a, 1.0, 0.0).astype(BF) for a in range(8)]

    def mask(kb, first, finish):
        key = kb * 128 + lax.broadcasted_iota(jnp.int32, (256, 128), 1)
        madd = jnp.where((key >= first) & (key < finish), 0.0, -jnp.inf)
        return jnp.concatenate([madd, madd], axis=1)

    def scores(Q8, p, kt, madd):
        part = kt[32 * p : 32 * p + 32, :]
        pair = jnp.concatenate([part * k_low, part * k_high], axis=1)
        return jnp.dot(Q8[p], pair, preferred_element_type=F32) + madd

    def step(kb, k0, Q8, KT, V, first, finish, M=None):
        kt = KT[:, pl.ds(k0, 128)]
        vb = V[pl.ds(k0, 128), :]
        madd = mask(kb, first, finish)
        out = []
        for h in range(2):
            vh = vb[:, 128 * h : 128 * h + 128]
            ps, vs = [], []
            for a in range(4):
                p = 4 * h + a
                s = scores(Q8, p, kt, madd)
                if M is not None:
                    s = s - M[p]
                ps.append(jnp.exp2(s).astype(BF))
                for c in (cols[2 * a], cols[2 * a + 1]):
                    vs.append(jnp.concatenate([vh * c, c], axis=1))
            out.append(
                jnp.dot(
                    jnp.concatenate(ps, axis=1),
                    jnp.concatenate(vs, axis=0),
                    preferred_element_type=F32,
                )
            )
        return out

    return mask, scores, step


def near_kernel(
    sc, plen, own, oth, qkvm, qkvo, qbm, qbo, acc_h, q_h, most_h, NE, KT, V, Q8, acc_o, q_o,
    most_o, QW, QB, PL, sems,
):
    g, base, total = sc[0], sc[1], sc[2]
    wait(
        copies(
            sems,
            [
                (own, NE.at[:, g]), (oth, NE.at[:, 1 - g]), (qkvm, QW.at[0]), (qkvo, QW.at[1]),
                (qbm, QB.at[0]), (qbo, QB.at[1]), (plen, PL),
            ],
        )
    )
    block = key_values(NE, KT, V, QW, QB)
    most = lax.fori_loop(0, 8, block, jnp.zeros((8, 256), F32))
    most_o[...] = jnp.broadcast_to(jnp.max(most), (8, 128))
    leave = pltpu.make_async_copy(most_o, most_h, sems.at[7])
    leave.start()

    def results(qb):
        at = pl.ds(pl.multiple_of(256 * qb, 256), 256)
        return (
            pltpu.make_async_copy(acc_o.at[qb], acc_h.at[qb], sems.at[8 + qb]),
            pltpu.make_async_copy(q_o.at[at], q_h.at[at], sems.at[12 + qb]),
        )

    starts_row, ends_row = patch_rows(PL[...])
    mask, scores, step = pair_tools()

    def q_block(qb, _):
        r0 = pl.multiple_of(qb * 256, 256)
        q = queries(NE[pl.ds(8 * qb, 8), g].reshape(256, 256), QW, QB)
        q_o[pl.ds(r0, 256), :] = q
        for p in range(8):
            Q8[p] = q[:, 32 * p : 32 * p + 32]
        first, finish, kb0, kb1 = limits(qb, g, base, total, starts_row, ends_row)
        acc_o[qb] = jnp.zeros((2, 256, 256), F32)

        def body(kb, _):
            k0 = pl.multiple_of((kb - 8) * 128, 128)
            for h, x in enumerate(step(kb, k0, Q8, KT, V, first, finish)):
                acc_o[qb, h] += x
            return 0

        lax.fori_loop(jnp.maximum(kb0, 8), jnp.minimum(kb1, 24), body, 0)
        for copy in results(qb):
            copy.start()
        return 0

    lax.fori_loop(0, 4, q_block, 0)
    leave.wait()
    for qb in range(4):
        wait(results(qb))


QKV_SCRATCH = [((2, 3, 256, 128), BF), ((2, 3, 128), F32), ((1, 256), jnp.int32)]


def near_call(*args):
    out = [
        jax.ShapeDtypeStruct((4, 2, 256, 256), F32),
        jax.ShapeDtypeStruct((1024, 256), BF),
        jax.ShapeDtypeStruct((8, 128), F32),
    ]
    scratch = [
        ((32, 2, 32, 256), BF), ((256, 2048), BF), ((2048, 256), BF), ((8, 256, 32), BF),
        ((4, 2, 256, 256), F32), ((1024, 256), BF), ((8, 128), F32),
    ] + QKV_SCRATCH
    return call(near_kernel, "near", 1, args, out, scratch, 16, 20 * 10**9, space=pltpu.HBM)


def far_kernel(
    sc, sel, plen, own, oth, lo_own, lo_oth, hi_own, hi_oth, sec_i, acc_i, q_i, most_i, qkvm, qkvo,
    qbm, qbo, prw, prb, n2g, f1m, f1o, b1m, b1o, f2m, f2o, f2b, send, NE, KT, V, Q8, ACC, OUT, M,
    SEC, AI, QI, MI, PW, VEC, F1, B1, F2, QW, QB, PL, sems,
):
    g, base, total = sc[0], sc[1], sc[2]
    pw_a, pw_b = turned(prw, g)
    started = copies(
        sems,
        [
            (lo_own, NE.at[0:16, g]), (lo_oth, NE.at[0:16, 1 - g]), (hi_own, NE.at[48:64, g]),
            (hi_oth, NE.at[48:64, 1 - g]), (qkvm, QW.at[0]), (qkvo, QW.at[1]), (qbm, QB.at[0]),
            (qbo, QB.at[1]), (plen, PL), (most_i, MI), (q_i, QI), (acc_i, AI), (sec_i, SEC),
            (pw_a, PW.at[0:128]), (pw_b, PW.at[128:256]), (prb, VEC.at[0]), (n2g, VEC.at[1]),
            (f2b, VEC.at[2]), (f1m, F1.at[0]), (f1o, F1.at[1]), (b1m, B1.at[0]), (b1o, B1.at[1]),
            (f2m, F2.at[0]), (f2o, F2.at[1]),
        ],
    )
    wait(started[:11])
    block = key_values(NE, KT, V, QW, QB)
    starts_row, ends_row = patch_rows(PL[...])
    edge_lo = limits(0, g, base, total, starts_row, ends_row)[2]
    edge_hi = limits(3, g, base, total, starts_row, ends_row)[3]
    most = lax.fori_loop(jnp.minimum(edge_lo // 2, 4), 4, block, jnp.zeros((8, 256), F32))
    most = lax.fori_loop(12, jnp.maximum((edge_hi + 1) // 2, 12), block, most)
    key_most = jnp.maximum(jnp.max(most), jnp.max(MI[...]))
    mask, scores, step = pair_tools()
    hs = lax.broadcasted_iota(jnp.int32, (256, 128), 0) // 16
    hl = lax.broadcasted_iota(jnp.int32, (256, 128), 1)
    head_sel = jnp.where(hs == hl, 1.0, 0.0).astype(BF)
    def q_most(r0):
        q = QI[pl.ds(r0, 256), :]
        return jnp.max(jnp.dot(q * q, head_sel, preferred_element_type=F32))

    bound = q_most(0)
    for i in range(1, 4):
        bound = jnp.maximum(bound, q_most(256 * i))
    calm = bound * key_most * 1.05 <= 1e4

    @pl.when(jnp.logical_not(calm))
    def _():
        wait(copies(sems.at[24:26], [(own, NE.at[16:48, g]), (oth, NE.at[16:48, 1 - g])]))
        lax.fori_loop(4, 12, block, jnp.zeros((8, 256), F32))

    wait(started[11:])

    def q_block(qb, _):
        r0 = pl.multiple_of(qb * 256, 256)
        q = QI[pl.ds(r0, 256), :]
        for p in range(8):
            Q8[p] = q[:, 32 * p : 32 * p + 32]
        first, finish, kb0, kb1 = limits(qb, g, base, total, starts_row, ends_row)

        def body(kb, _, M=None):
            k0 = pl.multiple_of(kb * 128, 128)
            for h, x in enumerate(step(kb, k0, Q8, KT, V, first, finish, M)):
                ACC[h] += x
            return 0

        @pl.when(calm)
        def _():
            ACC[...] = AI[qb]
            lax.fori_loop(kb0, jnp.minimum(kb1, 8), body, 0)
            lax.fori_loop(jnp.maximum(kb0, 24), kb1, body, 0)

        @pl.when(jnp.logical_not(calm))
        def _():
            ACC[...] = jnp.zeros_like(ACC)
            M[...] = jnp.full(M.shape, -jnp.inf, F32)

            def top(kb, _):
                kt = KT[:, pl.ds(pl.multiple_of(kb * 128, 128), 128)]
                madd = mask(kb, first, finish)
                for p in range(8):
                    M[p] = jnp.maximum(M[p], scores(Q8, p, kt, madd))
                return 0

            lax.fori_loop(kb0, kb1, top, 0)
            for p in range(8):
                for h in range(2):
                    part = M[p, :, 128 * h : 128 * h + 128]
                    M[p, :, 128 * h : 128 * h + 128] = jnp.broadcast_to(
                        jnp.max(part, axis=1, keepdims=True), (256, 128)
                    )
            lax.fori_loop(kb0, kb1, lambda kb, c: body(kb, c, M), 0)

        attn = jnp.concatenate(
            [ACC[h, :, 0:128] / ACC[h, :, 128:256] for h in range(2)], axis=1
        ).astype(BF)
        two = (
            SEC[pl.ds(r0, 256), :].astype(F32)
            + jnp.dot(attn, PW[...], preferred_element_type=F32)
            + VEC[0]
        ).astype(BF)
        wide = two.astype(F32)
        normed = layer_norm(wide, VEC[1]).astype(BF)
        total_rows = wide + VEC[2]
        for h in range(2):
            x = jnp.dot(normed, F1[h], preferred_element_type=F32) + B1[h]
            x = (0.5 * x * (1.0 + lax.erf(x * 0.7071067811865476))).astype(BF)
            total_rows = total_rows + jnp.dot(x, F2[h], preferred_element_type=F32)
        OUT[pl.ds(r0, 256), :] = total_rows.astype(BF)
        return 0

    lax.fori_loop(0, 4, q_block, 0)

    def place(d, _):
        send[pl.ds(pl.multiple_of(32 * d, 32), 32), :] = OUT[
            pl.ds(pl.multiple_of(32 * sel[d, 0, 0], 32), 32), :
        ]
        return 0

    lax.fori_loop(0, 64, place, 0, unroll=4)


def far_call(*args):
    scratch = [
        ((64, 2, 32, 256), BF), ((256, 4096), BF), ((4096, 256), BF), ((8, 256, 32), BF),
        ((2, 256, 256), F32), ((1024, 256), BF), ((8, 256, 256), F32), ((1024, 256), BF),
        ((4, 2, 256, 256), F32), ((1024, 256), BF), ((8, 128), F32), ((256, 256), BF),
        ((3, 1, 256), F32), ((2, 256, 512), BF), ((2, 1, 512), F32), ((2, 512, 256), BF),
    ] + QKV_SCRATCH
    out = [jax.ShapeDtypeStruct((2048, 256), BF)]
    return call(far_kernel, "far", 2, args, out, scratch, 26, 20 * 10**9)[0]


def last_kernel(sc, zs, zv, own, oth, out):
    g = sc[0]
    place = zv[0:1, 0:64] % 64
    place = place % 32 + jnp.where(place // 32 == g, 0, 32)
    place = jnp.where(lax.broadcasted_iota(jnp.int32, (64, 64), 0) == place, 1.0, 0.0)
    perm = jnp.transpose(place).astype(BF)

    def step(k, _):
        source = lax.shift_right_logical(zs[64 * k], 11)
        rows = jnp.concatenate([own[source], oth[source]], axis=0)
        out[pl.ds(pl.multiple_of(64 * k, 64), 64), :] = jnp.dot(
            perm, rows, preferred_element_type=F32
        ).astype(BF)
        return 0

    lax.fori_loop(0, 32, step, 0, unroll=8)


def last_call(*args):
    smem, vmem = pl.BlockSpec(memory_space=pltpu.SMEM), pl.BlockSpec(memory_space=pltpu.VMEM)
    return pl.pallas_call(
        last_kernel,
        out_shape=jax.ShapeDtypeStruct((2048, 256), BF),
        in_specs=[smem] * 2 + [vmem] * 3,
        out_specs=vmem,
        compiler_params=pltpu.CompilerParams(vmem_limit_bytes=16 * 2**20),
        name="relabel",
    )(*args)


def local(
    points, neighbours, patch_len, zorder, conv_w, conv_b, cpe_w, cpe_b, cpe_gain, norm1_gain,
    qkv_w, qkv_b, proj_w, proj_b, norm2_gain, fc1_w, fc1_b, fc2_w, fc2_b,
):
    g = lax.axis_index("grp").astype(jnp.int32)
    me = lax.axis_index("pts").astype(jnp.int32)
    peers = lax.axis_size("pts")
    rows = points.shape[0]
    forward = [(i, i + 1) for i in range(peers - 1)]
    backward = [(i + 1, i) for i in range(peers - 1)]

    def swap(x):
        return lax.ppermute(x, "grp", [(0, 1), (1, 0)])

    def pieces(x):
        return x.reshape(-1, 32, 256)

    order = zorder.reshape(16, 128)
    low = lax.ppermute(points[rows - 256 :], "pts", forward)
    high = lax.ppermute(points[:256], "pts", backward)
    conv_m = conv_w.reshape(27 * 256, 128)
    conv_o, bias_o = swap(conv_m), swap(conv_b)
    sources = jnp.arange(peers, dtype=jnp.int32)[:, None]
    run = zorder[::64][None, :]
    wanted = jnp.max(jnp.where(run // rows == sources, run % rows // 64, 0), axis=1)
    wanted = jnp.broadcast_to(wanted[:, None, None], (peers, 1, 128))
    wanted, bias_o = lax.optimization_barrier((wanted, bias_o))
    sel = lax.all_to_all(wanted, "pts", split_axis=0, concat_axis=0, tiled=True)
    sel, low = lax.optimization_barrier((sel, low))
    scalars = jnp.stack([g, me * rows, jnp.int32(rows * peers)])
    section_one, normed, lo_half, hi_half = conv_call(
        scalars, points, low, high, neighbours.T, conv_m, conv_o, conv_b[None], bias_o[None],
        cpe_w, cpe_b[None], cpe_gain[None], norm1_gain[None],
    )
    qkv_m = jnp.transpose(qkv_w, (1, 0, 2))
    weights = (qkv_m, swap(qkv_m), qkv_b, swap(qkv_b))
    fc1_o, fc2_o, b1_o = swap(fc1_w), swap(fc2_w), swap(fc1_b)
    other, b1_o = lax.optimization_barrier((swap(normed), b1_o))
    lo_own = lax.ppermute(lo_half, "pts", forward)
    hi_own = lax.ppermute(hi_half, "pts", backward)
    acc, query, most = near_call(scalars, patch_len[None], pieces(normed), pieces(other), *weights)
    lo_own, hi_own, most = lax.optimization_barrier((lo_own, hi_own, most))
    lo_oth, hi_oth = swap(lo_own), swap(hi_own)
    send = far_call(
        scalars, sel, patch_len[None], pieces(normed), pieces(other), pieces(lo_own),
        pieces(lo_oth), pieces(hi_own), pieces(hi_oth), section_one, acc, query, most, *weights,
        proj_w, proj_b[None], norm2_gain[None], fc1_w, fc1_o, fc1_b[None], b1_o[None], fc2_w,
        fc2_o, fc2_b[None],
    )
    got = lax.all_to_all(send, "pts", split_axis=0, concat_axis=0, tiled=True)
    return last_call(scalars, zorder, order, pieces(got), pieces(swap(got)))


def solution(mesh):
    placed = (
        P("pts", None), P("pts", None), P(), P("pts"), P(None, None, "grp"), P("grp"), P(), P(), P(),
        P(), P(None, None, "grp"), P(None, "grp"), P(), P(), P(), P(None, "grp"), P("grp"),
        P("grp", None), P(),
    )
    return jax.shard_map(
        local, mesh=mesh, in_specs=placed, out_specs=P("pts", None), check_vma=False
    )
```

```python
import jax
import jax.numpy as jnp
from jax import lax
from jax.experimental import pallas as pl
from jax.experimental.pallas import tpu as pltpu
from jax.sharding import PartitionSpec as P

F32=jnp.float32; BF=jnp.bfloat16

VMEM_BYTES = 64 * 2**20 - 65536
Q_SCALE = 0.25 * 1.4426950408889634


def layer_norm(v, gain):
    c = v - jnp.mean(v, axis=-1, keepdims=True)
    s = jnp.mean(c * c, axis=-1, keepdims=True)
    return c * lax.rsqrt(s + 1e-05) * gain

RB = 128
TAPS = [t for t in range(27) if t != 13]


def copies(sems, pairs):
    out = [pltpu.make_async_copy(src, dst, sems.at[i]) for i, (src, dst) in enumerate(pairs)]
    for copy in out:
        copy.start()
    return out


def wait(some):
    for copy in some:
        copy.wait()


def turned(ref, g):
    first = ref.at[pl.ds(pl.multiple_of(128 * g, 128), 128)]
    return first, ref.at[pl.ds(pl.multiple_of(128 - 128 * g, 128), 128)]


def conv_kernel(
    sc, pts, low, high, nbs, wm, wo, cbm, cbo, cpw, cpb, cpg, n1g, sec_o, nrm_o, lo_o, hi_o,
    X, NT, NB, OH, G, W, CW, CB, CV, sems,
):
    g = sc[0]
    base = sc[1]
    cw_a, cw_b = turned(cpw, g)
    started = copies(
        sems,
        [
            (nbs, NT), (pts, X.at[256:2304]), (low, X.at[0:256]), (high, X.at[2304:2560]),
            (wm, W.at[:, 0:128]), (wo, W.at[:, 128:256]), (cw_a, CW.at[0:128]),
            (cw_b, CW.at[128:256]), (cbm, CB.at[:, 0:128]), (cbo, CB.at[:, 128:256]),
            (cpb, CV.at[0]), (cpg, CV.at[1]), (n1g, CV.at[2]),
        ],
    )
    wait(started[:4])
    lanes = lax.broadcasted_iota(jnp.int32, (RB, 768), 1)
    for b in range(8):
        NB[256 * b : 256 * b + 256, :] = jnp.transpose(NT[:, 256 * b : 256 * b + 256])

    def block(b, OH):
        rel = []
        for j in range(RB // 32):
            rel.append(NB[pl.ds(pl.multiple_of(256 * b + 64 * j + 32 * g, 32), 32), :])
        rel = jnp.concatenate(rel, axis=0)
        rel = jnp.where(rel < 0, -1, rel - (base + 256 * b - 256))
        for i, t in enumerate(TAPS):
            col = rel[:, t : t + 1]
            OH[i * RB : (i + 1) * RB, :] = jnp.where(
                lanes == col, jnp.array(1, BF), jnp.array(0, BF)
            )
        win = X[pl.ds(256 * b, 768), :]
        to = pl.ds(b * RB, RB)
        out = jnp.dot(OH[...], win, preferred_element_type=F32).astype(BF)
        for i, t in enumerate(TAPS):
            G[to, t * 256 : (t + 1) * 256] = out[i * RB : (i + 1) * RB, :]
        for j in range(RB // 32):
            G[pl.ds(b * RB + 32 * j, 32), 13 * 256 : 14 * 256] = X[
                pl.ds(pl.multiple_of(256 + 256 * b + 64 * j + 32 * g, 32), 32), :
            ]

    for b in range(1024 // RB):
        block(b, OH.at[b % 2])
    wait(started[4:])

    def finish(m, _):
        r0 = pl.multiple_of(m * 512, 512)
        at = pl.ds(r0, 512)
        acc = jnp.dot(G[at, :], W[...], preferred_element_type=F32)
        conv = (acc + CB[...]).astype(BF)
        c = jnp.dot(conv, CW[...], preferred_element_type=F32) + CV[0]
        own = G[at, 13 * 256 : 14 * 256].astype(F32)
        sec = (own + layer_norm(c, CV[1])).astype(BF)
        sec_o[at, :] = sec
        normed = layer_norm(sec.astype(F32), CV[2]).astype(BF)
        nrm_o[at, :] = normed

        @pl.when(m == 0)
        def _():
            hi_o[...] = normed

        @pl.when(m == 1)
        def _():
            lo_o[...] = normed

        return 0

    lax.fori_loop(0, 2, finish, 0)


def call(kernel, name, smem, args, out_shape, scratch, sems, flops, space=pltpu.VMEM):
    return pl.pallas_call(
        kernel,
        out_shape=out_shape,
        in_specs=[pl.BlockSpec(memory_space=pltpu.SMEM)] * smem
        + [pl.BlockSpec(memory_space=pltpu.HBM)] * (len(args) - smem),
        out_specs=[pl.BlockSpec(memory_space=space)] * len(out_shape),
        scratch_shapes=[pltpu.VMEM(*x) for x in scratch] + [pltpu.SemaphoreType.DMA((sems,))],
        compiler_params=pltpu.CompilerParams(vmem_limit_bytes=VMEM_BYTES),
        cost_estimate=pl.CostEstimate(flops=flops, bytes_accessed=8 * 10**6, transcendentals=0),
        name=name,
    )(*args)


def conv_call(*args):
    out = [jax.ShapeDtypeStruct((n, 256), BF) for n in (1024, 1024, 512, 512)]
    scratch = [
        ((2560, 256), BF), ((27, 2048), jnp.int32), ((2048, 27), jnp.int32), ((2, 26 * RB, 768), BF), ((1024, 6912), BF),
        ((6912, 256), BF), ((256, 256), BF), ((1, 256), F32), ((3, 1, 256), F32),
    ]
    return call(conv_kernel, "conv", 1, args, out, scratch, 13, 30 * 10**9)


def key_values(NE, KT, V, QW, QB):
    wkt = [jnp.transpose(QW[h, 1]) for h in range(2)]
    bkc = [jnp.transpose(jnp.broadcast_to(QB[h, 1:2, :], (8, 128)))[:, :1] for h in range(2)]
    wv = jnp.concatenate([QW[0, 2], QW[1, 2]], axis=1)
    bv = jnp.concatenate([QB[0, 2:3, :], QB[1, 2:3, :]], axis=1)

    def block(i, most):
        r0 = pl.multiple_of(i * 256, 256)
        rows = NE[pl.ds(4 * i, 4)].reshape(256, 256)
        for h in range(2):
            kt = (
                lax.dot_general(
                    wkt[h], rows, (((1,), (1,)), ((), ())), preferred_element_type=F32
                )
                + bkc[h]
            )
            most = jnp.maximum(most, jnp.sum((kt * kt).reshape(8, 16, 256), axis=1))
            KT[128 * h : 128 * h + 128, pl.ds(r0, 256)] = kt.astype(BF)
        V[pl.ds(r0, 256), :] = (jnp.dot(rows, wv, preferred_element_type=F32) + bv).astype(BF)
        return most

    return block


def patch_rows(plen):
    lens = jnp.broadcast_to(plen.astype(F32), (256, 256))
    sub = lax.broadcasted_iota(jnp.int32, (256, 256), 0)
    lane = lax.broadcasted_iota(jnp.int32, (256, 256), 1)
    ends_col = jnp.sum(jnp.where(lane <= sub, lens, 0.0), axis=1, keepdims=True)
    ends_row = jnp.sum(jnp.where(lane == sub, ends_col, 0.0), axis=0, keepdims=True)
    return ends_row - plen.astype(F32), ends_row


def limits(qb, g, base, total, starts_row, ends_row):
    r = lax.broadcasted_iota(jnp.int32, (256, 1), 0)
    row = (base + 512 * qb + 64 * (r // 32) + 32 * g + r % 32).astype(F32)
    first = jnp.max(jnp.where(starts_row <= row, starts_row, 0.0), axis=1, keepdims=True)
    finish = jnp.min(jnp.where(ends_row > row, ends_row, total.astype(F32)), axis=1, keepdims=True)
    shift = (1024 - base).astype(F32)
    first = (first + shift).astype(jnp.int32)
    finish = (finish + shift).astype(jnp.int32)
    kb0 = jnp.maximum(jnp.min(first) // 128, 0)
    kb1 = jnp.minimum((jnp.max(finish) + 127) // 128, 32)
    return first, finish, kb0, kb1


def queries(rows, QW, QB):
    wq = jnp.concatenate([QW[0, 0], QW[1, 0]], axis=1)
    bq = jnp.concatenate([QB[0, 0:1, :], QB[1, 0:1, :]], axis=1)
    return ((jnp.dot(rows, wq, preferred_element_type=F32) + bq) * Q_SCALE).astype(BF)


def pair_tools():
    half = lax.broadcasted_iota(jnp.int32, (32, 128), 0) < 16
    k_low = jnp.where(half, 1.0, 0.0).astype(BF)
    k_high = jnp.where(half, 0.0, 1.0).astype(BF)
    col_head = lax.broadcasted_iota(jnp.int32, (128, 128), 1) // 16
    cols = [jnp.where(col_head == a, 1.0, 0.0).astype(BF) for a in range(8)]

    def mask(kb, first, finish):
        key = kb * 128 + lax.broadcasted_iota(jnp.int32, (256, 128), 1)
        madd = jnp.where((key >= first) & (key < finish), 0.0, -jnp.inf)
        return jnp.concatenate([madd, madd], axis=1)

    def scores(Q8, p, kt, madd):
        part = kt[32 * p : 32 * p + 32, :]
        pair = jnp.concatenate([part * k_low, part * k_high], axis=1)
        return jnp.dot(Q8[p], pair, preferred_element_type=F32) + madd

    def step(kb, k0, Q8, KT, V, first, finish, M=None):
        kt = KT[:, pl.ds(k0, 128)]
        vb = V[pl.ds(k0, 128), :]
        madd = mask(kb, first, finish)
        out = []
        for h in range(2):
            vh = vb[:, 128 * h : 128 * h + 128]
            ps, vs = [], []
            for a in range(4):
                p = 4 * h + a
                s = scores(Q8, p, kt, madd)
                if M is not None:
                    s = s - M[p]
                ps.append(jnp.exp2(s).astype(BF))
                for c in (cols[2 * a], cols[2 * a + 1]):
                    vs.append(jnp.concatenate([vh * c, c], axis=1))
            out.append(
                jnp.dot(
                    jnp.concatenate(ps, axis=1),
                    jnp.concatenate(vs, axis=0),
                    preferred_element_type=F32,
                )
            )
        return out

    return mask, scores, step


def near_kernel(
    sc, plen, own, oth, qkvm, qkvo, qbm, qbo, acc_h, q_h, most_h, NE, KT, V, Q8, acc_o, q_o,
    most_o, QW, QB, PL, sems,
):
    g, base, total = sc[0], sc[1], sc[2]
    wait(
        copies(
            sems,
            [
                (own, NE.at[:, g]), (oth, NE.at[:, 1 - g]), (qkvm, QW.at[0]), (qkvo, QW.at[1]),
                (qbm, QB.at[0]), (qbo, QB.at[1]), (plen, PL),
            ],
        )
    )
    block = key_values(NE, KT, V, QW, QB)
    most = lax.fori_loop(0, 8, block, jnp.zeros((8, 256), F32))
    most_o[...] = jnp.broadcast_to(jnp.max(most), (8, 128))
    leave = pltpu.make_async_copy(most_o, most_h, sems.at[7])
    leave.start()

    def results(qb):
        at = pl.ds(pl.multiple_of(256 * qb, 256), 256)
        return (
            pltpu.make_async_copy(acc_o.at[qb], acc_h.at[qb], sems.at[8 + qb]),
            pltpu.make_async_copy(q_o.at[at], q_h.at[at], sems.at[12 + qb]),
        )

    starts_row, ends_row = patch_rows(PL[...])
    mask, scores, step = pair_tools()

    def q_block(qb, _):
        r0 = pl.multiple_of(qb * 256, 256)
        q = queries(NE[pl.ds(8 * qb, 8), g].reshape(256, 256), QW, QB)
        q_o[pl.ds(r0, 256), :] = q
        for p in range(8):
            Q8[p] = q[:, 32 * p : 32 * p + 32]
        first, finish, kb0, kb1 = limits(qb, g, base, total, starts_row, ends_row)
        acc_o[qb] = jnp.zeros((2, 256, 256), F32)

        def body(kb, _):
            k0 = pl.multiple_of((kb - 8) * 128, 128)
            for h, x in enumerate(step(kb, k0, Q8, KT, V, first, finish)):
                acc_o[qb, h] += x
            return 0

        lax.fori_loop(jnp.maximum(kb0, 8), jnp.minimum(kb1, 24), body, 0)
        for copy in results(qb):
            copy.start()
        return 0

    lax.fori_loop(0, 4, q_block, 0)
    leave.wait()
    for qb in range(4):
        wait(results(qb))


QKV_SCRATCH = [((2, 3, 256, 128), BF), ((2, 3, 128), F32), ((1, 256), jnp.int32)]


def near_call(*args):
    out = [
        jax.ShapeDtypeStruct((4, 2, 256, 256), F32),
        jax.ShapeDtypeStruct((1024, 256), BF),
        jax.ShapeDtypeStruct((8, 128), F32),
    ]
    scratch = [
        ((32, 2, 32, 256), BF), ((256, 2048), BF), ((2048, 256), BF), ((8, 256, 32), BF),
        ((4, 2, 256, 256), F32), ((1024, 256), BF), ((8, 128), F32),
    ] + QKV_SCRATCH
    return call(near_kernel, "near", 1, args, out, scratch, 16, 20 * 10**9, space=pltpu.HBM)


def far_kernel(
    sc, sel, plen, own, oth, lo_own, lo_oth, hi_own, hi_oth, sec_i, acc_i, q_i, most_i, qkvm, qkvo,
    qbm, qbo, prw, prb, n2g, f1m, f1o, b1m, b1o, f2m, f2o, f2b, send, NE, KT, V, Q8, ACC, OUT, M,
    SEC, AI, QI, MI, PW, VEC, F1, B1, F2, QW, QB, PL, sems,
):
    g, base, total = sc[0], sc[1], sc[2]
    pw_a, pw_b = turned(prw, g)
    started = copies(
        sems,
        [
            (lo_own, NE.at[0:16, g]), (lo_oth, NE.at[0:16, 1 - g]), (hi_own, NE.at[48:64, g]),
            (hi_oth, NE.at[48:64, 1 - g]), (qkvm, QW.at[0]), (qkvo, QW.at[1]), (qbm, QB.at[0]),
            (qbo, QB.at[1]), (plen, PL), (most_i, MI), (q_i, QI), (acc_i, AI), (sec_i, SEC),
            (pw_a, PW.at[0:128]), (pw_b, PW.at[128:256]), (prb, VEC.at[0]), (n2g, VEC.at[1]),
            (f2b, VEC.at[2]), (f1m, F1.at[0]), (f1o, F1.at[1]), (b1m, B1.at[0]), (b1o, B1.at[1]),
            (f2m, F2.at[0]), (f2o, F2.at[1]),
        ],
    )
    wait(started[:11])
    block = key_values(NE, KT, V, QW, QB)
    starts_row, ends_row = patch_rows(PL[...])
    edge_lo = limits(0, g, base, total, starts_row, ends_row)[2]
    edge_hi = limits(3, g, base, total, starts_row, ends_row)[3]
    most = lax.fori_loop(jnp.minimum(edge_lo // 2, 4), 4, block, jnp.zeros((8, 256), F32))
    most = lax.fori_loop(12, jnp.maximum((edge_hi + 1) // 2, 12), block, most)
    key_most = jnp.maximum(jnp.max(most), jnp.max(MI[...]))
    mask, scores, step = pair_tools()
    hs = lax.broadcasted_iota(jnp.int32, (256, 128), 0) // 16
    hl = lax.broadcasted_iota(jnp.int32, (256, 128), 1)
    head_sel = jnp.where(hs == hl, 1.0, 0.0).astype(BF)
    def q_most(r0):
        q = QI[pl.ds(r0, 256), :]
        return jnp.max(jnp.dot(q * q, head_sel, preferred_element_type=F32))

    bound = q_most(0)
    for i in range(1, 4):
        bound = jnp.maximum(bound, q_most(256 * i))
    calm = bound * key_most * 1.05 <= 1e4

    @pl.when(jnp.logical_not(calm))
    def _():
        wait(copies(sems.at[24:26], [(own, NE.at[16:48, g]), (oth, NE.at[16:48, 1 - g])]))
        lax.fori_loop(4, 12, block, jnp.zeros((8, 256), F32))

    wait(started[11:])

    def q_block(qb, _):
        r0 = pl.multiple_of(qb * 256, 256)
        q = QI[pl.ds(r0, 256), :]
        for p in range(8):
            Q8[p] = q[:, 32 * p : 32 * p + 32]
        first, finish, kb0, kb1 = limits(qb, g, base, total, starts_row, ends_row)

        def body(kb, _, M=None):
            k0 = pl.multiple_of(kb * 128, 128)
            for h, x in enumerate(step(kb, k0, Q8, KT, V, first, finish, M)):
                ACC[h] += x
            return 0

        @pl.when(calm)
        def _():
            ACC[...] = AI[qb]
            lax.fori_loop(kb0, jnp.minimum(kb1, 8), body, 0)
            lax.fori_loop(jnp.maximum(kb0, 24), kb1, body, 0)

        @pl.when(jnp.logical_not(calm))
        def _():
            ACC[...] = jnp.zeros_like(ACC)
            M[...] = jnp.full(M.shape, -jnp.inf, F32)

            def top(kb, _):
                kt = KT[:, pl.ds(pl.multiple_of(kb * 128, 128), 128)]
                madd = mask(kb, first, finish)
                for p in range(8):
                    M[p] = jnp.maximum(M[p], scores(Q8, p, kt, madd))
                return 0

            lax.fori_loop(kb0, kb1, top, 0)
            for p in range(8):
                for h in range(2):
                    part = M[p, :, 128 * h : 128 * h + 128]
                    M[p, :, 128 * h : 128 * h + 128] = jnp.broadcast_to(
                        jnp.max(part, axis=1, keepdims=True), (256, 128)
                    )
            lax.fori_loop(kb0, kb1, lambda kb, c: body(kb, c, M), 0)

        attn = jnp.concatenate(
            [ACC[h, :, 0:128] / ACC[h, :, 128:256] for h in range(2)], axis=1
        ).astype(BF)
        two = (
            SEC[pl.ds(r0, 256), :].astype(F32)
            + jnp.dot(attn, PW[...], preferred_element_type=F32)
            + VEC[0]
        ).astype(BF)
        wide = two.astype(F32)
        normed = layer_norm(wide, VEC[1]).astype(BF)
        total_rows = wide + VEC[2]
        for h in range(2):
            x = jnp.dot(normed, F1[h], preferred_element_type=F32) + B1[h]
            x = (0.5 * x * (1.0 + lax.erf(x * 0.7071067811865476))).astype(BF)
            total_rows = total_rows + jnp.dot(x, F2[h], preferred_element_type=F32)
        OUT[pl.ds(r0, 256), :] = total_rows.astype(BF)
        return 0

    lax.fori_loop(0, 4, q_block, 0)

    def place(d, _):
        send[pl.ds(pl.multiple_of(32 * d, 32), 32), :] = OUT[
            pl.ds(pl.multiple_of(32 * sel[d, 0, 0], 32), 32), :
        ]
        return 0

    lax.fori_loop(0, 64, place, 0, unroll=4)


def far_call(*args):
    scratch = [
        ((64, 2, 32, 256), BF), ((256, 4096), BF), ((4096, 256), BF), ((8, 256, 32), BF),
        ((2, 256, 256), F32), ((1024, 256), BF), ((8, 256, 256), F32), ((1024, 256), BF),
        ((4, 2, 256, 256), F32), ((1024, 256), BF), ((8, 128), F32), ((256, 256), BF),
        ((3, 1, 256), F32), ((2, 256, 512), BF), ((2, 1, 512), F32), ((2, 512, 256), BF),
    ] + QKV_SCRATCH
    out = [jax.ShapeDtypeStruct((2048, 256), BF)]
    return call(far_kernel, "far", 2, args, out, scratch, 26, 20 * 10**9)[0]


def last_kernel(sc, zs, zv, own, oth, out):
    g = sc[0]
    place = zv[0:1, 0:64] % 64
    place = place % 32 + jnp.where(place // 32 == g, 0, 32)
    place = jnp.where(lax.broadcasted_iota(jnp.int32, (64, 64), 0) == place, 1.0, 0.0)
    perm = jnp.transpose(place).astype(BF)

    def step(k, _):
        source = lax.shift_right_logical(zs[64 * k], 11)
        rows = jnp.concatenate([own[source], oth[source]], axis=0)
        out[pl.ds(pl.multiple_of(64 * k, 64), 64), :] = jnp.dot(
            perm, rows, preferred_element_type=F32
        ).astype(BF)
        return 0

    lax.fori_loop(0, 32, step, 0, unroll=8)


def last_call(*args):
    smem, vmem = pl.BlockSpec(memory_space=pltpu.SMEM), pl.BlockSpec(memory_space=pltpu.VMEM)
    return pl.pallas_call(
        last_kernel,
        out_shape=jax.ShapeDtypeStruct((2048, 256), BF),
        in_specs=[smem] * 2 + [vmem] * 3,
        out_specs=vmem,
        compiler_params=pltpu.CompilerParams(vmem_limit_bytes=16 * 2**20),
        name="relabel",
    )(*args)


def local(
    points, neighbours, patch_len, zorder, conv_w, conv_b, cpe_w, cpe_b, cpe_gain, norm1_gain,
    qkv_w, qkv_b, proj_w, proj_b, norm2_gain, fc1_w, fc1_b, fc2_w, fc2_b,
):
    g = lax.axis_index("grp").astype(jnp.int32)
    me = lax.axis_index("pts").astype(jnp.int32)
    peers = lax.axis_size("pts")
    rows = points.shape[0]
    forward = [(i, i + 1) for i in range(peers - 1)]
    backward = [(i + 1, i) for i in range(peers - 1)]

    def swap(x):
        return lax.ppermute(x, "grp", [(0, 1), (1, 0)])

    def pieces(x):
        return x.reshape(-1, 32, 256)

    order = zorder.reshape(16, 128)
    low = lax.ppermute(points[rows - 256 :], "pts", forward)
    high = lax.ppermute(points[:256], "pts", backward)
    conv_m = conv_w.reshape(27 * 256, 128)
    conv_o, bias_o = swap(conv_m), swap(conv_b)
    sources = jnp.arange(peers, dtype=jnp.int32)[:, None]
    run = zorder[::64][None, :]
    wanted = jnp.max(jnp.where(run // rows == sources, run % rows // 64, 0), axis=1)
    wanted = jnp.broadcast_to(wanted[:, None, None], (peers, 1, 128))
    wanted, bias_o = lax.optimization_barrier((wanted, bias_o))
    sel = lax.all_to_all(wanted, "pts", split_axis=0, concat_axis=0, tiled=True)
    scalars = jnp.stack([g, me * rows, jnp.int32(rows * peers)])
    section_one, normed, lo_half, hi_half = conv_call(
        scalars, points, low, high, neighbours.T, conv_m, conv_o, conv_b[None], bias_o[None],
        cpe_w, cpe_b[None], cpe_gain[None], norm1_gain[None],
    )
    sel, normed, lo_half, hi_half = lax.optimization_barrier((sel, normed, lo_half, hi_half))
    qkv_m = jnp.transpose(qkv_w, (1, 0, 2))
    weights = (qkv_m, swap(qkv_m), qkv_b, swap(qkv_b))
    fc1_o, fc2_o, b1_o = swap(fc1_w), swap(fc2_w), swap(fc1_b)
    other, b1_o = lax.optimization_barrier((swap(normed), b1_o))
    lo_own = lax.ppermute(lo_half, "pts", forward)
    hi_own = lax.ppermute(hi_half, "pts", backward)
    acc, query, most = near_call(scalars, patch_len[None], pieces(normed), pieces(other), *weights)
    lo_own, hi_own, most = lax.optimization_barrier((lo_own, hi_own, most))
    lo_oth, hi_oth = swap(lo_own), swap(hi_own)
    send = far_call(
        scalars, sel, patch_len[None], pieces(normed), pieces(other), pieces(lo_own),
        pieces(lo_oth), pieces(hi_own), pieces(hi_oth), section_one, acc, query, most, *weights,
        proj_w, proj_b[None], norm2_gain[None], fc1_w, fc1_o, fc1_b[None], b1_o[None], fc2_w,
        fc2_o, fc2_b[None],
    )
    got = lax.all_to_all(send, "pts", split_axis=0, concat_axis=0, tiled=True)
    return last_call(scalars, zorder, order, pieces(got), pieces(swap(got)))


def solution(mesh):
    placed = (
        P("pts", None), P("pts", None), P(), P("pts"), P(None, None, "grp"), P("grp"), P(), P(), P(),
        P(), P(None, None, "grp"), P(None, "grp"), P(), P(), P(), P(None, "grp"), P("grp"),
        P("grp", None), P(),
    )
    return jax.shard_map(
        local, mesh=mesh, in_specs=placed, out_specs=P("pts", None), check_vma=False
    )
```

```python
import jax
import jax.numpy as jnp
from jax import lax
from jax.experimental import pallas as pl
from jax.experimental.pallas import tpu as pltpu
from jax.sharding import PartitionSpec as P

F32=jnp.float32; BF=jnp.bfloat16

VMEM_BYTES = 64 * 2**20 - 65536
Q_SCALE = 0.25 * 1.4426950408889634


def layer_norm(v, gain):
    c = v - jnp.mean(v, axis=-1, keepdims=True)
    s = jnp.mean(c * c, axis=-1, keepdims=True)
    return c * lax.rsqrt(s + 1e-05) * gain

RB = 128
TAPS = [t for t in range(27) if t != 13]


def copies(sems, pairs):
    out = [pltpu.make_async_copy(src, dst, sems.at[i]) for i, (src, dst) in enumerate(pairs)]
    for copy in out:
        copy.start()
    return out


def wait(some):
    for copy in some:
        copy.wait()


def turned(ref, g):
    first = ref.at[pl.ds(pl.multiple_of(128 * g, 128), 128)]
    return first, ref.at[pl.ds(pl.multiple_of(128 - 128 * g, 128), 128)]


def conv_kernel(
    sc, pts, low, high, nbs, wm, wo, cbm, cbo, cpw, cpb, cpg, n1g, sec_o, nrm_o, lo_o, hi_o,
    X, NT, NB, OH, G, W, CW, CB, CV, sems,
):
    g = sc[0]
    base = sc[1]
    cw_a, cw_b = turned(cpw, g)
    started = copies(
        sems,
        [
            (nbs, NT), (pts, X.at[256:2304]), (low, X.at[0:256]), (high, X.at[2304:2560]),
            (wm, W.at[:, 0:128]), (wo, W.at[:, 128:256]), (cw_a, CW.at[0:128]),
            (cw_b, CW.at[128:256]), (cbm, CB.at[:, 0:128]), (cbo, CB.at[:, 128:256]),
            (cpb, CV.at[0]), (cpg, CV.at[1]), (n1g, CV.at[2]),
        ],
    )
    wait(started[:1])
    lanes = lax.broadcasted_iota(jnp.int32, (RB, 768), 1)
    for b in range(8):
        NB[256 * b : 256 * b + 256, :] = jnp.transpose(NT[:, 256 * b : 256 * b + 256])

    def block(b, OH):
        rel = []
        for j in range(RB // 32):
            rel.append(NB[pl.ds(pl.multiple_of(256 * b + 64 * j + 32 * g, 32), 32), :])
        rel = jnp.concatenate(rel, axis=0)
        rel = jnp.where(rel < 0, -1, rel - (base + 256 * b - 256))
        for i, t in enumerate(TAPS):
            col = rel[:, t : t + 1]
            OH[i * RB : (i + 1) * RB, :] = jnp.where(
                lanes == col, jnp.array(1, BF), jnp.array(0, BF)
            )
        win = X[pl.ds(256 * b, 768), :]
        to = pl.ds(b * RB, RB)
        out = jnp.dot(OH[...], win, preferred_element_type=F32).astype(BF)
        for i, t in enumerate(TAPS):
            G[to, t * 256 : (t + 1) * 256] = out[i * RB : (i + 1) * RB, :]
        for j in range(RB // 32):
            G[pl.ds(b * RB + 32 * j, 32), 13 * 256 : 14 * 256] = X[
                pl.ds(pl.multiple_of(256 + 256 * b + 64 * j + 32 * g, 32), 32), :
            ]

    wait(started[1:4])
    for b in range(1024 // RB):
        block(b, OH.at[b % 2])
    wait(started[4:])

    def finish(m, _):
        r0 = pl.multiple_of(m * 512, 512)
        at = pl.ds(r0, 512)
        acc = jnp.dot(G[at, :], W[...], preferred_element_type=F32)
        conv = (acc + CB[...]).astype(BF)
        c = jnp.dot(conv, CW[...], preferred_element_type=F32) + CV[0]
        own = G[at, 13 * 256 : 14 * 256].astype(F32)
        sec = (own + layer_norm(c, CV[1])).astype(BF)
        sec_o[at, :] = sec
        normed = layer_norm(sec.astype(F32), CV[2]).astype(BF)
        nrm_o[at, :] = normed

        @pl.when(m == 0)
        def _():
            hi_o[...] = normed

        @pl.when(m == 1)
        def _():
            lo_o[...] = normed

        return 0

    lax.fori_loop(0, 2, finish, 0)


def call(kernel, name, smem, args, out_shape, scratch, sems, flops, space=pltpu.VMEM):
    return pl.pallas_call(
        kernel,
        out_shape=out_shape,
        in_specs=[pl.BlockSpec(memory_space=pltpu.SMEM)] * smem
        + [pl.BlockSpec(memory_space=pltpu.HBM)] * (len(args) - smem),
        out_specs=[pl.BlockSpec(memory_space=space)] * len(out_shape),
        scratch_shapes=[pltpu.VMEM(*x) for x in scratch] + [pltpu.SemaphoreType.DMA((sems,))],
        compiler_params=pltpu.CompilerParams(vmem_limit_bytes=VMEM_BYTES),
        cost_estimate=pl.CostEstimate(flops=flops, bytes_accessed=8 * 10**6, transcendentals=0),
        name=name,
    )(*args)


def conv_call(*args):
    out = [jax.ShapeDtypeStruct((n, 256), BF) for n in (1024, 1024, 512, 512)]
    scratch = [
        ((2560, 256), BF), ((27, 2048), jnp.int32), ((2048, 27), jnp.int32), ((2, 26 * RB, 768), BF), ((1024, 6912), BF),
        ((6912, 256), BF), ((256, 256), BF), ((1, 256), F32), ((3, 1, 256), F32),
    ]
    return call(conv_kernel, "conv", 1, args, out, scratch, 13, 30 * 10**9)


def key_values(NE, KT, V, QW, QB):
    wkt = [jnp.transpose(QW[h, 1]) for h in range(2)]
    bkc = [jnp.transpose(jnp.broadcast_to(QB[h, 1:2, :], (8, 128)))[:, :1] for h in range(2)]
    wv = jnp.concatenate([QW[0, 2], QW[1, 2]], axis=1)
    bv = jnp.concatenate([QB[0, 2:3, :], QB[1, 2:3, :]], axis=1)

    def block(i, most):
        r0 = pl.multiple_of(i * 256, 256)
        rows = NE[pl.ds(4 * i, 4)].reshape(256, 256)
        for h in range(2):
            kt = (
                lax.dot_general(
                    wkt[h], rows, (((1,), (1,)), ((), ())), preferred_element_type=F32
                )
                + bkc[h]
            )
            most = jnp.maximum(most, jnp.sum((kt * kt).reshape(8, 16, 256), axis=1))
            KT[128 * h : 128 * h + 128, pl.ds(r0, 256)] = kt.astype(BF)
        V[pl.ds(r0, 256), :] = (jnp.dot(rows, wv, preferred_element_type=F32) + bv).astype(BF)
        return most

    return block


def patch_rows(plen):
    lens = jnp.broadcast_to(plen.astype(F32), (256, 256))
    sub = lax.broadcasted_iota(jnp.int32, (256, 256), 0)
    lane = lax.broadcasted_iota(jnp.int32, (256, 256), 1)
    ends_col = jnp.sum(jnp.where(lane <= sub, lens, 0.0), axis=1, keepdims=True)
    ends_row = jnp.sum(jnp.where(lane == sub, ends_col, 0.0), axis=0, keepdims=True)
    return ends_row - plen.astype(F32), ends_row


def limits(qb, g, base, total, starts_row, ends_row):
    r = lax.broadcasted_iota(jnp.int32, (256, 1), 0)
    row = (base + 512 * qb + 64 * (r // 32) + 32 * g + r % 32).astype(F32)
    first = jnp.max(jnp.where(starts_row <= row, starts_row, 0.0), axis=1, keepdims=True)
    finish = jnp.min(jnp.where(ends_row > row, ends_row, total.astype(F32)), axis=1, keepdims=True)
    shift = (1024 - base).astype(F32)
    first = (first + shift).astype(jnp.int32)
    finish = (finish + shift).astype(jnp.int32)
    kb0 = jnp.maximum(jnp.min(first) // 128, 0)
    kb1 = jnp.minimum((jnp.max(finish) + 127) // 128, 32)
    return first, finish, kb0, kb1


def queries(rows, QW, QB):
    wq = jnp.concatenate([QW[0, 0], QW[1, 0]], axis=1)
    bq = jnp.concatenate([QB[0, 0:1, :], QB[1, 0:1, :]], axis=1)
    return ((jnp.dot(rows, wq, preferred_element_type=F32) + bq) * Q_SCALE).astype(BF)


def pair_tools():
    half = lax.broadcasted_iota(jnp.int32, (32, 128), 0) < 16
    k_low = jnp.where(half, 1.0, 0.0).astype(BF)
    k_high = jnp.where(half, 0.0, 1.0).astype(BF)
    col_head = lax.broadcasted_iota(jnp.int32, (128, 128), 1) // 16
    cols = [jnp.where(col_head == a, 1.0, 0.0).astype(BF) for a in range(8)]

    def mask(kb, first, finish):
        key = kb * 128 + lax.broadcasted_iota(jnp.int32, (256, 128), 1)
        madd = jnp.where((key >= first) & (key < finish), 0.0, -jnp.inf)
        return jnp.concatenate([madd, madd], axis=1)

    def scores(Q8, p, kt, madd):
        part = kt[32 * p : 32 * p + 32, :]
        pair = jnp.concatenate([part * k_low, part * k_high], axis=1)
        return jnp.dot(Q8[p], pair, preferred_element_type=F32) + madd

    def step(kb, k0, Q8, KT, V, first, finish, M=None):
        kt = KT[:, pl.ds(k0, 128)]
        vb = V[pl.ds(k0, 128), :]
        madd = mask(kb, first, finish)
        out = []
        for h in range(2):
            vh = vb[:, 128 * h : 128 * h + 128]
            ps, vs = [], []
            for a in range(4):
                p = 4 * h + a
                s = scores(Q8, p, kt, madd)
                if M is not None:
                    s = s - M[p]
                ps.append(jnp.exp2(s).astype(BF))
                for c in (cols[2 * a], cols[2 * a + 1]):
                    vs.append(jnp.concatenate([vh * c, c], axis=1))
            out.append(
                jnp.dot(
                    jnp.concatenate(ps, axis=1),
                    jnp.concatenate(vs, axis=0),
                    preferred_element_type=F32,
                )
            )
        return out

    return mask, scores, step


def near_kernel(
    sc, plen, own, oth, qkvm, qkvo, qbm, qbo, acc_h, q_h, most_h, NE, KT, V, Q8, acc_o, q_o,
    most_o, QW, QB, PL, sems,
):
    g, base, total = sc[0], sc[1], sc[2]
    started = copies(
        sems,
        [
            (plen, PL), (own, NE.at[:, g]), (oth, NE.at[:, 1 - g]), (qkvm, QW.at[0]),
            (qkvo, QW.at[1]), (qbm, QB.at[0]), (qbo, QB.at[1]),
        ],
    )
    wait(started[:1])
    starts_row, ends_row = patch_rows(PL[...])
    wait(started[1:])
    block = key_values(NE, KT, V, QW, QB)
    most = lax.fori_loop(0, 8, block, jnp.zeros((8, 256), F32))
    most_o[...] = jnp.broadcast_to(jnp.max(most), (8, 128))
    leave = pltpu.make_async_copy(most_o, most_h, sems.at[7])
    leave.start()

    def results(qb):
        at = pl.ds(pl.multiple_of(256 * qb, 256), 256)
        return (
            pltpu.make_async_copy(acc_o.at[qb], acc_h.at[qb], sems.at[8 + qb]),
            pltpu.make_async_copy(q_o.at[at], q_h.at[at], sems.at[12 + qb]),
        )

    mask, scores, step = pair_tools()

    def q_block(qb, _):
        r0 = pl.multiple_of(qb * 256, 256)
        q = queries(NE[pl.ds(8 * qb, 8), g].reshape(256, 256), QW, QB)
        q_o[pl.ds(r0, 256), :] = q
        for p in range(8):
            Q8[p] = q[:, 32 * p : 32 * p + 32]
        first, finish, kb0, kb1 = limits(qb, g, base, total, starts_row, ends_row)
        acc_o[qb] = jnp.zeros((2, 256, 256), F32)

        def body(kb, _):
            k0 = pl.multiple_of((kb - 8) * 128, 128)
            for h, x in enumerate(step(kb, k0, Q8, KT, V, first, finish)):
                acc_o[qb, h] += x
            return 0

        lax.fori_loop(jnp.maximum(kb0, 8), jnp.minimum(kb1, 24), body, 0)
        for copy in results(qb):
            copy.start()
        return 0

    lax.fori_loop(0, 4, q_block, 0)
    leave.wait()
    for qb in range(4):
        wait(results(qb))


QKV_SCRATCH = [((2, 3, 256, 128), BF), ((2, 3, 128), F32), ((1, 256), jnp.int32)]


def near_call(*args):
    out = [
        jax.ShapeDtypeStruct((4, 2, 256, 256), F32),
        jax.ShapeDtypeStruct((1024, 256), BF),
        jax.ShapeDtypeStruct((8, 128), F32),
    ]
    scratch = [
        ((32, 2, 32, 256), BF), ((256, 2048), BF), ((2048, 256), BF), ((8, 256, 32), BF),
        ((4, 2, 256, 256), F32), ((1024, 256), BF), ((8, 128), F32),
    ] + QKV_SCRATCH
    return call(near_kernel, "near", 1, args, out, scratch, 16, 20 * 10**9, space=pltpu.HBM)


def far_kernel(
    sc, sel, plen, own, oth, lo_own, lo_oth, hi_own, hi_oth, sec_i, acc_i, q_i, most_i, qkvm, qkvo,
    qbm, qbo, prw, prb, n2g, f1m, f1o, b1m, b1o, f2m, f2o, f2b, send, NE, KT, V, Q8, ACC, OUT, M,
    SEC, AI, QI, MI, PW, VEC, F1, B1, F2, QW, QB, PL, sems,
):
    g, base, total = sc[0], sc[1], sc[2]
    pw_a, pw_b = turned(prw, g)
    started = copies(
        sems,
        [
            (lo_own, NE.at[0:16, g]), (lo_oth, NE.at[0:16, 1 - g]), (hi_own, NE.at[48:64, g]),
            (hi_oth, NE.at[48:64, 1 - g]), (qkvm, QW.at[0]), (qkvo, QW.at[1]), (qbm, QB.at[0]),
            (qbo, QB.at[1]), (plen, PL), (most_i, MI), (q_i, QI), (acc_i, AI), (sec_i, SEC),
            (pw_a, PW.at[0:128]), (pw_b, PW.at[128:256]), (prb, VEC.at[0]), (n2g, VEC.at[1]),
            (f2b, VEC.at[2]), (f1m, F1.at[0]), (f1o, F1.at[1]), (b1m, B1.at[0]), (b1o, B1.at[1]),
            (f2m, F2.at[0]), (f2o, F2.at[1]),
        ],
    )
    wait(started[8:9])
    starts_row, ends_row = patch_rows(PL[...])
    edge_lo = limits(0, g, base, total, starts_row, ends_row)[2]
    edge_hi = limits(3, g, base, total, starts_row, ends_row)[3]
    wait(started[:8] + started[9:11])
    block = key_values(NE, KT, V, QW, QB)
    most = lax.fori_loop(jnp.minimum(edge_lo // 2, 4), 4, block, jnp.zeros((8, 256), F32))
    most = lax.fori_loop(12, jnp.maximum((edge_hi + 1) // 2, 12), block, most)
    key_most = jnp.maximum(jnp.max(most), jnp.max(MI[...]))
    mask, scores, step = pair_tools()
    hs = lax.broadcasted_iota(jnp.int32, (256, 128), 0) // 16
    hl = lax.broadcasted_iota(jnp.int32, (256, 128), 1)
    head_sel = jnp.where(hs == hl, 1.0, 0.0).astype(BF)
    def q_most(r0):
        q = QI[pl.ds(r0, 256), :]
        return jnp.max(jnp.dot(q * q, head_sel, preferred_element_type=F32))

    bound = q_most(0)
    for i in range(1, 4):
        bound = jnp.maximum(bound, q_most(256 * i))
    calm = bound * key_most * 1.05 <= 1e4

    @pl.when(jnp.logical_not(calm))
    def _():
        wait(copies(sems.at[24:26], [(own, NE.at[16:48, g]), (oth, NE.at[16:48, 1 - g])]))
        lax.fori_loop(4, 12, block, jnp.zeros((8, 256), F32))

    wait(started[11:])

    def q_block(qb, _):
        r0 = pl.multiple_of(qb * 256, 256)
        q = QI[pl.ds(r0, 256), :]
        for p in range(8):
            Q8[p] = q[:, 32 * p : 32 * p + 32]
        first, finish, kb0, kb1 = limits(qb, g, base, total, starts_row, ends_row)

        def body(kb, _, M=None):
            k0 = pl.multiple_of(kb * 128, 128)
            for h, x in enumerate(step(kb, k0, Q8, KT, V, first, finish, M)):
                ACC[h] += x
            return 0

        @pl.when(calm)
        def _():
            ACC[...] = AI[qb]
            lax.fori_loop(kb0, jnp.minimum(kb1, 8), body, 0)
            lax.fori_loop(jnp.maximum(kb0, 24), kb1, body, 0)

        @pl.when(jnp.logical_not(calm))
        def _():
            ACC[...] = jnp.zeros_like(ACC)
            M[...] = jnp.full(M.shape, -jnp.inf, F32)

            def top(kb, _):
                kt = KT[:, pl.ds(pl.multiple_of(kb * 128, 128), 128)]
                madd = mask(kb, first, finish)
                for p in range(8):
                    M[p] = jnp.maximum(M[p], scores(Q8, p, kt, madd))
                return 0

            lax.fori_loop(kb0, kb1, top, 0)
            for p in range(8):
                for h in range(2):
                    part = M[p, :, 128 * h : 128 * h + 128]
                    M[p, :, 128 * h : 128 * h + 128] = jnp.broadcast_to(
                        jnp.max(part, axis=1, keepdims=True), (256, 128)
                    )
            lax.fori_loop(kb0, kb1, lambda kb, c: body(kb, c, M), 0)

        attn = jnp.concatenate(
            [ACC[h, :, 0:128] / ACC[h, :, 128:256] for h in range(2)], axis=1
        ).astype(BF)
        two = (
            SEC[pl.ds(r0, 256), :].astype(F32)
            + jnp.dot(attn, PW[...], preferred_element_type=F32)
            + VEC[0]
        ).astype(BF)
        wide = two.astype(F32)
        normed = layer_norm(wide, VEC[1]).astype(BF)
        total_rows = wide + VEC[2]
        for h in range(2):
            x = jnp.dot(normed, F1[h], preferred_element_type=F32) + B1[h]
            x = (0.5 * x * (1.0 + lax.erf(x * 0.7071067811865476))).astype(BF)
            total_rows = total_rows + jnp.dot(x, F2[h], preferred_element_type=F32)
        OUT[pl.ds(r0, 256), :] = total_rows.astype(BF)
        return 0

    lax.fori_loop(0, 4, q_block, 0)

    def place(d, _):
        send[pl.ds(pl.multiple_of(32 * d, 32), 32), :] = OUT[
            pl.ds(pl.multiple_of(32 * sel[d, 0, 0], 32), 32), :
        ]
        return 0

    lax.fori_loop(0, 64, place, 0, unroll=4)


def far_call(*args):
    scratch = [
        ((64, 2, 32, 256), BF), ((256, 4096), BF), ((4096, 256), BF), ((8, 256, 32), BF),
        ((2, 256, 256), F32), ((1024, 256), BF), ((8, 256, 256), F32), ((1024, 256), BF),
        ((4, 2, 256, 256), F32), ((1024, 256), BF), ((8, 128), F32), ((256, 256), BF),
        ((3, 1, 256), F32), ((2, 256, 512), BF), ((2, 1, 512), F32), ((2, 512, 256), BF),
    ] + QKV_SCRATCH
    out = [jax.ShapeDtypeStruct((2048, 256), BF)]
    return call(far_kernel, "far", 2, args, out, scratch, 26, 20 * 10**9)[0]


def last_kernel(sc, zs, zv, own, oth, out):
    g = sc[0]
    place = zv[0:1, 0:64] % 64
    place = place % 32 + jnp.where(place // 32 == g, 0, 32)
    place = jnp.where(lax.broadcasted_iota(jnp.int32, (64, 64), 0) == place, 1.0, 0.0)
    perm = jnp.transpose(place).astype(BF)

    def step(k, _):
        source = lax.shift_right_logical(zs[64 * k], 11)
        rows = jnp.concatenate([own[source], oth[source]], axis=0)
        out[pl.ds(pl.multiple_of(64 * k, 64), 64), :] = jnp.dot(
            perm, rows, preferred_element_type=F32
        ).astype(BF)
        return 0

    lax.fori_loop(0, 32, step, 0, unroll=8)


def last_call(*args):
    smem, vmem = pl.BlockSpec(memory_space=pltpu.SMEM), pl.BlockSpec(memory_space=pltpu.VMEM)
    return pl.pallas_call(
        last_kernel,
        out_shape=jax.ShapeDtypeStruct((2048, 256), BF),
        in_specs=[smem] * 2 + [vmem] * 3,
        out_specs=vmem,
        compiler_params=pltpu.CompilerParams(vmem_limit_bytes=16 * 2**20),
        name="relabel",
    )(*args)


def local(
    points, neighbours, patch_len, zorder, conv_w, conv_b, cpe_w, cpe_b, cpe_gain, norm1_gain,
    qkv_w, qkv_b, proj_w, proj_b, norm2_gain, fc1_w, fc1_b, fc2_w, fc2_b,
):
    g = lax.axis_index("grp").astype(jnp.int32)
    me = lax.axis_index("pts").astype(jnp.int32)
    peers = lax.axis_size("pts")
    rows = points.shape[0]
    forward = [(i, i + 1) for i in range(peers - 1)]
    backward = [(i + 1, i) for i in range(peers - 1)]

    def swap(x):
        return lax.ppermute(x, "grp", [(0, 1), (1, 0)])

    def pieces(x):
        return x.reshape(-1, 32, 256)

    order = zorder.reshape(16, 128)
    low = lax.ppermute(points[rows - 256 :], "pts", forward)
    high = lax.ppermute(points[:256], "pts", backward)
    conv_m = conv_w.reshape(27 * 256, 128)
    conv_o, bias_o = swap(conv_m), swap(conv_b)
    sources = jnp.arange(peers, dtype=jnp.int32)[:, None]
    run = zorder[::64][None, :]
    wanted = jnp.max(jnp.where(run // rows == sources, run % rows // 64, 0), axis=1)
    wanted = jnp.broadcast_to(wanted[:, None, None], (peers, 1, 128))
    wanted, bias_o = lax.optimization_barrier((wanted, bias_o))
    sel = lax.all_to_all(wanted, "pts", split_axis=0, concat_axis=0, tiled=True)
    qkv_m = jnp.transpose(qkv_w, (1, 0, 2))
    conv_o, *others = lax.optimization_barrier(
        (conv_o, swap(qkv_m), swap(qkv_b), swap(fc1_w), swap(fc2_w), swap(fc1_b))
    )
    qkv_o, qb_o, fc1_o, fc2_o, b1_o = others
    weights = (qkv_m, qkv_o, qkv_b, qb_o)
    scalars = jnp.stack([g, me * rows, jnp.int32(rows * peers)])
    section_one, normed, lo_half, hi_half = conv_call(
        scalars, points, low, high, neighbours.T, conv_m, conv_o, conv_b[None], bias_o[None],
        cpe_w, cpe_b[None], cpe_gain[None], norm1_gain[None],
    )
    sel, normed, lo_half, hi_half = lax.optimization_barrier((sel, normed, lo_half, hi_half))
    other = swap(normed)
    lo_own = lax.ppermute(lo_half, "pts", forward)
    hi_own = lax.ppermute(hi_half, "pts", backward)
    acc, query, most = near_call(scalars, patch_len[None], pieces(normed), pieces(other), *weights)
    lo_own, hi_own, most = lax.optimization_barrier((lo_own, hi_own, most))
    lo_oth, hi_oth = swap(lo_own), swap(hi_own)
    send = far_call(
        scalars, sel, patch_len[None], pieces(normed), pieces(other), pieces(lo_own),
        pieces(lo_oth), pieces(hi_own), pieces(hi_oth), section_one, acc, query, most, *weights,
        proj_w, proj_b[None], norm2_gain[None], fc1_w, fc1_o, fc1_b[None], b1_o[None], fc2_w,
        fc2_o, fc2_b[None],
    )
    got = lax.all_to_all(send, "pts", split_axis=0, concat_axis=0, tiled=True)
    return last_call(scalars, zorder, order, pieces(got), pieces(swap(got)))


def solution(mesh):
    placed = (
        P("pts", None), P("pts", None), P(), P("pts"), P(None, None, "grp"), P("grp"), P(), P(), P(),
        P(), P(None, None, "grp"), P(None, "grp"), P(), P(), P(), P(None, "grp"), P("grp"),
        P("grp", None), P(),
    )
    return jax.shard_map(
        local, mesh=mesh, in_specs=placed, out_specs=P("pts", None), check_vma=False
    )
```

```python
import jax
import jax.numpy as jnp
from jax import lax
from jax.experimental import pallas as pl
from jax.experimental.pallas import tpu as pltpu
from jax.sharding import PartitionSpec as P

F32=jnp.float32; BF=jnp.bfloat16

VMEM_BYTES = 64 * 2**20 - 65536
Q_SCALE = 0.25 * 1.4426950408889634


def layer_norm(v, gain):
    c = v - jnp.mean(v, axis=-1, keepdims=True)
    s = jnp.mean(c * c, axis=-1, keepdims=True)
    return c * lax.rsqrt(s + 1e-05) * gain

RB = 128
TAPS = [t for t in range(27) if t != 13]


def copies(sems, pairs):
    out = [pltpu.make_async_copy(src, dst, sems.at[i]) for i, (src, dst) in enumerate(pairs)]
    for copy in out:
        copy.start()
    return out


def wait(some):
    for copy in some:
        copy.wait()


def turned(ref, g):
    first = ref.at[pl.ds(pl.multiple_of(128 * g, 128), 128)]
    return first, ref.at[pl.ds(pl.multiple_of(128 - 128 * g, 128), 128)]


def conv_kernel(
    sc, pts, low, high, nbs, wm, wo, cbm, cbo, cpw, cpb, cpg, n1g, sec_o, nrm_o, lo_o, hi_o,
    X, NT, NB, OH, G, W, CW, CB, CV, sems,
):
    g = sc[0]
    base = sc[1]
    cw_a, cw_b = turned(cpw, g)
    started = copies(
        sems,
        [
            (nbs, NT), (pts, X.at[256:2304]), (low, X.at[0:256]), (high, X.at[2304:2560]),
            (wm, W.at[:, 0:128]), (wo, W.at[:, 128:256]), (cw_a, CW.at[0:128]),
            (cw_b, CW.at[128:256]), (cbm, CB.at[:, 0:128]), (cbo, CB.at[:, 128:256]),
            (cpb, CV.at[0]), (cpg, CV.at[1]), (n1g, CV.at[2]),
        ],
    )
    wait(started[:1])
    lanes = lax.broadcasted_iota(jnp.int32, (RB, 768), 1)
    for b in range(8):
        NB[256 * b : 256 * b + 256, :] = jnp.transpose(NT[:, 256 * b : 256 * b + 256])

    def block(b, OH):
        rel = []
        for j in range(RB // 32):
            rel.append(NB[pl.ds(pl.multiple_of(256 * b + 64 * j + 32 * g, 32), 32), :])
        rel = jnp.concatenate(rel, axis=0)
        rel = jnp.where(rel < 0, -1, rel - (base + 256 * b - 256))
        for i, t in enumerate(TAPS):
            col = rel[:, t : t + 1]
            OH[i * RB : (i + 1) * RB, :] = jnp.where(
                lanes == col, jnp.array(1, BF), jnp.array(0, BF)
            )
        win = X[pl.ds(256 * b, 768), :]
        to = pl.ds(b * RB, RB)
        out = jnp.dot(OH[...], win, preferred_element_type=F32).astype(BF)
        for i, t in enumerate(TAPS):
            G[to, t * 256 : (t + 1) * 256] = out[i * RB : (i + 1) * RB, :]
        for j in range(RB // 32):
            G[pl.ds(b * RB + 32 * j, 32), 13 * 256 : 14 * 256] = X[
                pl.ds(pl.multiple_of(256 + 256 * b + 64 * j + 32 * g, 32), 32), :
            ]

    wait(started[1:4])
    for b in range(1024 // RB):
        block(b, OH.at[b % 2])
    wait(started[4:])

    def finish(m, _):
        r0 = pl.multiple_of(m * 512, 512)
        at = pl.ds(r0, 512)
        acc = jnp.dot(G[at, :], W[...], preferred_element_type=F32)
        conv = (acc + CB[...]).astype(BF)
        c = jnp.dot(conv, CW[...], preferred_element_type=F32) + CV[0]
        own = G[at, 13 * 256 : 14 * 256].astype(F32)
        sec = (own + layer_norm(c, CV[1])).astype(BF)
        sec_o[at, :] = sec
        normed = layer_norm(sec.astype(F32), CV[2]).astype(BF)
        nrm_o[at, :] = normed

        @pl.when(m == 0)
        def _():
            hi_o[...] = normed

        @pl.when(m == 1)
        def _():
            lo_o[...] = normed

        return 0

    lax.fori_loop(0, 2, finish, 0)


def call(kernel, name, smem, args, out_shape, scratch, sems, flops, space=pltpu.VMEM):
    return pl.pallas_call(
        kernel,
        out_shape=out_shape,
        in_specs=[pl.BlockSpec(memory_space=pltpu.SMEM)] * smem
        + [pl.BlockSpec(memory_space=pltpu.HBM)] * (len(args) - smem),
        out_specs=[pl.BlockSpec(memory_space=space)] * len(out_shape),
        scratch_shapes=[pltpu.VMEM(*x) for x in scratch] + [pltpu.SemaphoreType.DMA((sems,))],
        compiler_params=pltpu.CompilerParams(vmem_limit_bytes=VMEM_BYTES),
        cost_estimate=pl.CostEstimate(flops=flops, bytes_accessed=8 * 10**6, transcendentals=0),
        name=name,
    )(*args)


def conv_call(*args):
    out = [jax.ShapeDtypeStruct((n, 256), BF) for n in (1024, 1024, 512, 512)]
    scratch = [
        ((2560, 256), BF), ((27, 2048), jnp.int32), ((2048, 27), jnp.int32), ((2, 26 * RB, 768), BF), ((1024, 6912), BF),
        ((6912, 256), BF), ((256, 256), BF), ((1, 256), F32), ((3, 1, 256), F32),
    ]
    return call(conv_kernel, "conv", 1, args, out, scratch, 13, 30 * 10**9)


def key_values(NE, KT, V, QW, QB):
    wkt = jnp.concatenate([jnp.transpose(QW[h, 1]) for h in range(2)], axis=0)
    bkc = jnp.concatenate(
        [jnp.transpose(jnp.broadcast_to(QB[h, 1:2, :], (8, 128)))[:, :1] for h in range(2)], axis=0
    )
    wv = jnp.concatenate([QW[0, 2], QW[1, 2]], axis=1)
    bv = jnp.concatenate([QB[0, 2:3, :], QB[1, 2:3, :]], axis=1)

    def block(i, most):
        r0 = pl.multiple_of(i * 256, 256)
        rows = NE[pl.ds(4 * i, 4)].reshape(256, 256)
        kt = (
            lax.dot_general(wkt, rows, (((1,), (1,)), ((), ())), preferred_element_type=F32) + bkc
        )
        most = jnp.maximum(most, jnp.sum((kt * kt).reshape(16, 16, 256), axis=1))
        KT[:, pl.ds(r0, 256)] = kt.astype(BF)
        V[pl.ds(r0, 256), :] = (jnp.dot(rows, wv, preferred_element_type=F32) + bv).astype(BF)
        return most

    return block


def patch_rows(plen):
    lens = jnp.broadcast_to(plen.astype(F32), (256, 256))
    sub = lax.broadcasted_iota(jnp.int32, (256, 256), 0)
    lane = lax.broadcasted_iota(jnp.int32, (256, 256), 1)
    ends_col = jnp.sum(jnp.where(lane <= sub, lens, 0.0), axis=1, keepdims=True)
    ends_row = jnp.sum(jnp.where(lane == sub, ends_col, 0.0), axis=0, keepdims=True)
    return ends_row - plen.astype(F32), ends_row


def limits(qb, g, base, total, starts_row, ends_row):
    r = lax.broadcasted_iota(jnp.int32, (256, 1), 0)
    row = (base + 512 * qb + 64 * (r // 32) + 32 * g + r % 32).astype(F32)
    first = jnp.max(jnp.where(starts_row <= row, starts_row, 0.0), axis=1, keepdims=True)
    finish = jnp.min(jnp.where(ends_row > row, ends_row, total.astype(F32)), axis=1, keepdims=True)
    shift = (1024 - base).astype(F32)
    first = (first + shift).astype(jnp.int32)
    finish = (finish + shift).astype(jnp.int32)
    kb0 = jnp.maximum(jnp.min(first) // 128, 0)
    kb1 = jnp.minimum((jnp.max(finish) + 127) // 128, 32)
    return first, finish, kb0, kb1


def queries(rows, QW, QB):
    wq = jnp.concatenate([QW[0, 0], QW[1, 0]], axis=1)
    bq = jnp.concatenate([QB[0, 0:1, :], QB[1, 0:1, :]], axis=1)
    return ((jnp.dot(rows, wq, preferred_element_type=F32) + bq) * Q_SCALE).astype(BF)


def pair_tools():
    half = lax.broadcasted_iota(jnp.int32, (32, 128), 0) < 16
    k_low = jnp.where(half, 1.0, 0.0).astype(BF)
    k_high = jnp.where(half, 0.0, 1.0).astype(BF)
    col_head = lax.broadcasted_iota(jnp.int32, (128, 128), 1) // 16
    cols = [jnp.where(col_head == a, 1.0, 0.0).astype(BF) for a in range(8)]

    def mask(kb, first, finish):
        key = kb * 128 + lax.broadcasted_iota(jnp.int32, (256, 128), 1)
        madd = jnp.where((key >= first) & (key < finish), 0.0, -jnp.inf)
        return jnp.concatenate([madd, madd], axis=1)

    def scores(Q8, p, kt, madd):
        part = kt[32 * p : 32 * p + 32, :]
        pair = jnp.concatenate([part * k_low, part * k_high], axis=1)
        return jnp.dot(Q8[p], pair, preferred_element_type=F32) + madd

    def step(kb, k0, Q8, KT, V, first, finish, M=None):
        kt = KT[:, pl.ds(k0, 128)]
        vb = V[pl.ds(k0, 128), :]
        madd = mask(kb, first, finish)
        out = []
        for h in range(2):
            vh = vb[:, 128 * h : 128 * h + 128]
            ps, vs = [], []
            for a in range(4):
                p = 4 * h + a
                s = scores(Q8, p, kt, madd)
                if M is not None:
                    s = s - M[p]
                ps.append(jnp.exp2(s).astype(BF))
                for c in (cols[2 * a], cols[2 * a + 1]):
                    vs.append(jnp.concatenate([vh * c, c], axis=1))
            out.append(
                jnp.dot(
                    jnp.concatenate(ps, axis=1),
                    jnp.concatenate(vs, axis=0),
                    preferred_element_type=F32,
                )
            )
        return out

    return mask, scores, step


def near_kernel(
    sc, plen, own, oth, qkvm, qkvo, qbm, qbo, acc_h, q_h, most_h, NE, KT, V, Q8, acc_o, q_o,
    most_o, QW, QB, PL, sems,
):
    g, base, total = sc[0], sc[1], sc[2]
    started = copies(
        sems,
        [
            (plen, PL), (own, NE.at[:, g]), (oth, NE.at[:, 1 - g]), (qkvm, QW.at[0]),
            (qkvo, QW.at[1]), (qbm, QB.at[0]), (qbo, QB.at[1]),
        ],
    )
    wait(started[:1])
    starts_row, ends_row = patch_rows(PL[...])
    wait(started[1:])
    block = key_values(NE, KT, V, QW, QB)
    most = lax.fori_loop(0, 8, block, jnp.zeros((16, 256), F32))
    most_o[...] = jnp.broadcast_to(jnp.max(most), (8, 128))
    leave = pltpu.make_async_copy(most_o, most_h, sems.at[7])
    leave.start()

    def results(qb):
        at = pl.ds(pl.multiple_of(256 * qb, 256), 256)
        return (
            pltpu.make_async_copy(acc_o.at[qb], acc_h.at[qb], sems.at[8 + qb]),
            pltpu.make_async_copy(q_o.at[at], q_h.at[at], sems.at[12 + qb]),
        )

    mask, scores, step = pair_tools()

    def q_block(qb, _):
        r0 = pl.multiple_of(qb * 256, 256)
        q = queries(NE[pl.ds(8 * qb, 8), g].reshape(256, 256), QW, QB)
        q_o[pl.ds(r0, 256), :] = q
        for p in range(8):
            Q8[p] = q[:, 32 * p : 32 * p + 32]
        first, finish, kb0, kb1 = limits(qb, g, base, total, starts_row, ends_row)
        acc_o[qb] = jnp.zeros((2, 256, 256), F32)

        def body(kb, _):
            k0 = pl.multiple_of((kb - 8) * 128, 128)
            for h, x in enumerate(step(kb, k0, Q8, KT, V, first, finish)):
                acc_o[qb, h] += x
            return 0

        lax.fori_loop(jnp.maximum(kb0, 8), jnp.minimum(kb1, 24), body, 0)
        for copy in results(qb):
            copy.start()
        return 0

    lax.fori_loop(0, 4, q_block, 0)
    leave.wait()
    for qb in range(4):
        wait(results(qb))


QKV_SCRATCH = [((2, 3, 256, 128), BF), ((2, 3, 128), F32), ((1, 256), jnp.int32)]


def near_call(*args):
    out = [
        jax.ShapeDtypeStruct((4, 2, 256, 256), F32),
        jax.ShapeDtypeStruct((1024, 256), BF),
        jax.ShapeDtypeStruct((8, 128), F32),
    ]
    scratch = [
        ((32, 2, 32, 256), BF), ((256, 2048), BF), ((2048, 256), BF), ((8, 256, 32), BF),
        ((4, 2, 256, 256), F32), ((1024, 256), BF), ((8, 128), F32),
    ] + QKV_SCRATCH
    return call(near_kernel, "near", 1, args, out, scratch, 16, 20 * 10**9, space=pltpu.HBM)


def far_kernel(
    sc, sel, plen, own, oth, lo_own, lo_oth, hi_own, hi_oth, sec_i, acc_i, q_i, most_i, qkvm, qkvo,
    qbm, qbo, prw, prb, n2g, f1m, f1o, b1m, b1o, f2m, f2o, f2b, send, NE, KT, V, Q8, ACC, OUT, M,
    SEC, AI, QI, MI, PW, VEC, F1, B1, F2, QW, QB, PL, sems,
):
    g, base, total = sc[0], sc[1], sc[2]
    pw_a, pw_b = turned(prw, g)
    started = copies(
        sems,
        [
            (lo_own, NE.at[0:16, g]), (lo_oth, NE.at[0:16, 1 - g]), (hi_own, NE.at[48:64, g]),
            (hi_oth, NE.at[48:64, 1 - g]), (qkvm, QW.at[0]), (qkvo, QW.at[1]), (qbm, QB.at[0]),
            (qbo, QB.at[1]), (plen, PL), (most_i, MI), (q_i, QI), (acc_i, AI), (sec_i, SEC),
            (pw_a, PW.at[0:128]), (pw_b, PW.at[128:256]), (prb, VEC.at[0]), (n2g, VEC.at[1]),
            (f2b, VEC.at[2]), (f1m, F1.at[0]), (f1o, F1.at[1]), (b1m, B1.at[0]), (b1o, B1.at[1]),
            (f2m, F2.at[0]), (f2o, F2.at[1]),
        ],
    )
    wait(started[8:9])
    starts_row, ends_row = patch_rows(PL[...])
    edge_lo = limits(0, g, base, total, starts_row, ends_row)[2]
    edge_hi = limits(3, g, base, total, starts_row, ends_row)[3]
    wait(started[:8] + started[9:11])
    block = key_values(NE, KT, V, QW, QB)
    most = lax.fori_loop(jnp.minimum(edge_lo // 2, 4), 4, block, jnp.zeros((16, 256), F32))
    most = lax.fori_loop(12, jnp.maximum((edge_hi + 1) // 2, 12), block, most)
    key_most = jnp.maximum(jnp.max(most), jnp.max(MI[...]))
    mask, scores, step = pair_tools()
    hs = lax.broadcasted_iota(jnp.int32, (256, 128), 0) // 16
    hl = lax.broadcasted_iota(jnp.int32, (256, 128), 1)
    head_sel = jnp.where(hs == hl, 1.0, 0.0).astype(BF)
    def q_most(r0):
        q = QI[pl.ds(r0, 256), :]
        return jnp.max(jnp.dot(q * q, head_sel, preferred_element_type=F32))

    bound = q_most(0)
    for i in range(1, 4):
        bound = jnp.maximum(bound, q_most(256 * i))
    calm = bound * key_most * 1.05 <= 1e4

    @pl.when(jnp.logical_not(calm))
    def _():
        wait(copies(sems.at[24:26], [(own, NE.at[16:48, g]), (oth, NE.at[16:48, 1 - g])]))
        lax.fori_loop(4, 12, block, jnp.zeros((16, 256), F32))

    wait(started[11:])

    def q_block(qb, _):
        r0 = pl.multiple_of(qb * 256, 256)
        q = QI[pl.ds(r0, 256), :]
        for p in range(8):
            Q8[p] = q[:, 32 * p : 32 * p + 32]
        first, finish, kb0, kb1 = limits(qb, g, base, total, starts_row, ends_row)

        def body(kb, _, M=None):
            k0 = pl.multiple_of(kb * 128, 128)
            for h, x in enumerate(step(kb, k0, Q8, KT, V, first, finish, M)):
                ACC[h] += x
            return 0

        @pl.when(calm)
        def _():
            ACC[...] = AI[qb]
            lax.fori_loop(kb0, jnp.minimum(kb1, 8), body, 0)
            lax.fori_loop(jnp.maximum(kb0, 24), kb1, body, 0)

        @pl.when(jnp.logical_not(calm))
        def _():
            ACC[...] = jnp.zeros_like(ACC)
            M[...] = jnp.full(M.shape, -jnp.inf, F32)

            def top(kb, _):
                kt = KT[:, pl.ds(pl.multiple_of(kb * 128, 128), 128)]
                madd = mask(kb, first, finish)
                for p in range(8):
                    M[p] = jnp.maximum(M[p], scores(Q8, p, kt, madd))
                return 0

            lax.fori_loop(kb0, kb1, top, 0)
            for p in range(8):
                for h in range(2):
                    part = M[p, :, 128 * h : 128 * h + 128]
                    M[p, :, 128 * h : 128 * h + 128] = jnp.broadcast_to(
                        jnp.max(part, axis=1, keepdims=True), (256, 128)
                    )
            lax.fori_loop(kb0, kb1, lambda kb, c: body(kb, c, M), 0)

        attn = jnp.concatenate(
            [ACC[h, :, 0:128] / ACC[h, :, 128:256] for h in range(2)], axis=1
        ).astype(BF)
        two = (
            SEC[pl.ds(r0, 256), :].astype(F32)
            + jnp.dot(attn, PW[...], preferred_element_type=F32)
            + VEC[0]
        ).astype(BF)
        wide = two.astype(F32)
        normed = layer_norm(wide, VEC[1]).astype(BF)
        total_rows = wide + VEC[2]
        for h in range(2):
            x = jnp.dot(normed, F1[h], preferred_element_type=F32) + B1[h]
            x = (0.5 * x * (1.0 + lax.erf(x * 0.7071067811865476))).astype(BF)
            total_rows = total_rows + jnp.dot(x, F2[h], preferred_element_type=F32)
        OUT[pl.ds(r0, 256), :] = total_rows.astype(BF)
        return 0

    lax.fori_loop(0, 4, q_block, 0)

    def place(d, _):
        send[pl.ds(pl.multiple_of(32 * d, 32), 32), :] = OUT[
            pl.ds(pl.multiple_of(32 * sel[d, 0, 0], 32), 32), :
        ]
        return 0

    lax.fori_loop(0, 64, place, 0, unroll=4)


def far_call(*args):
    scratch = [
        ((64, 2, 32, 256), BF), ((256, 4096), BF), ((4096, 256), BF), ((8, 256, 32), BF),
        ((2, 256, 256), F32), ((1024, 256), BF), ((8, 256, 256), F32), ((1024, 256), BF),
        ((4, 2, 256, 256), F32), ((1024, 256), BF), ((8, 128), F32), ((256, 256), BF),
        ((3, 1, 256), F32), ((2, 256, 512), BF), ((2, 1, 512), F32), ((2, 512, 256), BF),
    ] + QKV_SCRATCH
    out = [jax.ShapeDtypeStruct((2048, 256), BF)]
    return call(far_kernel, "far", 2, args, out, scratch, 26, 20 * 10**9)[0]


def last_kernel(sc, zs, zv, own, oth, out):
    g = sc[0]
    place = zv[0:1, 0:64] % 64
    place = place % 32 + jnp.where(place // 32 == g, 0, 32)
    place = jnp.where(lax.broadcasted_iota(jnp.int32, (64, 64), 0) == place, 1.0, 0.0)
    perm = jnp.transpose(place).astype(BF)

    def step(k, _):
        source = lax.shift_right_logical(zs[64 * k], 11)
        rows = jnp.concatenate([own[source], oth[source]], axis=0)
        out[pl.ds(pl.multiple_of(64 * k, 64), 64), :] = jnp.dot(
            perm, rows, preferred_element_type=F32
        ).astype(BF)
        return 0

    lax.fori_loop(0, 32, step, 0, unroll=8)


def last_call(*args):
    smem, vmem = pl.BlockSpec(memory_space=pltpu.SMEM), pl.BlockSpec(memory_space=pltpu.VMEM)
    return pl.pallas_call(
        last_kernel,
        out_shape=jax.ShapeDtypeStruct((2048, 256), BF),
        in_specs=[smem] * 2 + [vmem] * 3,
        out_specs=vmem,
        compiler_params=pltpu.CompilerParams(vmem_limit_bytes=16 * 2**20),
        name="relabel",
    )(*args)


def local(
    points, neighbours, patch_len, zorder, conv_w, conv_b, cpe_w, cpe_b, cpe_gain, norm1_gain,
    qkv_w, qkv_b, proj_w, proj_b, norm2_gain, fc1_w, fc1_b, fc2_w, fc2_b,
):
    g = lax.axis_index("grp").astype(jnp.int32)
    me = lax.axis_index("pts").astype(jnp.int32)
    peers = lax.axis_size("pts")
    rows = points.shape[0]
    forward = [(i, i + 1) for i in range(peers - 1)]
    backward = [(i + 1, i) for i in range(peers - 1)]

    def swap(x):
        return lax.ppermute(x, "grp", [(0, 1), (1, 0)])

    def pieces(x):
        return x.reshape(-1, 32, 256)

    order = zorder.reshape(16, 128)
    low = lax.ppermute(points[rows - 256 :], "pts", forward)
    high = lax.ppermute(points[:256], "pts", backward)
    conv_m = conv_w.reshape(27 * 256, 128)
    conv_o, bias_o = swap(conv_m), swap(conv_b)
    sources = jnp.arange(peers, dtype=jnp.int32)[:, None]
    run = zorder[::64][None, :]
    wanted = jnp.max(jnp.where(run // rows == sources, run % rows // 64, 0), axis=1)
    wanted = jnp.broadcast_to(wanted[:, None, None], (peers, 1, 128))
    wanted, bias_o = lax.optimization_barrier((wanted, bias_o))
    sel = lax.all_to_all(wanted, "pts", split_axis=0, concat_axis=0, tiled=True)
    qkv_m = jnp.transpose(qkv_w, (1, 0, 2))
    conv_o, *others = lax.optimization_barrier(
        (conv_o, swap(qkv_m), swap(qkv_b), swap(fc1_w), swap(fc2_w), swap(fc1_b))
    )
    qkv_o, qb_o, fc1_o, fc2_o, b1_o = others
    weights = (qkv_m, qkv_o, qkv_b, qb_o)
    scalars = jnp.stack([g, me * rows, jnp.int32(rows * peers)])
    section_one, normed, lo_half, hi_half = conv_call(
        scalars, points, low, high, neighbours.T, conv_m, conv_o, conv_b[None], bias_o[None],
        cpe_w, cpe_b[None], cpe_gain[None], norm1_gain[None],
    )
    sel, normed, lo_half, hi_half = lax.optimization_barrier((sel, normed, lo_half, hi_half))
    other = swap(normed)
    lo_own = lax.ppermute(lo_half, "pts", forward)
    hi_own = lax.ppermute(hi_half, "pts", backward)
    acc, query, most = near_call(scalars, patch_len[None], pieces(normed), pieces(other), *weights)
    lo_own, hi_own, most = lax.optimization_barrier((lo_own, hi_own, most))
    lo_oth, hi_oth = swap(lo_own), swap(hi_own)
    send = far_call(
        scalars, sel, patch_len[None], pieces(normed), pieces(other), pieces(lo_own),
        pieces(lo_oth), pieces(hi_own), pieces(hi_oth), section_one, acc, query, most, *weights,
        proj_w, proj_b[None], norm2_gain[None], fc1_w, fc1_o, fc1_b[None], b1_o[None], fc2_w,
        fc2_o, fc2_b[None],
    )
    got = lax.all_to_all(send, "pts", split_axis=0, concat_axis=0, tiled=True)
    return last_call(scalars, zorder, order, pieces(got), pieces(swap(got)))


def solution(mesh):
    placed = (
        P("pts", None), P("pts", None), P(), P("pts"), P(None, None, "grp"), P("grp"), P(), P(), P(),
        P(), P(None, None, "grp"), P(None, "grp"), P(), P(), P(), P(None, "grp"), P("grp"),
        P("grp", None), P(),
    )
    return jax.shard_map(
        local, mesh=mesh, in_specs=placed, out_specs=P("pts", None), check_vma=False
    )
```
